32 devices in a mesh: dp: 8 (over y, x, core), fsdp: 4 (over z).
Axes of the slice: x: 2, y: 2, z: 4, core: 2. Of those that a mesh axis runs over, the one named last changes fastest.
Arguments:
- tokens: bfloat16 [256, 128, 768], P(('dp', 'fsdp')), may hold values from -6 to 6
- cotangent: float32 [256, 128, 768], P(('dp', 'fsdp')), may hold values from -6 to 6
- placement: int32 [256], replicated, may hold values from 0 to 255, as said below
- project_weight: bfloat16 [2, 768, 2304], P(None, None, ('dp', 'fsdp')), may hold values from -0.3125 to 0.3125
- project_bias: bfloat16 [2, 1536], P(None, ('dp', 'fsdp')), may hold values from -4 to 4
- output_weight: bfloat16 [2, 768, 768], P(None, None, ('dp', 'fsdp')), may hold values from -0.875 to 0.875
- output_bias: bfloat16 [2, 768], P(None, ('dp', 'fsdp')), may hold values from -4 to 4
- up_weight: bfloat16 [2, 768, 3072], P(None, None, ('dp', 'fsdp')), may hold values from -0.21875 to 0.21875
- up_bias: bfloat16 [2, 3072], P(None, ('dp', 'fsdp')), may hold values from -4 to 4
- down_weight: bfloat16 [2, 3072, 768], P(None, ('dp', 'fsdp')), may hold values from -0.109375 to 0.109375
- down_bias: bfloat16 [2, 768], P(None, ('dp', 'fsdp')), may hold values from -4 to 4
- norm_gain: bfloat16 [2, 2, 768], P(None, None, ('dp', 'fsdp')), may hold values from 0.5 to 1.5
- norm_bias: bfloat16 [2, 2, 768], P(None, None, ('dp', 'fsdp')), may hold values from -4 to 4
- position_table: bfloat16 [64, 768], P(None, ('dp', 'fsdp')), may hold values from -6 to 6
Outputs:
- layer_output: bfloat16 [256, 128, 768], P(('dp', 'fsdp'))
- token_gradient: float32 [256, 128, 768], P(('dp', 'fsdp'))
- project_weight_gradient: float32 [2, 768, 2304], P(None, None, ('dp', 'fsdp'))
- project_bias_gradient: float32 [2, 1536], P(None, ('dp', 'fsdp'))
- output_weight_gradient: float32 [2, 768, 768], P(None, None, ('dp', 'fsdp'))
- output_bias_gradient: float32 [2, 768], P(None, ('dp', 'fsdp'))
- up_weight_gradient: float32 [2, 768, 3072], P(None, None, ('dp', 'fsdp'))
- up_bias_gradient: float32 [2, 3072], P(None, ('dp', 'fsdp'))
- down_weight_gradient: float32 [2, 3072, 768], P(None, ('dp', 'fsdp'))
- down_bias_gradient: float32 [2, 768], P(None, ('dp', 'fsdp'))
- norm_gain_gradient: float32 [2, 2, 768], P(None, None, ('dp', 'fsdp'))
- norm_bias_gradient: float32 [2, 2, 768], P(None, None, ('dp', 'fsdp'))
- position_table_gradient: float32 [64, 768], P(None, ('dp', 'fsdp'))
The draws below stay inside these ranges and needn't reach their ends.
Inputs may be any that keep to these rules, and one draw needn't show every extreme that they name: placement is a permutation: slot s holds segment placement[s] of the documents laid end to end, first 2 documents of 64 segments, then 8 of 16; slot 0 holds the first segment of a long document and slot 255 the last segment of the same document.
All inputs are finite; a program needn't handle non-finite values.
Results may differ from the reference program's by a relative error of at most 0.03.
Values may be sent and summed in bfloat16 or wider, within the bound.
A program may use at most 320 MiB of HBM per device.

```python
import jax
import jax.numpy as jnp
from jax import lax

D = 768
HEADS = 12
HEAD_DIM = 64
FF = 3072
SEG_LEN = 128
LONG_SEGS = 64
SHORT_SEGS = 16
SEGS = 256
LONG_DOCS = 2


def draw_placement(key, part):
    order = jax.random.permutation(key, SEGS).astype(jnp.int32)
    chosen = jax.random.randint(jax.random.fold_in(key, 11), (), 0, LONG_DOCS).astype(jnp.int32)
    opening = chosen * LONG_SEGS
    closing = opening + LONG_SEGS - 1
    where_open = jnp.argmax(order == opening)
    order = order.at[where_open].set(order[0]).at[0].set(opening)
    where_close = jnp.argmax(order == closing)
    order = order.at[where_close].set(order[SEGS - 1]).at[SEGS - 1].set(closing)
    return order.astype(jnp.int32)


def strengthened(values, key, source, target, parts, factor):
    def block_of(position):
        return (jnp.arange(values.shape[position]) // (values.shape[position] // parts)).reshape((-1,) + (1,) * (values.ndim - 1 - position))

    first = jax.random.permutation(key, parts)[block_of(target)]
    second = (block_of(target) + parts // 2) % parts
    return jnp.where((block_of(source) == first) | (block_of(source) == second), factor * values, values)


def steps_of(stream_key, shape, cuts, least, high):
    def one(dim, shards_of):
        heights = jax.random.uniform(jax.random.fold_in(jax.random.fold_in(stream_key, 6), dim), (shards_of,), jnp.float32, least / len(cuts), high / len(cuts))
        return jnp.repeat(jnp.exp(heights), shape[dim] // shards_of).reshape((-1,) + (1,) * (len(shape) - dim - 1))

    factor_of = one(*cuts[0])
    for cut in cuts[1:]:
        factor_of = factor_of * one(*cut)
    return factor_of


def gaussian(rng, shape, scale, limit, pieces=(), held_as=jnp.bfloat16):
    drawn = jax.random.normal(rng, shape, jnp.float32) * scale
    if len(pieces) > 0:
        drawn = steps_of(rng, shape, pieces, -0.22, 0.18) * drawn
    return jnp.clip(drawn, min=-limit, max=limit).astype(held_as)


def noise_with(rng, dims, width, bound, cuts, heavy, kind=jnp.bfloat16):
    values = width * jax.random.normal(rng, dims, jnp.float32)
    if cuts:
        values = values * steps_of(rng, dims, cuts, -0.22, 0.18)
    return jnp.clip(strengthened(values, jax.random.fold_in(rng, 3), *heavy), -bound, bound).astype(kind)


def setup_inputs(seed: int = 0) -> dict:
    keys = jax.random.split(jax.random.key(seed), 15)
    tokens = gaussian(keys[0], (SEGS, SEG_LEN, D), 1.0, 6.0, ((0, 32),))
    cotangent = noise_with(keys[1], (SEGS, SEG_LEN, D), 1.0, 6.0, ((0, 32),), (0, 2, 32, 2.75), jnp.float32)
    placement = draw_placement(jax.random.fold_in(keys[14], 71), 0)
    project_weight = gaussian(keys[3], (2, D, 3 * D), (D // 2) ** -0.5, 0.3125, ((2, 32),))
    project_bias = gaussian(keys[4], (2, 2 * D), 0.3, 4.0, ((1, 32),))
    output_weight = gaussian(keys[5], (2, D, D), (D // 16) ** -0.5, 0.875, ((2, 32),))
    output_bias = gaussian(keys[6], (2, D), 0.3, 4.0, ((1, 32),))
    up_weight = gaussian(keys[7], (2, D, FF), D ** -0.5, 0.21875, ((2, 32),))
    up_bias = gaussian(keys[8], (2, FF), 0.3, 4.0, ((1, 32),))
    down_weight = gaussian(keys[9], (2, FF, D), FF ** -0.5, 0.109375, ((1, 32),))
    down_bias = gaussian(keys[10], (2, D), 0.3, 4.0, ((1, 32),))
    norm_gain = jnp.clip(1.0 + 0.1 * jax.random.normal(keys[11], (2, 2, D), jnp.float32), 0.5, 1.5).astype(jnp.bfloat16)
    norm_bias = gaussian(keys[12], (2, 2, D), 0.3, 4.0, ((2, 32),))
    position_table = gaussian(keys[13], (LONG_SEGS, D), 0.5, 6.0, ((1, 32),))
    return dict(tokens=tokens, cotangent=cotangent, placement=placement, project_weight=project_weight, project_bias=project_bias, output_weight=output_weight, output_bias=output_bias, up_weight=up_weight, up_bias=up_bias, down_weight=down_weight, down_bias=down_bias, norm_gain=norm_gain, norm_bias=norm_bias, position_table=position_table)


@jax.custom_vjp
def low(v):
    return lax.optimization_barrier(v.astype(jnp.bfloat16)).astype(jnp.float32)

@jax.custom_vjp
def low_back(v):
    return v

def low_keep(v):
    return (low(v), None)

def low_pass(kept, grad):
    return (grad,)

def back_keep(v):
    return (v, None)

def back_low(kept, grad):
    return (low(grad),)
low.defvjp(low_keep, low_pass)
low_back.defvjp(back_keep, back_low)
highest = lax.Precision.HIGHEST
epsilon = 1e-06
group_size = 32
masked_score = -1e+30

def document_table(placement):
    long_total = placement.shape[0] // 2
    long_docs = long_total // LONG_SEGS
    is_long = placement < long_total
    remainder = placement - long_total
    doc_ids = jnp.where(is_long, placement // LONG_SEGS, long_docs + remainder // SHORT_SEGS).astype(jnp.int32)
    places = jnp.where(is_long, placement % LONG_SEGS, remainder % SHORT_SEGS).astype(jnp.int32)
    return (doc_ids, places)

def layer_norm(value, gain, shift):
    centre = lax.optimization_barrier(jnp.mean(value, -1, keepdims=True))
    offset = value - centre
    spread = lax.optimization_barrier(jnp.mean(offset * offset, -1, keepdims=True))
    return offset * lax.rsqrt(spread + epsilon) * gain + shift

def gelu_exact(value):
    return jax.nn.gelu(value, approximate=False)

def product(left, right):
    return jnp.dot(left, right, precision=highest)

def softmax_rows(scores):
    row_peak = lax.optimization_barrier(jnp.max(scores, -1, keepdims=True))
    raised = jnp.exp(scores - row_peak)
    return raised / lax.optimization_barrier(jnp.sum(raised, -1, keepdims=True))

def block_params(weights, layer_id):
    project_weight, project_bias, output_weight, output_bias, up_weight, up_bias, down_weight, down_bias, norm_gain, norm_bias = weights
    model_width = output_weight.shape[1]
    bias_pair = project_bias[layer_id]
    full_bias = jnp.concatenate([bias_pair[:model_width], jnp.zeros((model_width,), bias_pair.dtype), bias_pair[model_width:]])
    return (project_weight[layer_id], full_bias, output_weight[layer_id], output_bias[layer_id], up_weight[layer_id], up_bias[layer_id], down_weight[layer_id], down_bias[layer_id], norm_gain[layer_id], norm_bias[layer_id])

def run_block(inputs, params, attend):
    project_weight, full_bias, output_weight, output_bias, up_weight, up_bias, down_weight, down_bias, gains, shifts = params
    model_width = output_weight.shape[0]
    projected = low_back(low(product(low(inputs), project_weight) + full_bias))
    attended = low_back(low(attend(projected[:, :model_width], projected[:, model_width:2 * model_width], projected[:, 2 * model_width:])))
    first_sum = inputs + low_back(product(attended, output_weight) + output_bias)
    normed = layer_norm(first_sum, gains[0], shifts[0])
    pre_act = low_back(product(low(normed), up_weight) + up_bias)
    second = normed + low_back(product(low(gelu_exact(pre_act)), down_weight) + down_bias)
    return layer_norm(second, gains[1], shifts[1])

def segment_attend(queries, key_rows, values):
    grid_shape = (queries.shape[0] // SEG_LEN, SEG_LEN, HEADS, HEAD_DIM)
    scores = low_back(jnp.einsum('glhd,gmhd->ghlm', queries.reshape(grid_shape), key_rows.reshape(grid_shape), precision=highest) * HEAD_DIM ** (-0.5))
    shares = softmax_rows(scores)
    return jnp.einsum('ghlm,gmhd->glhd', low(shares), values.reshape(grid_shape), precision=highest).reshape(queries.shape)

def cross_attend_with(same_doc):

    def attend(queries, key_rows, values):
        head_shape = (queries.shape[0], HEADS, HEAD_DIM)
        scores = low_back(jnp.einsum('rhd,shd->hrs', queries.reshape(head_shape), key_rows.reshape(head_shape), precision=highest) * HEAD_DIM ** (-0.5))
        scores = jnp.where(same_doc[None], scores, masked_score)
        shares = softmax_rows(scores)
        return jnp.einsum('hrs,shd->rhd', low(shares), values.reshape(head_shape), precision=highest).reshape(queries.shape)
    return attend

def layer_forward(tokens, project_weight, project_bias, output_weight, output_bias, up_weight, up_bias, down_weight, down_bias, norm_gain, norm_bias, position_table, doc_ids, places):
    weights = (project_weight, project_bias, output_weight, output_bias, up_weight, up_bias, down_weight, down_bias, norm_gain, norm_bias)
    seg_params = block_params(weights, 0)

    def segment_group(seg_group):
        flat_rows = seg_group.reshape(-1, D)
        return run_block(flat_rows, seg_params, segment_attend).reshape(seg_group.shape)
    grouped = tokens.reshape(SEGS // group_size, group_size, SEG_LEN, D)
    seg_out = lax.map(jax.checkpoint(segment_group), grouped).reshape(SEGS, SEG_LEN, D)
    cls_in = seg_out[:, 0, :] + position_table[places]
    same_doc = doc_ids[:, None] == doc_ids[None, :]
    cross_out = run_block(cls_in, block_params(weights, 1), cross_attend_with(same_doc))
    return seg_out.at[:, 0, :].set(cross_out)

def reference(tokens, cotangent, placement, project_weight, project_bias, output_weight, output_bias, up_weight, up_bias, down_weight, down_bias, norm_gain, norm_bias, position_table):
    doc_ids, places = document_table(placement)

    def forward(*arrays):
        return layer_forward(*arrays, doc_ids, places)
    inputs = (tokens.astype(jnp.float32), project_weight.astype(jnp.float32), project_bias.astype(jnp.float32), output_weight.astype(jnp.float32), output_bias.astype(jnp.float32), up_weight.astype(jnp.float32), up_bias.astype(jnp.float32), down_weight.astype(jnp.float32), down_bias.astype(jnp.float32), norm_gain.astype(jnp.float32), norm_bias.astype(jnp.float32), position_table.astype(jnp.float32))
    output, pullback = jax.vjp(forward, *inputs)
    gradients = pullback(cotangent.astype(jnp.float32))
    return (output.astype(jnp.bfloat16), gradients[0], gradients[1], gradients[2], gradients[3], gradients[4], gradients[5], gradients[6], gradients[7], gradients[8], gradients[9], gradients[10], gradients[11])
```

```python
import functools
import math

import jax
import jax.numpy as jnp
from jax import lax
from jax.experimental import pallas as pl
from jax.experimental.pallas import tpu as pltpu
from jax.sharding import PartitionSpec as P

HEADS = 12
HEAD_DIM = 64
SEG_LEN = 128
LONG_SEGS = 64
SHORT_SEGS = 16
MESH = pl.DeviceIdType.MESH
AXES = ("dp", "fsdp")

highest = lax.Precision.HIGHEST
epsilon = 1e-06
masked_score = -1e30


class Grid:
    def __init__(self, mesh):
        self.dp, self.fsdp = mesh.shape["dp"], mesh.shape["fsdp"]
        twos = int(math.log2(self.dp))
        self.dims = (2,) * twos + (self.fsdp,)
        self.n = self.dp * self.fsdp
        self.last = len(self.dims) - 1

    def coords(self):
        dp, fs = lax.axis_index("dp"), lax.axis_index("fsdp")
        twos = self.last
        return tuple((dp // 2 ** (twos - 1 - i)) % 2 for i in range(twos)) + (fs,)

    def peer(self, coords, dim, step):
        other = list(coords)
        other[dim] = lax.rem(coords[dim] + step, self.dims[dim])
        dp = 0
        for value in other[:-1]:
            dp = dp * 2 + value
        return (dp, other[-1]), other[dim]

    def greet(self, coords):
        barrier = pltpu.get_barrier_semaphore()
        count = 0
        for dim, size in enumerate(self.dims):
            for step in range(1, size):
                where, unused = self.peer(coords, dim, step)
                pl.semaphore_signal(barrier, inc=1, device_id=where, device_id_type=MESH)
                count += 1
        pl.semaphore_wait(barrier, count)

    def orders(self):
        middle = list(range(self.last - 1))
        return (
            [self.last] + middle[::-1] + [self.last - 1],
            [self.last] + middle + [self.last - 1],
        )


def index_of(coords, free, ndims):
    return tuple(slice(None) if d in free else coords[d] for d in range(ndims))


def chunks_of(shapes, dtypes):
    out = []
    colour = 0
    for a, (rows, dtype) in enumerate(zip(shapes, dtypes)):
        tile = 16 if dtype == jnp.bfloat16 else 8
        if rows % (2 * tile) == 0:
            out.append([(a, 0, rows // 2, 0), (a, rows // 2, rows // 2, 1)])
        else:
            out.append([(a, 0, rows, colour)])
            colour = 1 - colour
    return out


def gather_all(grid, parts, cid):
    shapes = [p.shape[0] for p in parts]
    groups = chunks_of(shapes, [p.dtype for p in parts])
    flat = [c for g in groups for c in g]
    ndims = len(grid.dims)
    most = max(grid.dims) - 1
    orders = grid.orders()
    nparts = len(parts)

    def kernel(*refs):
        sources, dests = refs[:nparts], refs[nparts : 2 * nparts]
        send_sem, recv_sem, own_sem = refs[2 * nparts :]
        coords = grid.coords()
        own = [
            pltpu.make_async_copy(sources[a], dests[a].at[coords], own_sem.at[a])
            for a in range(nparts)
        ]
        for copy in own:
            copy.start()
        grid.greet(coords)

        def copies(k, stage):
            a, first, rows, colour = flat[k]
            order = orders[colour]
            dim = order[stage]
            where = index_of(coords, order[:stage], ndims) + (pl.ds(first, rows),)
            made = []
            for step in range(1, grid.dims[dim]):
                target, unused = grid.peer(coords, dim, step)
                source = sources[a].at[pl.ds(first, rows)] if stage == 0 else dests[a].at[where]
                made.append(
                    pltpu.make_async_remote_copy(
                        source,
                        dests[a].at[where],
                        send_sem.at[k, stage, step - 1],
                        recv_sem.at[k, stage, step - 1],
                        device_id=target,
                        device_id_type=MESH,
                    )
                )
            return made

        first_of = []
        k = 0
        for g in groups:
            first_of.append(list(range(k, k + len(g))))
            k += len(g)
        for tick in range(len(groups) + ndims - 1):
            for g in range(len(groups)):
                stage = tick - g
                if not 0 <= stage < ndims:
                    continue
                for k in first_of[g]:
                    if stage == 1:
                        pass
                    if stage >= 1:
                        for copy in copies(k, stage - 1):
                            copy.wait_recv()
                    if stage == 1 and k == first_of[g][0]:
                        own[flat[k][0]].wait()
                    for copy in copies(k, stage):
                        copy.start()
        for k in range(len(flat)):
            for copy in copies(k, ndims - 1):
                copy.wait_recv()
        for k in range(len(flat)):
            for stage in range(ndims):
                for copy in copies(k, stage):
                    copy.wait_send()

    out = pl.pallas_call(
        kernel,
        out_shape=[
            jax.ShapeDtypeStruct(tuple(grid.dims) + p.shape, p.dtype) for p in parts
        ],
        in_specs=[pl.BlockSpec(memory_space=pl.ANY)] * nparts,
        out_specs=[pl.BlockSpec(memory_space=pl.ANY)] * nparts,
        scratch_shapes=[
            pltpu.SemaphoreType.DMA((len(flat), ndims, most)),
            pltpu.SemaphoreType.DMA((len(flat), ndims, most)),
            pltpu.SemaphoreType.DMA((nparts,)),
        ],
        compiler_params=pltpu.CompilerParams(collective_id=cid, has_side_effects=True),
    )(*parts)
    return [o.reshape((grid.n,) + p.shape) for o, p in zip(out, parts)]


def scatter_sum(grid, parts, cid):
    shapes = [p.shape[1] for p in parts]
    groups = chunks_of(shapes, [p.dtype for p in parts])
    flat = [c for g in groups for c in g]
    ndims = len(grid.dims)
    most = max(grid.dims) - 1
    orders = [o[::-1] for o in grid.orders()]
    nparts = len(parts)
    landing = []
    for a, first, rows, colour in flat:
        order = orders[colour]
        for stage in range(ndims):
            left = [grid.dims[d] for d in range(ndims) if d in order[stage + 1 :]]
            landing.append((grid.dims[order[stage]] - 1,) + tuple(left) + (rows, parts[a].shape[2]))

    def kernel(*refs):
        sources, outs = refs[:nparts], refs[nparts : 2 * nparts]
        lands = refs[2 * nparts : -2]
        send_sem, recv_sem = refs[-2:]
        coords = grid.coords()
        grid.greet(coords)

        def copies(k, stage):
            a, first, rows, colour = flat[k]
            order = orders[colour]
            dim = order[stage]
            made = []
            for step in range(1, grid.dims[dim]):
                target, value = grid.peer(coords, dim, step)
                there = list(coords)
                there[dim] = value
                where = index_of(there, order[stage + 1 :], ndims) + (pl.ds(first, rows),)
                made.append(
                    pltpu.make_async_remote_copy(
                        sources[a].at[where],
                        lands[k * ndims + stage].at[step - 1],
                        send_sem.at[k, stage, step - 1],
                        recv_sem.at[k, stage, step - 1],
                        device_id=target,
                        device_id_type=MESH,
                    )
                )
            return made

        def add(k, stage):
            a, first, rows, colour = flat[k]
            order = orders[colour]
            free = [d for d in range(ndims) if d in order[stage + 1 :]]
            land = lands[k * ndims + stage]
            count = grid.dims[order[stage]] - 1
            sizes = [grid.dims[d] for d in free]

            def body(i, unused):
                there = list(coords)
                rest = i
                inner = [None] * len(free)
                for pos in range(len(free) - 1, -1, -1):
                    inner[pos] = rest % sizes[pos]
                    rest = rest // sizes[pos]
                    there[free[pos]] = inner[pos]
                where = tuple(there) + (pl.ds(first, rows),)
                total = sources[a][where].astype(jnp.float32)
                for step in range(count):
                    total += land[(step,) + tuple(inner)].astype(jnp.float32)
                if stage == ndims - 1:
                    outs[a][pl.ds(first, rows)] = total
                else:
                    sources[a][where] = total.astype(sources[a].dtype)
                return unused

            lax.fori_loop(0, math.prod(sizes), body, 0)

        first_of = []
        k = 0
        for g in groups:
            first_of.append(list(range(k, k + len(g))))
            k += len(g)
        for tick in range(len(groups) + ndims):
            for g in range(len(groups)):
                stage = tick - g
                if not 0 <= stage <= ndims:
                    continue
                for k in first_of[g]:
                    if stage >= 1:
                        for copy in copies(k, stage - 1):
                            copy.wait_recv()
                        add(k, stage - 1)
                    if stage < ndims:
                        for copy in copies(k, stage):
                            copy.start()
        for k in range(len(flat)):
            for stage in range(ndims):
                for copy in copies(k, stage):
                    copy.wait_send()

    def outer(*refs):
        given, outs = refs[:nparts], refs[nparts : 2 * nparts]
        held = refs[2 * nparts : 3 * nparts]
        load_sem = refs[-1]
        loads = [
            pltpu.make_async_copy(given[a], held[a], load_sem.at[a]) for a in range(nparts)
        ]
        for load in loads:
            load.start()
        for load in loads:
            load.wait()
        kernel(*held, *outs, *refs[3 * nparts : -1])

    shaped = [p.reshape(tuple(grid.dims) + p.shape[1:]) for p in parts]
    return pl.pallas_call(
        outer,
        out_shape=[jax.ShapeDtypeStruct(p.shape[1:], jnp.float32) for p in parts],
        in_specs=[pl.BlockSpec(memory_space=pl.ANY)] * nparts,
        out_specs=[pl.BlockSpec(memory_space=pltpu.VMEM)] * nparts,
        scratch_shapes=[pltpu.VMEM(s.shape, s.dtype) for s in shaped]
        + [
            pltpu.VMEM(landing[k * ndims + s], parts[flat[k][0]].dtype)
            for k in range(len(flat))
            for s in range(ndims)
        ]
        + [
            pltpu.SemaphoreType.DMA((len(flat), ndims, most)),
            pltpu.SemaphoreType.DMA((len(flat), ndims, most)),
            pltpu.SemaphoreType.DMA((nparts,)),
        ],
        compiler_params=pltpu.CompilerParams(
            collective_id=cid, has_side_effects=True, vmem_limit_bytes=56 * 2**20
        ),
    )(*shaped)


def document_table(placement):
    long_total = placement.shape[0] // 2
    long_docs = long_total // LONG_SEGS
    is_long = placement < long_total
    remainder = placement - long_total
    doc_ids = jnp.where(is_long, placement // LONG_SEGS, long_docs + remainder // SHORT_SEGS)
    places = jnp.where(is_long, placement % LONG_SEGS, remainder % SHORT_SEGS)
    return (doc_ids, places)


def layer_norm(value, gain, shift):
    centre = jnp.mean(value, -1, keepdims=True)
    offset = value - centre
    spread = jnp.mean(offset * offset, -1, keepdims=True)
    return offset * lax.rsqrt(spread + epsilon) * gain + shift


def gelu_exact(value):
    return jax.nn.gelu(value, approximate=False)


def softmax_rows(scores):
    row_peak = jnp.max(scores, -1, keepdims=True)
    raised = jnp.exp(scores - row_peak)
    return raised / jnp.sum(raised, -1, keepdims=True)


def dot_nt(left, right):
    return lax.dot_general(
        left, right, (((1,), (1,)), ((), ())), preferred_element_type=jnp.float32
    )


def dot_nn(left, right):
    return jnp.dot(left, right, preferred_element_type=jnp.float32)


def dot_tn(left, right):
    return lax.dot_general(
        left, right, (((0,), (0,)), ((), ())), preferred_element_type=jnp.float32
    )


def column_sums(grad_low):
    return jnp.sum(grad_low.astype(jnp.float32), 0)


def split_heads(matrix):
    return matrix.reshape(matrix.shape[0], HEADS, HEAD_DIM)


def run_forward(inputs, params, attend):
    project_t, full_bias, output_t, output_bias, up_t, up_bias, down, down_bias, gains, shifts = params
    inputs_low = inputs.astype(jnp.bfloat16)
    projected = (dot_nt(inputs_low, project_t) + full_bias).astype(jnp.bfloat16)
    attended_low, kept_state = attend(projected)
    first_sum = inputs + (dot_nt(attended_low, output_t) + output_bias)
    normed = layer_norm(first_sum, gains[0], shifts[0])
    normed_low = normed.astype(jnp.bfloat16)
    pre_act = dot_nt(normed_low, up_t) + up_bias
    hidden_low = gelu_exact(pre_act).astype(jnp.bfloat16)
    second = normed + (dot_nn(hidden_low, down) + down_bias)
    output = layer_norm(second, gains[1], shifts[1])
    return (
        output,
        (inputs_low, projected, attended_low, first_sum, normed_low, pre_act, hidden_low, second, kept_state),
    )


def run_backward(grad_out, kept_values, params, attend_back, mine):
    project_t, full_bias, output_t, output_bias, up_t, up_bias, down, down_bias, gains, shifts = params
    inputs_low, projected, attended_low, first_sum, normed_low, pre_act, hidden_low, second, kept_state = kept_values
    width = output_t.shape[1]
    norm_pull = jax.vjp(layer_norm, second, gains[1], shifts[1])[1]
    grad_second, gain_two, shift_two = norm_pull(grad_out)
    down_low = grad_second.astype(jnp.bfloat16)
    grad_down = dot_tn(mine(hidden_low), down_low)
    gelu_pull = jax.vjp(gelu_exact, pre_act)[1]
    up_low = gelu_pull(dot_nt(down_low, down))[0].astype(jnp.bfloat16)
    grad_up = dot_tn(mine(up_low), normed_low)
    grad_normed = grad_second + dot_nn(up_low, up_t)
    norm_pull = jax.vjp(layer_norm, first_sum, gains[0], shifts[0])[1]
    grad_first, gain_one, shift_one = norm_pull(grad_normed)
    branch_low = grad_first.astype(jnp.bfloat16)
    grad_output = dot_tn(mine(branch_low), attended_low)
    mixed_low = dot_nn(branch_low, output_t).astype(jnp.bfloat16)
    project_low = attend_back(mixed_low, projected, kept_state).astype(jnp.bfloat16)
    grad_project = dot_tn(mine(project_low), inputs_low)
    sums_project = column_sums(project_low)
    grad_pair = jnp.concatenate([sums_project[:width], sums_project[2 * width :]])
    grad_inputs = grad_first + dot_nn(project_low, project_t)
    small = (
        grad_pair,
        column_sums(branch_low),
        column_sums(up_low),
        column_sums(down_low),
        jnp.stack([gain_one, gain_two]),
        jnp.stack([shift_one, shift_two]),
    )
    return (grad_inputs, (grad_project, grad_output, grad_up, grad_down), small)


def segment_parts(projected):
    grid = projected.reshape(projected.shape[0] // SEG_LEN, SEG_LEN, 3, HEADS, HEAD_DIM)
    return (grid[:, :, 0], grid[:, :, 1], grid[:, :, 2])


def segment_shares(queries, key_rows):
    scores = jnp.einsum(
        "glhd,gmhd->ghlm", queries, key_rows, preferred_element_type=jnp.float32
    ) * HEAD_DIM ** (-0.5)
    return softmax_rows(scores)


def segment_attend(projected):
    queries, key_rows, values = segment_parts(projected)
    shares = segment_shares(queries, key_rows)
    attended = jnp.einsum(
        "ghlm,gmhd->glhd", shares.astype(jnp.bfloat16), values, preferred_element_type=jnp.float32
    )
    return (attended.reshape(projected.shape[0], -1).astype(jnp.bfloat16), shares)


def segment_back(mixed_low, projected, shares):
    queries, key_rows, values = segment_parts(projected)
    grad_low = mixed_low.reshape(queries.shape)
    grad_shares = jnp.einsum(
        "glhd,gmhd->ghlm", grad_low, values, preferred_element_type=jnp.float32
    )
    row_dot = jnp.sum(shares * grad_shares, -1, keepdims=True)
    score_low = (shares * (grad_shares - row_dot)).astype(jnp.bfloat16)
    grad_queries = jnp.einsum(
        "ghlm,gmhd->glhd", score_low, key_rows, preferred_element_type=jnp.float32
    ) * HEAD_DIM ** (-0.5)
    grad_keys = jnp.einsum(
        "ghlm,glhd->gmhd", score_low, queries, preferred_element_type=jnp.float32
    ) * HEAD_DIM ** (-0.5)
    grad_values = jnp.einsum(
        "ghlm,glhd->gmhd", shares.astype(jnp.bfloat16), grad_low, preferred_element_type=jnp.float32
    )
    return jnp.stack([grad_queries, grad_keys, grad_values], 2).reshape(projected.shape)


def cross_shares(queries, key_rows, same_doc):
    scores = jnp.einsum(
        "rhd,shd->hrs", queries, key_rows, preferred_element_type=jnp.float32
    ) * HEAD_DIM ** (-0.5)
    return softmax_rows(jnp.where(same_doc[None], scores, masked_score))


def cross_parts(projected):
    width = projected.shape[1] // 3
    return [split_heads(projected[:, i * width : (i + 1) * width]) for i in range(3)]


def cross_attend_with(same_doc):
    def attend(projected):
        queries, key_rows, values = cross_parts(projected)
        shares = cross_shares(queries, key_rows, same_doc)
        attended = jnp.einsum(
            "hrs,shd->rhd", shares.astype(jnp.bfloat16), values, preferred_element_type=jnp.float32
        )
        return (attended.reshape(projected.shape[0], -1).astype(jnp.bfloat16), shares)

    return attend


def cross_back(mixed_low, projected, shares):
    queries, key_rows, values = cross_parts(projected)
    grad_heads = split_heads(mixed_low)
    grad_shares = jnp.einsum(
        "rhd,shd->hrs", grad_heads, values, preferred_element_type=jnp.float32
    )
    row_dot = jnp.sum(shares * grad_shares, -1, keepdims=True)
    score_low = (shares * (grad_shares - row_dot)).astype(jnp.bfloat16)
    grad_queries = jnp.einsum(
        "hrs,shd->rhd", score_low, key_rows, preferred_element_type=jnp.float32
    ) * HEAD_DIM ** (-0.5)
    grad_keys = jnp.einsum(
        "hrs,rhd->shd", score_low, queries, preferred_element_type=jnp.float32
    ) * HEAD_DIM ** (-0.5)
    grad_values = jnp.einsum(
        "hrs,rhd->shd", shares.astype(jnp.bfloat16), grad_heads, preferred_element_type=jnp.float32
    )
    rows = projected.shape[0]
    return jnp.concatenate([g.reshape(rows, -1) for g in (grad_queries, grad_keys, grad_values)], 1)


def shards(
    grid,
    tokens,
    cotangent,
    placement,
    project_weight,
    project_bias,
    output_weight,
    output_bias,
    up_weight,
    up_bias,
    down_weight,
    down_bias,
    norm_gain,
    norm_bias,
    position_table,
):
    n = grid.n
    seg_count, seg_len, width = tokens.shape
    slots, rows = placement.shape[0], seg_count * seg_len
    per_project, per_output = project_weight.shape[2], output_weight.shape[2]
    per_pair, per_up = project_bias.shape[1], up_bias.shape[1]
    places_n = position_table.shape[0]
    me = lax.axis_index(AXES)

    mixed_part = [
        jnp.concatenate([project_weight[b].T, output_weight[b].T], 0) for b in range(2)
    ]
    up_part = [up_weight[b].T for b in range(2)]
    down_part = [down_weight[b] for b in range(2)]
    small = [
        jnp.concatenate(
            [
                project_bias[b], output_bias[b], up_bias[b], down_bias[b],
                norm_gain[b].reshape(-1), norm_bias[b].reshape(-1),
            ]
        )
        for b in range(2)
    ]
    small_size = small[0].shape[0]
    table_rows = -(-position_table.size // width)
    flat_table = jnp.pad(position_table.reshape(-1), (0, table_rows * width - position_table.size))
    misc = jnp.concatenate(
        [jnp.pad(s, (0, width - small_size))[None] for s in small]
        + [flat_table.reshape(table_rows, width)],
        0,
    )
    misc = jnp.pad(misc, ((0, 16 - misc.shape[0]), (0, 0)))

    misc_all, mixed0, up0, down0, mixed1, up1, down1 = gather_all(
        grid,
        [misc, mixed_part[0], up_part[0], down_part[0], mixed_part[1], up_part[1], down_part[1]],
        0,
    )

    def params_of(b, mixed_all, up_all, down_all):
        project_t = mixed_all[:, :per_project].reshape(n * per_project, width)
        output_t = mixed_all[:, per_project:].reshape(n * per_output, width)
        values = misc_all[:, b, :small_size].astype(jnp.float32)
        cuts, at = [], 0
        for size in (per_pair, per_output, per_up, per_output):
            cuts.append(values[:, at : at + size].reshape(-1))
            at += size
        norms = []
        for unused in range(2):
            pair = values[:, at : at + 2 * per_output].reshape(n, 2, per_output)
            norms.append(pair.transpose(1, 0, 2).reshape(2, width))
            at += 2 * per_output
        pair_bias, out_bias, up_b, down_b = cuts
        full_bias = jnp.concatenate(
            [pair_bias[:width], jnp.zeros((width,), jnp.float32), pair_bias[width:]]
        )
        return (
            project_t, full_bias, output_t, out_bias, up_all.reshape(n * per_up, width), up_b,
            down_all.reshape(n * per_up, width), down_b, norms[0], norms[1],
        )

    seg_params = params_of(0, mixed0, up0, down0)
    cross_params = params_of(1, mixed1, up1, down1)
    table = (
        misc_all[:, 2 : 2 + table_rows]
        .reshape(n, -1)[:, : position_table.size]
        .reshape(n, places_n, per_output)
        .transpose(1, 0, 2)
        .reshape(places_n, width)
    )

    doc_ids, places = document_table(placement)
    same_doc = doc_ids[:, None] == doc_ids[None, :]
    picker = places[:, None] == jnp.arange(places_n, dtype=jnp.int32)[None, :]

    inputs = tokens.reshape(rows, width).astype(jnp.float32)
    seg_out, seg_kept = run_forward(inputs, seg_params, segment_attend)
    seg_grid = seg_out.reshape(seg_count, seg_len, width)

    cls_rows, cot_rows = gather_all(grid, [seg_grid[:, 0, :], cotangent[:, 0, :]], 1)
    cls_in = cls_rows.reshape(slots, width) + dot_nn(picker.astype(jnp.bfloat16), table)
    cross_out, cross_kept = run_forward(cls_in, cross_params, cross_attend_with(same_doc))

    def own_columns(matrix):
        size = matrix.shape[1] // n
        return lax.dynamic_slice_in_dim(matrix, me * size, size, 1)

    grad_cls_all, cross_big, cross_small = run_backward(
        cot_rows.reshape(slots, width), cross_kept, cross_params, cross_back, own_columns
    )
    position_gradient = lax.dot_general(
        picker.astype(jnp.float32), own_columns(grad_cls_all), (((0,), (0,)), ((), ())), precision=highest
    )
    my_cross = lax.dynamic_slice_in_dim(cross_out, me * seg_count, seg_count, 0)
    grad_cls = lax.dynamic_slice_in_dim(grad_cls_all, me * seg_count, seg_count, 0)
    layer_output = seg_grid.at[:, 0, :].set(my_cross).astype(jnp.bfloat16)

    grad_rows = cotangent.at[:, 0, :].set(grad_cls).reshape(rows, width)
    grad_inputs, seg_big, seg_small = run_backward(
        grad_rows, seg_kept, seg_params, segment_back, lambda matrix: matrix
    )

    def small_slots(pair, out_b, up_b, down_b, gains, shifts):
        def per_device(vector):
            return vector.reshape(vector.shape[:-1] + (n, -1))

        return jnp.concatenate(
            [
                per_device(pair), per_device(out_b), per_device(up_b), per_device(down_b),
                per_device(gains).transpose(1, 0, 2).reshape(n, -1),
                per_device(shifts).transpose(1, 0, 2).reshape(n, -1),
            ],
            1,
        )

    grad_project, grad_output, grad_up, grad_down = [
        g.astype(jnp.bfloat16).reshape(n, -1, width) for g in seg_big
    ]
    seg_small_slots = small_slots(*seg_small)
    seg_small_slots = jnp.pad(seg_small_slots[:, None], ((0, 0), (0, 7), (0, width - small_size)))
    down_sum, up_sum, mixed_sum, small_sum = scatter_sum(
        grid,
        [grad_down, grad_up, jnp.concatenate([grad_project, grad_output], 1), seg_small_slots],
        2,
    )
    my_small = [
        small_sum[0, :small_size],
        lax.dynamic_slice_in_dim(small_slots(*cross_small), me, 1, 0)[0],
    ]
    small_pair = jnp.stack(my_small)
    cuts, at = [], 0
    for size in (per_pair, per_output, per_up, per_output, 2 * per_output, 2 * per_output):
        cuts.append(small_pair[:, at : at + size])
        at += size
    pair_g, out_g, up_g, down_g, gain_g, shift_g = cuts
    return (
        layer_output,
        grad_inputs.reshape(tokens.shape),
        jnp.stack([mixed_sum[:per_project].T, cross_big[0].T]),
        pair_g,
        jnp.stack([mixed_sum[per_project:].T, cross_big[1].T]),
        out_g,
        jnp.stack([up_sum.T, cross_big[2].T]),
        up_g,
        jnp.stack([down_sum, cross_big[3]]),
        down_g,
        gain_g.reshape(2, 2, per_output),
        shift_g.reshape(2, 2, per_output),
        position_gradient,
    )


def solution(mesh):
    grid = Grid(mesh)
    rows, cols, last = P(AXES, None, None), P(None, AXES), P(None, None, AXES)
    middle = P(None, AXES, None)
    return jax.shard_map(
        functools.partial(shards, grid),
        mesh=mesh,
        in_specs=(
            rows, rows, P(), last, cols, last, cols, last, cols, middle, cols, last, last, cols,
        ),
        out_specs=(rows, rows, last, cols, last, cols, last, cols, middle, cols, last, last, cols),
        check_vma=False,
    )
```

```python
import functools
import math

import jax
import jax.numpy as jnp
from jax import lax
from jax.experimental import pallas as pl
from jax.experimental.pallas import tpu as pltpu
from jax.sharding import PartitionSpec as P

HEADS = 12
HEAD_DIM = 64
SEG_LEN = 128
LONG_SEGS = 64
SHORT_SEGS = 16
MESH = pl.DeviceIdType.MESH
AXES = ("dp", "fsdp")

highest = lax.Precision.HIGHEST
epsilon = 1e-06
masked_score = -1e30


class Grid:
    def __init__(self, mesh):
        self.dp, self.fsdp = mesh.shape["dp"], mesh.shape["fsdp"]
        twos = int(math.log2(self.dp))
        self.dims = (2,) * twos + (self.fsdp,)
        self.n = self.dp * self.fsdp
        self.last = len(self.dims) - 1
        self.most = max(self.dims) - 1
        middle = list(range(self.last - 1))
        self.orders = (
            [self.last] + middle[::-1] + [self.last - 1],
            [self.last] + middle + [self.last - 1],
        )

    def coords(self):
        dp, fs = lax.axis_index("dp"), lax.axis_index("fsdp")
        twos = self.last
        return tuple((dp // 2 ** (twos - 1 - i)) % 2 for i in range(twos)) + (fs,)

    def flat(self):
        return lax.axis_index("dp") * self.fsdp + lax.axis_index("fsdp")

    def peer(self, coords, dim, step):
        other = list(coords)
        other[dim] = lax.rem(coords[dim] + step, self.dims[dim])
        dp = 0
        for value in other[:-1]:
            dp = dp * 2 + value
        return (dp, other[-1]), other[dim]

    def greet(self, coords):
        barrier = pltpu.get_barrier_semaphore()
        count = 0
        for dim, size in enumerate(self.dims):
            for step in range(1, size):
                where, unused = self.peer(coords, dim, step)
                pl.semaphore_signal(barrier, inc=1, device_id=where, device_id_type=MESH)
                count += 1
        pl.semaphore_wait(barrier, count)

    def sems(self, chunks):
        shape = (chunks, len(self.dims), self.most)
        return [pltpu.SemaphoreType.DMA(shape), pltpu.SemaphoreType.DMA(shape)]


def index_of(coords, free, ndims):
    return tuple(slice(None) if d in free else coords[d] for d in range(ndims))


def halves(rows, dtype):
    tile = 16 if dtype == jnp.bfloat16 else 8
    if rows % (2 * tile) == 0:
        return [(0, rows // 2, 0), (rows // 2, rows // 2, 1)]
    return [(0, rows, 0)]


class Gather:
    def __init__(self, grid, coords, chunks, send_sem, recv_sem, base=0):
        self.grid, self.coords, self.chunks = grid, coords, chunks
        self.send_sem, self.recv_sem, self.base = send_sem, recv_sem, base
        self.stages = len(grid.dims)

    def copies(self, k, stage):
        own, line, dest, first, rows, colour = self.chunks[k]
        grid, coords = self.grid, self.coords
        order = grid.orders[colour]
        dim = order[stage]
        cut = (pl.ds(first, rows),)
        if stage == 0:
            source = own.at[cut]
            target_ref = dest.at[coords + cut] if line is None else line.at[(coords[-1],) + cut]
        else:
            target_ref = dest.at[index_of(coords, order[:stage], len(grid.dims)) + cut]
            source = line.at[(slice(None),) + cut] if line is not None and stage == 1 else target_ref
        made = []
        for step in range(1, grid.dims[dim]):
            target, unused = grid.peer(coords, dim, step)
            made.append(
                pltpu.make_async_remote_copy(
                    source,
                    target_ref,
                    self.send_sem.at[self.base + k, stage, step - 1],
                    self.recv_sem.at[self.base + k, stage, step - 1],
                    device_id=target,
                    device_id_type=MESH,
                )
            )
        return made

    def start(self, k, stage):
        for copy in self.copies(k, stage):
            copy.start()

    def landed(self, k, stage):
        for copy in self.copies(k, stage):
            copy.wait_recv()

    def sent(self, k, first_stage, last_stage):
        for stage in range(first_stage, last_stage):
            for copy in self.copies(k, stage):
                copy.wait_send()


class Scatter:
    def __init__(self, grid, coords, chunks, send_sem, recv_sem, base=0):
        self.grid, self.coords, self.chunks = grid, coords, chunks
        self.send_sem, self.recv_sem, self.base = send_sem, recv_sem, base
        self.stages = len(grid.dims)

    @staticmethod
    def landing(grid, rows, width, dtype, colour):
        order = grid.orders[colour][::-1]
        made = []
        for stage, dim in enumerate(order):
            left = [grid.dims[d] for d in range(len(order)) if d in order[stage + 1 :]]
            made.append(pltpu.VMEM((grid.dims[dim] - 1, *left, rows, width), dtype))
        return made

    def copies(self, k, stage):
        held, lands, out, first, rows, colour = self.chunks[k]
        grid, coords = self.grid, self.coords
        order = grid.orders[colour][::-1]
        dim = order[stage]
        made = []
        for step in range(1, grid.dims[dim]):
            target, value = grid.peer(coords, dim, step)
            there = list(coords)
            there[dim] = value
            where = index_of(there, order[stage + 1 :], len(order)) + (pl.ds(first, rows),)
            made.append(
                pltpu.make_async_remote_copy(
                    held.at[where],
                    lands[stage].at[step - 1],
                    self.send_sem.at[self.base + k, stage, step - 1],
                    self.recv_sem.at[self.base + k, stage, step - 1],
                    device_id=target,
                    device_id_type=MESH,
                )
            )
        return made

    def start(self, k, stage):
        for copy in self.copies(k, stage):
            copy.start()

    def add(self, k, stage):
        for copy in self.copies(k, stage):
            copy.wait_recv()
        held, lands, out, first, rows, colour = self.chunks[k]
        grid, coords = self.grid, self.coords
        order = grid.orders[colour][::-1]
        free = [d for d in range(len(order)) if d in order[stage + 1 :]]
        sizes = [grid.dims[d] for d in free]
        final = stage == self.stages - 1
        land = lands[stage]

        def body(i, unused):
            there = list(coords)
            rest = i
            inner = [None] * len(free)
            for pos in range(len(free) - 1, -1, -1):
                inner[pos] = rest % sizes[pos]
                rest = rest // sizes[pos]
                there[free[pos]] = inner[pos]
            where = tuple(there) + (pl.ds(first, rows),)
            total = held[where]
            if final:
                total = total.astype(jnp.float32)
            for step in range(grid.dims[order[stage]] - 1):
                total += land[(step,) + tuple(inner)].astype(total.dtype)
            if final:
                out[pl.ds(first, rows)] = total
            else:
                held[where] = total
            return unused

        if free:
            lax.fori_loop(0, math.prod(sizes), body, 0)
        else:
            body(0, 0)

    def sent(self, k):
        for stage in range(self.stages):
            for copy in self.copies(k, stage):
                copy.wait_send()


def dot_nt(left, right):
    return lax.dot_general(
        left, right, (((1,), (1,)), ((), ())), preferred_element_type=jnp.float32
    )


def dot_nn(left, right):
    return lax.dot_general(
        left, right, (((1,), (0,)), ((), ())), preferred_element_type=jnp.float32
    )


def dot_tn(left, right):
    return lax.dot_general(
        left, right, (((0,), (0,)), ((), ())), preferred_element_type=jnp.float32
    )


def normalise(value):
    offset = value - jnp.mean(value, -1, keepdims=True)
    scale = lax.rsqrt(jnp.mean(offset * offset, -1, keepdims=True) + epsilon)
    return offset * scale, scale


def norm_back(grad, unit, scale, gain):
    pulled = grad * gain
    along = jnp.mean(pulled * unit, -1, keepdims=True)
    return scale * (pulled - jnp.mean(pulled, -1, keepdims=True) - unit * along)


def gelu_pair(x):
    bell = jnp.exp(-0.5 * x * x)
    t = 1.0 / (1.0 + (0.3275911 * 0.5**0.5) * jnp.abs(x))
    tail = t * (0.5 * 0.254829592 + t * (0.5 * -0.284496736 + t * (
        0.5 * 1.421413741 + t * (0.5 * -1.453152027 + t * (0.5 * 1.061405429)))))
    tail = tail * bell
    below = jnp.where(x < 0, tail, 1.0 - tail)
    return x * below, below + (x * 0.3989422804014327) * bell


def first_lanes():
    return lax.broadcasted_iota(jnp.int32, (1, 2 * HEAD_DIM), 1) < HEAD_DIM


def stack_heads(pair):
    zero = jnp.zeros_like(pair)
    left = first_lanes()
    return jnp.concatenate([jnp.where(left, pair, zero), jnp.where(left, zero, pair)], 0)


def unstack_heads(stacked):
    rows = stacked.shape[0] // 2
    return jnp.where(first_lanes(), stacked[:rows], stacked[rows:])


def pair_shares(query_stack, key_pair, allowed):
    scores = dot_nt(query_stack, key_pair)
    if allowed is not None:
        scores = jnp.where(allowed, scores, masked_score)
    raised = jnp.exp(scores - jnp.max(scores, -1, keepdims=True))
    return raised * (1.0 / jnp.sum(raised, -1, keepdims=True))


def attend_rows(qkv, mixed, rows, span, width, allowed):
    for start in range(0, rows, span):
        here = pl.ds(start, span)
        for p in range(width // (2 * HEAD_DIM)):
            at = p * 2 * HEAD_DIM
            query = stack_heads(qkv[here, pl.ds(at, 2 * HEAD_DIM)] * jnp.bfloat16(HEAD_DIM**-0.5))
            key = qkv[here, pl.ds(width + at, 2 * HEAD_DIM)]
            value = qkv[here, pl.ds(2 * width + at, 2 * HEAD_DIM)]
            shares = pair_shares(query, key, allowed)
            both = dot_nn(shares.astype(jnp.bfloat16), value)
            mixed[here, pl.ds(at, 2 * HEAD_DIM)] = unstack_heads(both).astype(jnp.bfloat16)


def attend_back(qkv, d_mixed, d_qkv, rows, span, width, allowed):
    scale = HEAD_DIM**-0.5
    for start in range(0, rows, span):
        here = pl.ds(start, span)
        for p in range(width // (2 * HEAD_DIM)):
            at = p * 2 * HEAD_DIM
            query = stack_heads(qkv[here, pl.ds(at, 2 * HEAD_DIM)] * jnp.bfloat16(scale))
            key = qkv[here, pl.ds(width + at, 2 * HEAD_DIM)]
            value = qkv[here, pl.ds(2 * width + at, 2 * HEAD_DIM)]
            grad = stack_heads(d_mixed[here, pl.ds(at, 2 * HEAD_DIM)])
            shares = pair_shares(query, key, allowed)
            d_shares = dot_nt(grad, value)
            delta = jnp.sum(shares * d_shares, -1, keepdims=True)
            d_scores = (shares * (d_shares - delta)).astype(jnp.bfloat16)
            d_query = unstack_heads(dot_nn(d_scores, key)) * scale
            d_key = dot_tn(d_scores, query)
            d_value = dot_tn(shares.astype(jnp.bfloat16), grad)
            d_qkv[here, pl.ds(at, 2 * HEAD_DIM)] = d_query.astype(jnp.bfloat16)
            d_qkv[here, pl.ds(width + at, 2 * HEAD_DIM)] = d_key.astype(jnp.bfloat16)
            d_qkv[here, pl.ds(2 * width + at, 2 * HEAD_DIM)] = d_value.astype(jnp.bfloat16)


def row_sums(value):
    return jnp.sum(value.astype(jnp.float32), 0, keepdims=True)


def whole(shape):
    return pl.BlockSpec(shape, lambda *i: (0,) * len(shape), pipeline_mode=pl.Buffered(1))


def select(rows, columns, first):
    row = lax.broadcasted_iota(jnp.int32, (rows, columns), 0)
    column = lax.broadcasted_iota(jnp.int32, (rows, columns), 1)
    return jnp.where(row == first + column, 1.0, 0.0).astype(jnp.bfloat16)


def spread_slots(rows_of_slots, n, per, size):
    columns = n * size
    step = min(columns, 768)
    out = []
    lane = lax.broadcasted_iota(jnp.int32, (128, 1), 0)
    slot = lax.broadcasted_iota(jnp.int32, (n * per, 1), 0) // per
    for c in range(0, columns, step):
        column = lax.broadcasted_iota(jnp.int32, (1, step), 1) + c
        ones = jnp.where(column % size == lane, 1.0, 0.0).astype(jnp.bfloat16)
        laid = dot_nn(rows_of_slots, ones)
        kept = jnp.where(slot == column // size, laid, 0.0)
        out.append(jnp.sum(kept.reshape(n, per, step), 0))
    return out[0] if len(out) == 1 else jnp.concatenate(out, 1)


SMALL_ROWS = 16


def weights_kernel(grid, sizes, *refs):
    width, per_project, per_output, per_up, per_pair, places_n = sizes
    n, ndims = grid.n, len(grid.dims)
    pw, ow, uw, dw, pb, ob, ub, db, ng, nb, pt, cot = refs[:12]
    mixed0, up0, down0, mixed1, up1, cot1, own_down1, vec, vec_pair, vec_up, table = refs[12:23]
    own_mixed, own_up, own_down, own_misc, misc_f, misc_all, own_cot, cot_head = refs[23:31]
    send_sem, recv_sem, local_sem = refs[31:]
    coords = grid.coords()
    me_line = coords[-1]
    cot_copy = pltpu.make_async_copy(cot.at[:, pl.ds(0, 8)], cot_head, local_sem.at[0])
    cot_copy.start()

    misc_f[...] = jnp.zeros_like(misc_f)
    at = 0
    for ref, size in ((pb, per_pair), (ob, per_output), (ub, per_up), (db, per_output)):
        misc_f[pl.ds(at, 2), pl.ds(0, size)] = ref[...].astype(jnp.float32)
        at += 2
    for ref in (ng, nb):
        for b in range(2):
            misc_f[pl.ds(at, 2), pl.ds(0, per_output)] = ref[b].astype(jnp.float32)
            at += 2
    misc_f[pl.ds(SMALL_ROWS, places_n), pl.ds(0, per_output)] = pt[...].astype(jnp.float32)
    own_misc[...] = misc_f[...].astype(jnp.bfloat16)

    def pack(b):
        rows = per_project + per_output
        own_mixed[b] = (
            dot_nt(place_rows(rows, per_project, 0), pw[b]) + dot_nt(place_rows(rows, per_output, per_project), ow[b])
        ).astype(jnp.bfloat16)

    def place_rows(rows, size, first):
        row = lax.broadcasted_iota(jnp.int32, (rows, size), 0)
        column = lax.broadcasted_iota(jnp.int32, (rows, size), 1)
        return jnp.where(row == first + column, 1.0, 0.0).astype(jnp.bfloat16)

    pack(0)
    grid.greet(coords)

    units, chunks = [], []

    def add(own, line, dest, cuts):
        for cut in cuts:
            chunks.append((own, line, dest, *cut))
        return list(range(len(chunks) - len(cuts), len(chunks)))

    mixed_rows = per_project + per_output
    units += [add(own_mixed.at[0], None, mixed0, u) for u in pairs(mixed_rows)]
    units[0] += add(own_misc, None, misc_all, [(0, SMALL_ROWS + places_n, 0)])
    up_units = len(units)
    units += [add(own_up.at[0], None, up0, u) for u in pairs(per_up)]
    down_units = len(units)
    units += [add(own_down.at[0], None, down0, u) for u in pairs(per_up)]
    line_units = [add(own_mixed.at[1], mixed1, None, [h]) for h in halves(mixed_rows, jnp.bfloat16)]
    line_units += [add(own_up.at[1], up1, None, [h]) for h in halves(per_up, jnp.bfloat16)]
    line_units[0] += add(own_cot, cot1, None, [(0, own_cot.shape[0], 0)])
    gather = Gather(grid, coords, chunks, send_sem, recv_sem)

    def start(unit, stage):
        for k in unit:
            gather.start(k, stage)

    start(units[0], 0)
    own_up[0] = dot_nt(place_rows(per_up, per_up, 0), uw[0]).astype(jnp.bfloat16)
    own_down[0] = dw[0]
    pack(1)
    own_up[1] = dot_nt(place_rows(per_up, per_up, 0), uw[1]).astype(jnp.bfloat16)
    own_down[1] = dw[1]
    cot_copy.wait()
    for s in range(own_cot.shape[0]):
        own_cot[pl.ds(s, 1), :] = cot_head[s, 0:1, :]
    locals_ = [
        pltpu.make_async_copy(own_mixed.at[0], mixed0.at[coords], local_sem.at[0]),
        pltpu.make_async_copy(own_up.at[0], up0.at[coords], local_sem.at[1]),
        pltpu.make_async_copy(own_down.at[0], down0.at[coords], local_sem.at[2]),
        pltpu.make_async_copy(own_mixed.at[1], mixed1.at[me_line], local_sem.at[3]),
        pltpu.make_async_copy(own_up.at[1], up1.at[me_line], local_sem.at[4]),
        pltpu.make_async_copy(own_down.at[1], own_down1, local_sem.at[5]),
        pltpu.make_async_copy(own_cot, cot1.at[me_line], local_sem.at[6]),
    ]
    for copy in locals_:
        copy.start()
    misc_all[coords] = own_misc[...]
    for copy in locals_:
        copy.wait()

    def vectors():
        small = misc_all[..., 0:SMALL_ROWS, :].reshape(n * SMALL_ROWS, 128)
        singles = spread_slots(small, n, SMALL_ROWS, per_output)
        pairs = spread_slots(small, n, SMALL_ROWS, per_pair)
        ups = spread_slots(small, n, SMALL_ROWS, per_up)
        for b in range(2):
            vec[b, 0:1, :] = singles[2 + b : 3 + b]
            vec[b, 1:2, :] = singles[6 + b : 7 + b]
            vec[b, 2:4, :] = singles[8 + 2 * b : 10 + 2 * b]
            vec[b, 4:6, :] = singles[12 + 2 * b : 14 + 2 * b]
            vec[b, 6:8, :] = jnp.zeros((2, width), jnp.float32)
            vec_pair[b, :, 0:width] = pairs[b : b + 1, :width]
            vec_pair[b, :, width : 2 * width] = jnp.zeros((1, width), jnp.float32)
            vec_pair[b, :, 2 * width : 3 * width] = pairs[b : b + 1, width:]
            vec_up[b] = ups[4 + b : 5 + b]
        lead = grid.dims[0]
        total = jnp.zeros((places_n, width), jnp.float32)
        per = n // lead
        lane = lax.broadcasted_iota(jnp.int32, (128, 1), 0)
        column = lax.broadcasted_iota(jnp.int32, (1, width), 1)
        ones = jnp.where(column % per_output == lane, 1.0, 0.0).astype(jnp.bfloat16)
        owner = column // per_output
        for i in range(lead):
            rows = misc_all[i, ..., SMALL_ROWS : SMALL_ROWS + places_n, :].reshape(per * places_n, 128)
            laid = dot_nn(rows, ones)
            slot = lax.broadcasted_iota(jnp.int32, (per * places_n, 1), 0) // places_n + i * per
            kept = jnp.where(slot == owner, laid, 0.0)
            total += jnp.sum(kept.reshape(per, places_n, width), 0)
        table[...] = total.astype(jnp.bfloat16)

    count = len(units)
    line_ticks = {count - 6: line_units[:1], count - 4: line_units[1:2], count - 1: line_units[2:]} if count >= 7 else {0: line_units}
    for tick in range(1, count + ndims):
        for stage in range(1, ndims + 1):
            u = tick - stage
            if not 0 <= u < count:
                continue
            for k in units[u]:
                gather.landed(k, stage - 1)
                if stage < ndims:
                    gather.start(k, stage)
            if stage == 1:
                if u + 1 < count:
                    start(units[u + 1], 0)
                for unit in line_ticks.get(u, []):
                    start(unit, 0)
            if stage == ndims and u == 0:
                vectors()
    for unit in line_units:
        for k in unit:
            gather.landed(k, 0)
            gather.sent(k, 0, 1)
    for unit in units:
        for k in unit:
            gather.sent(k, 0, ndims)


def pairs(rows):
    if rows % 32:
        return [[(0, rows, 0)]]
    return [[(r, 16, 0), (r + 16, 16, 1)] for r in range(0, rows, 32)]


def gather_weights(grid, arrays, cid):
    project_weight, output_weight, up_weight, down_weight, project_bias = arrays[:5]
    width = project_weight.shape[1]
    per_project, per_output, per_up = project_weight.shape[2], output_weight.shape[2], up_weight.shape[2]
    per_pair = project_bias.shape[1]
    places_n = arrays[10].shape[0]
    segs = arrays[11].shape[0]
    n = grid.n
    low, full = jnp.bfloat16, jnp.float32
    mixed_rows = per_project + per_output
    misc_rows = SMALL_ROWS + places_n
    fs = grid.fsdp
    count = 2 + sum(len(u) for r in (mixed_rows, per_up, per_up) for u in pairs(r)) + sum(len(halves(r, low)) for r in (mixed_rows, per_up))
    vmem, anywhere = pl.BlockSpec(memory_space=pltpu.VMEM), pl.BlockSpec(memory_space=pl.ANY)

    def shape(s, d):
        return jax.ShapeDtypeStruct(s, d)

    return pl.pallas_call(
        functools.partial(weights_kernel, grid, (width, per_project, per_output, per_up, per_pair, places_n)),
        in_specs=[vmem] * 11 + [anywhere],
        out_specs=[anywhere] * 7 + [vmem] * 4,
        out_shape=[
            shape((*grid.dims, mixed_rows, width), low), shape((*grid.dims, per_up, width), low), shape((*grid.dims, per_up, width), low),
            shape((fs, mixed_rows, width), low), shape((fs, per_up, width), low), shape((fs, segs, width), full), shape((per_up, width), low),
            shape((2, 8, width), full), shape((2, 1, 3 * width), full), shape((2, 1, n * per_up), full), shape((places_n, width), low),
        ],
        scratch_shapes=[
            pltpu.VMEM((2, mixed_rows, width), low), pltpu.VMEM((2, per_up, width), low), pltpu.VMEM((2, per_up, width), low),
            pltpu.VMEM((misc_rows, 128), low), pltpu.VMEM((misc_rows, 128), full), pltpu.VMEM((*grid.dims, misc_rows, 128), low),
            pltpu.VMEM((segs, width), full), pltpu.VMEM((segs, 8, width), full),
        ]
        + grid.sems(count)
        + [pltpu.SemaphoreType.DMA((7,))],
        compiler_params=pltpu.CompilerParams(collective_id=cid, has_side_effects=True, vmem_limit_bytes=56 * 2**20),
        name="gather_weights",
    )(*arrays)


def forward_rows(x_low, x, w, r, rows, span, allowed, hook=lambda name: None):
    width = x.shape[1]
    step = width
    hook("project")
    for c in range(0, 3 * width, step):
        cut = pl.ds(c, step)
        r["qkv"][:, cut] = (dot_nt(x_low, w["project"][cut, :]) + w["project_b"][:, cut]).astype(jnp.bfloat16)
    attend_rows(r["qkv"], r["mixed"], rows, span, width, allowed)
    first = x + (dot_nt(r["mixed"][...], w["output"][...]) + w["output_b"])
    if "first" in r:
        r["first"](first)
    hook("first")
    unit_one, scale_one, unit_two, scale_two = feed_forward(first, w, r, hook)
    return unit_one, scale_one, unit_two, scale_two


def feed_forward(first, w, r, hook=lambda name: None):
    unit_one, scale_one = normalise(first)
    normed = unit_one * w["gains"][0:1, :] + w["shifts"][0:1, :]
    normed_low = normed.astype(jnp.bfloat16)
    r["normed"][...] = normed_low
    hidden_units = w["up"].shape[0]
    step = normed.shape[1]
    for c in range(0, hidden_units, step):
        cut = pl.ds(c, step)
        inner = dot_nt(normed_low, w["up"][cut, :]) + w["up_b"][:, cut]
        value, slope = gelu_pair(inner)
        r["hidden"][:, cut] = value.astype(jnp.bfloat16)
        r["slope"][:, cut] = slope.astype(r["slope"].dtype)
    hook("down")
    second = normed + (dot_nn(r["hidden"][...], w["down"][...]) + w["down_b"])
    unit_two, scale_two = normalise(second)
    return unit_one, scale_one, unit_two, scale_two


def mlp_back(grad, unit_one, scale_one, unit_two, scale_two, w, r, hook=lambda name: None):
    d_second = norm_back(grad, unit_two, scale_two, w["gains"][1:2, :])
    d_down = d_second.astype(jnp.bfloat16)
    r["d_down"][...] = d_down
    hidden_units = w["up"].shape[0]
    step = grad.shape[1]
    for c in range(0, hidden_units, step):
        cut = pl.ds(c, step)
        d_hidden = dot_nt(d_down, w["down"][cut, :])
        r["d_inner"][:, cut] = (d_hidden * r["slope"][:, cut].astype(jnp.float32)).astype(jnp.bfloat16)
    hook("up")
    d_normed = d_second + dot_nn(r["d_inner"][...], w["up"][...])
    d_first = norm_back(d_normed, unit_one, scale_one, w["gains"][0:1, :])
    sums = (
        row_sums(d_normed * unit_one), row_sums(grad * unit_two), row_sums(d_normed), row_sums(grad),
        row_sums(d_down), row_sums(r["d_inner"][...]),
    )
    return d_first, sums


def small_of(vec, vec_pair, vec_up, b):
    return {
        "project_b": vec_pair.at[b], "output_b": vec[b, 0:1, :], "up_b": vec_up.at[b], "down_b": vec[b, 1:2, :],
        "gains": vec[b, 2:4, :], "shifts": vec[b, 4:6, :],
    }


def unpack_mixed(grid, mixed, project, output, per_project):
    rows, width = mixed.shape[-2:]
    per_output = rows - per_project
    for d in range(grid.n):
        where, rest = [], d
        for size in grid.dims[::-1]:
            where.append(rest % size)
            rest //= size
        part = mixed[tuple(where[::-1])]
        project[pl.ds(d * per_project, per_project), :] = part[:per_project]
        output[pl.ds(d * per_output, per_output), :] = part[per_project:]


def spread(events, points):
    return [events[len(events) * p // points : len(events) * (p + 1) // points] for p in range(points)]


def segment_forward_kernel(grid, tile, steps, per_project, *refs):
    (tokens, grads, mixed0, up0, down0, vec, vec_pair, vec_up, line_mixed, line_up, line_cot, own_down) = refs[:12]
    names = ("qkv", "mixed", "normed", "hidden", "d_down", "d_inner", "d_first", "seg_low", "norm_sums", "up_sums")
    r = dict(zip(names, refs[12:22]))
    project_out, output_out, all_first, mixed1, up1, down1, all_cot = refs[22:29]
    r["slope"], held_mixed, project, output, up, down, own_first = refs[29:36]
    send_sem, recv_sem, local_sem = refs[36:]
    w = small_of(vec, vec_pair, vec_up, 0)
    w.update(project=project, output=output, up=up, down=down)
    width = tokens.shape[1]
    step = pl.program_id(0)
    last = steps - 1
    ndims = len(grid.dims)
    coords = grid.coords()
    loads = [pltpu.make_async_copy(*p, local_sem.at[i]) for i, p in enumerate(
        ((mixed0, held_mixed), (up0, up), (down0, down)))]
    stores = [pltpu.make_async_copy(*p, local_sem.at[3 + i]) for i, p in enumerate(
        ((project, project_out), (output, output_out)))]
    here = (coords[:-1]) + (slice(None),)
    lines = [pltpu.make_async_copy(a, b.at[here], local_sem.at[5 + i]) for i, (a, b) in enumerate(
        ((line_mixed, mixed1), (line_up, up1), (line_cot, all_cot)))]
    lines.append(pltpu.make_async_copy(own_down, down1.at[coords], local_sem.at[8]))
    keep_first = pltpu.make_async_copy(own_first, all_first.at[coords], local_sem.at[9])

    chunks, groups = [], []
    for own, line, dest, rows in (
        (None, line_mixed, mixed1, line_mixed.shape[1]), (None, line_up, up1, line_up.shape[1]), (own_down, None, down1, own_down.shape[0])
    ):
        cuts = halves(rows, jnp.bfloat16)
        groups.append(list(range(len(chunks), len(chunks) + len(cuts))))
        chunks += [(own, line, dest, *cut) for cut in cuts]
    groups[0].append(len(chunks))
    chunks.append((None, line_cot, all_cot, 0, line_cot.shape[1], 1))
    first_chunk = len(chunks)
    chunks.append((own_first, None, all_first, 0, own_first.shape[0], 0))
    gather = Gather(grid, coords, chunks, send_sem, recv_sem)

    ticks = ndims - 1 + len(groups)

    def go(tick):
        if tick == 1:
            for copy in lines:
                copy.wait()
        for g in range(len(groups) - 1, -1, -1):
            stage = tick - g + 1
            late = chunks[groups[g][0]][1] is None
            for k in groups[g]:
                if late and tick == 0:
                    gather.start(k, 0)
                if (late and stage == 1) or 1 < stage <= ndims:
                    gather.landed(k, stage - 1)
                if 1 <= stage < ndims:
                    gather.start(k, stage)

    plan = {}
    for tick in range(1, ticks - 1):
        at = min(2 * steps - 1, round(2 * steps * (tick - 0.65) / (ticks - 3)) - 1)
        plan.setdefault(at, []).append(tick)

    def at_point(which):
        for at, some in plan.items():
            if at % 2 == which:

                @pl.when(step == at // 2)
                def _(some=some):
                    for tick in some:
                        go(tick)

    first_points = ["first", "down", "back", "up"]
    first_events = [[] for unused in first_points]
    stages = list(range(ndims))
    for i, stage in enumerate(stages):
        first_events[min(i, len(first_points) - 1)].append(stage)

    def first_point(name):
        @pl.when(step == last)
        def _():
            for stage in first_events[first_points.index(name)]:
                if stage == 0:
                    keep_first.start()
                else:
                    gather.landed(first_chunk, stage - 1)
                    if stage == 1:
                        keep_first.wait()
                gather.start(first_chunk, stage)

    @pl.when(step == 0)
    def _():
        for copy in loads:
            copy.start()
        grid.greet(coords)
        go(0)
        for copy in lines:
            copy.start()
        loads[0].wait()
        unpack_mixed(grid, held_mixed, project, output, per_project)
        for copy in stores:
            copy.start()

    def hook(name):
        if name == "first":
            first_point("first")

            @pl.when(step == 0)
            def _():
                for copy in loads[1:]:
                    copy.wait()

            at_point(0)
        if name == "down":
            first_point("down")
        if name == "up":
            first_point("up")

    def take_first(first):
        for s in range(tile // SEG_LEN):
            own_first[pl.ds(step * (tile // SEG_LEN) + s, 1), :] = first[s * SEG_LEN : s * SEG_LEN + 1]

    r["first"] = take_first
    x_low = tokens[...]
    x = x_low.astype(jnp.float32)
    unit_one, scale_one, unit_two, scale_two = forward_rows(x_low, x, w, r, tile, SEG_LEN, None, hook)
    seg_out = unit_two * w["gains"][1:2, :] + w["shifts"][1:2, :]
    r["seg_low"][...] = seg_out.astype(jnp.bfloat16)
    first_point("back")
    place = lax.broadcasted_iota(jnp.int32, (tile, 1), 0) % SEG_LEN
    grad = jnp.where(place == 0, 0.0, grads[...])
    d_first, sums = mlp_back(grad, unit_one, scale_one, unit_two, scale_two, w, r, hook)
    r["d_first"][...] = d_first
    gathered = jnp.concatenate(list(sums[:5]) + [jnp.zeros((3, width), jnp.float32)], 0)

    @pl.when(step == 0)
    def _():
        r["norm_sums"][...] = jnp.zeros_like(r["norm_sums"])
        r["up_sums"][...] = jnp.zeros_like(r["up_sums"])

    r["norm_sums"][...] += gathered
    r["up_sums"][...] += jnp.broadcast_to(sums[5], r["up_sums"].shape)

    at_point(1)

    @pl.when(step == last)
    def _():
        go(ticks - 1)
        for g in range(len(groups)):
            for k in groups[g]:
                gather.sent(k, 1 if chunks[k][1] is not None else 0, ndims)
        gather.landed(first_chunk, ndims - 1)
        gather.sent(first_chunk, 0, ndims)
        for copy in stores:
            copy.wait()


def segment_forward(grid, tokens, grads, mixed0, up0, down0, smalls, lines, per_project, cid):
    rows, width = tokens.shape
    per_up = up0.shape[-2]
    mixed_rows = mixed0.shape[-2]
    hidden_units = per_up * grid.n
    tile = 2 * SEG_LEN
    steps = rows // tile
    segs = rows // SEG_LEN
    low, full = jnp.bfloat16, jnp.float32
    up0, down0 = up0.reshape(hidden_units, width), down0.reshape(hidden_units, width)
    count = 2 + sum(len(halves(r, low)) for r in (mixed_rows, per_up, per_up))
    vmem, anywhere = pl.BlockSpec(memory_space=pltpu.VMEM), pl.BlockSpec(memory_space=pl.ANY)

    def cut(columns):
        return pl.BlockSpec((tile, columns), lambda i: (i, 0))

    def shape(columns, dtype):
        return jax.ShapeDtypeStruct((rows, columns), dtype)

    return pl.pallas_call(
        functools.partial(segment_forward_kernel, grid, tile, steps, per_project),
        grid=(steps,),
        in_specs=[cut(width), cut(width)] + [anywhere] * 3 + [whole(s.shape) for s in (*smalls, *lines)],
        out_specs=[
            cut(3 * width), cut(width), cut(width), cut(hidden_units), cut(width), cut(hidden_units), cut(width), cut(width),
            pl.BlockSpec((8, width), lambda i: (0, 0)), pl.BlockSpec((8, hidden_units), lambda i: (0, 0)),
        ]
        + [anywhere] * 7,
        out_shape=[
            shape(3 * width, low), shape(width, low), shape(width, low), shape(hidden_units, low), shape(width, low),
            shape(hidden_units, low), shape(width, full), shape(width, low),
            jax.ShapeDtypeStruct((8, width), full), jax.ShapeDtypeStruct((8, hidden_units), full),
            jax.ShapeDtypeStruct((3 * width, width), low), jax.ShapeDtypeStruct((width, width), low),
            jax.ShapeDtypeStruct((*grid.dims, segs, width), full),
            jax.ShapeDtypeStruct((*grid.dims, mixed_rows, width), low),
            jax.ShapeDtypeStruct((*grid.dims, per_up, width), low), jax.ShapeDtypeStruct((*grid.dims, per_up, width), low),
            jax.ShapeDtypeStruct((*grid.dims, segs, width), full),
        ],
        scratch_shapes=[
            pltpu.VMEM((tile, hidden_units), low), pltpu.VMEM((*grid.dims, mixed_rows, width), low),
            pltpu.VMEM((3 * width, width), low), pltpu.VMEM((width, width), low),
            pltpu.VMEM((hidden_units, width), low), pltpu.VMEM((hidden_units, width), low), pltpu.VMEM((segs, width), full),
        ]
        + grid.sems(count)
        + [pltpu.SemaphoreType.DMA((10,))],
        compiler_params=pltpu.CompilerParams(collective_id=cid, has_side_effects=True, vmem_limit_bytes=60 * 2**20),
        name="segment_forward",
    )(tokens, grads, mixed0, up0, down0, *smalls, *lines)


def own_columns(value, first, size):
    return dot_nn(value, select(value.shape[1], size, first)).astype(jnp.bfloat16)


def own_sums(value, first, size):
    row = lax.broadcasted_iota(jnp.int32, (value.shape[1], size), 0)
    column = lax.broadcasted_iota(jnp.int32, (value.shape[1], size), 1)
    ones = jnp.where(row == first + column, 1.0, 0.0)
    return jnp.dot(value, ones, precision=highest, preferred_element_type=jnp.float32)


def document_of(placed, long_total):
    long_docs = long_total // LONG_SEGS
    is_long = placed < long_total
    rest = placed - long_total
    doc = jnp.where(is_long, placed // LONG_SEGS, long_docs + rest // SHORT_SEGS)
    return doc, jnp.where(is_long, placed % LONG_SEGS, rest % SHORT_SEGS)


def cross_kernel(grid, sizes, *refs):
    per_project, per_output, per_up, per_pair = sizes
    (firsts, grads, placed_row, placed_col, mixed1, up1, down1, up0, down0, vec, vec_pair, vec_up, table) = refs[:13]
    g_project, g_output, g_up, g_down, z_up, z_down, smalls, g_table, cross_own, d_first_own = refs[13:23]
    names = ("qkv", "slope", "d_mixed", "mixed", "normed", "hidden", "d_down", "d_inner", "d_qkv")
    r = dict(zip(names, refs[23:32]))
    held_mixed, project, output, up, down, z_up_w, z_down_w, z_slope, z_normed, z_hidden, z_d_down, z_d_inner, rows_f = refs[32:45]
    local_sem = refs[45]
    loads = [pltpu.make_async_copy(*p, local_sem.at[i]) for i, p in enumerate(
        ((up0, z_up_w), (down0, z_down_w), (mixed1, held_mixed), (up1, up), (down1, down)))]
    for copy in loads:
        copy.start()
    slots, width = firsts.shape
    places_n = table.shape[0]
    me = grid.flat()
    per_slots = slots // grid.n

    w0 = small_of(vec, vec_pair, vec_up, 0)
    w0.update(up=z_up_w, down=z_down_w)
    r0 = {"normed": z_normed, "hidden": z_hidden, "slope": z_slope, "d_down": z_d_down, "d_inner": z_d_inner}

    def hook0(name):
        if name == "down":
            loads[1].wait()

    loads[0].wait()
    kept0 = feed_forward(firsts[...], w0, r0, hook0)
    seg_first = kept0[2] * w0["gains"][1:2, :] + w0["shifts"][1:2, :]
    doc_row, unused = document_of(placed_row[...], slots // 2)
    doc_col, place_col = document_of(placed_col[...], slots // 2)
    picker = place_col == lax.broadcasted_iota(jnp.int32, (slots, places_n), 1)
    picker_f = jnp.where(picker, 1.0, 0.0)
    x = seg_first + dot_nn(picker_f.astype(jnp.bfloat16), table[...])

    w = small_of(vec, vec_pair, vec_up, 1)
    w.update(project=project, output=output, up=up, down=down)
    loads[2].wait()
    unpack_mixed(grid, held_mixed, project, output, per_project)
    x_low = x.astype(jnp.bfloat16)
    allowed = doc_col == doc_row
    allowed = jnp.concatenate([allowed, allowed], 0)

    def hook(name):
        if name == "first":
            loads[3].wait()
        if name == "down":
            loads[4].wait()

    kept = forward_rows(x_low, x, w, r, slots, slots, allowed, hook)
    mine = pl.ds(pl.multiple_of(me * per_slots, per_slots), per_slots)
    rows_f[...] = kept[2] * w["gains"][1:2, :] + w["shifts"][1:2, :]
    cross_own[...] = rows_f[mine, :]
    d_first, sums = mlp_back(grads[...], *kept, w, r)
    branch = d_first.astype(jnp.bfloat16)
    r["d_mixed"][...] = dot_nn(branch, output[...]).astype(jnp.bfloat16)
    attend_back(r["qkv"], r["d_mixed"], r["d_qkv"], slots, slots, width, allowed)
    d_x = d_first + dot_nn(r["d_qkv"][...], project[...])

    g_project[...] = dot_tn(x_low, own_columns(r["d_qkv"][...], me * per_project, per_project))
    g_output[...] = dot_tn(r["mixed"][...], own_columns(branch, me * per_output, per_output))
    g_up[...] = dot_tn(r["normed"][...], own_columns(r["d_inner"][...], me * per_up, per_up))
    g_down[...] = dot_tn(own_columns(r["hidden"][...], me * per_up, per_up), r["d_down"][...])
    smalls[...] = jnp.zeros_like(smalls)
    norm_rows = jnp.concatenate(list(sums[:5]) + [row_sums(branch), jnp.zeros((2, width), jnp.float32)], 0)
    smalls[0:8, 0:per_output] = own_sums(norm_rows, me * per_output, per_output)
    smalls[8:16, 0:per_up] = own_sums(jnp.broadcast_to(sums[5], (8, sums[5].shape[1])), me * per_up, per_up)
    qkv_sums = row_sums(r["d_qkv"][...])
    pair = jnp.concatenate([qkv_sums[:, :width], qkv_sums[:, 2 * width :]], 1)
    smalls[16:24, 0:per_pair] = own_sums(jnp.broadcast_to(pair, (8, 2 * width)), me * per_pair, per_pair)
    g_table[...] = lax.dot_general(
        picker_f, own_sums(d_x, me * per_output, per_output), (((0,), (0,)), ((), ())),
        precision=highest, preferred_element_type=jnp.float32,
    )

    d_first0, sums = mlp_back(d_x, *kept0, w0, r0)
    rows_f[...] = d_first0
    d_first_own[...] = rows_f[mine, :]
    z_up[...] = dot_tn(own_columns(z_d_inner[...], me * per_up, per_up), z_normed[...])
    z_down[...] = dot_tn(own_columns(z_hidden[...], me * per_up, per_up), z_d_down[...])
    norm_rows = jnp.concatenate(list(sums[:5]) + [jnp.zeros((3, width), jnp.float32)], 0)
    smalls[24:32, 0:per_output] = own_sums(norm_rows, me * per_output, per_output)
    smalls[32:40, 0:per_up] = own_sums(jnp.broadcast_to(sums[5], (8, sums[5].shape[1])), me * per_up, per_up)


def cross_block(grid, firsts, grads, placement, mixed1, up1, down1, up0, down0, smalls, table, sizes):
    slots, width = firsts.shape
    per_project, per_output, per_up, per_pair = sizes
    hidden_units = per_up * grid.n
    low, full = jnp.bfloat16, jnp.float32
    per_slots = slots // grid.n
    flat = lambda ref: ref.reshape(hidden_units, width)
    vmem, anywhere = pl.BlockSpec(memory_space=pltpu.VMEM), pl.BlockSpec(memory_space=pl.ANY)
    outs = [
        (width, per_project), (width, per_output), (width, per_up), (per_up, width), (per_up, width), (per_up, width),
        (40, 128), (table.shape[0], per_output), (per_slots, width), (per_slots, width),
    ]

    def held(*shape, dtype=low):
        return pltpu.VMEM(shape, dtype)

    return pl.pallas_call(
        functools.partial(cross_kernel, grid, sizes),
        in_specs=[vmem] * 4 + [anywhere] * 5 + [vmem] * 4,
        out_specs=[vmem] * len(outs),
        out_shape=[jax.ShapeDtypeStruct(s, full) for s in outs],
        scratch_shapes=[
            held(slots, 3 * width), held(slots, hidden_units), held(slots, width), held(slots, width), held(slots, width),
            held(slots, hidden_units), held(slots, width), held(slots, hidden_units), held(slots, 3 * width),
            held(*mixed1.shape), held(3 * width, width), held(width, width), held(hidden_units, width), held(hidden_units, width),
            held(hidden_units, width), held(hidden_units, width), held(slots, hidden_units), held(slots, width),
            held(slots, hidden_units), held(slots, width), held(slots, hidden_units), held(slots, width, dtype=full),
            pltpu.SemaphoreType.DMA((5,)),
        ],
        compiler_params=pltpu.CompilerParams(vmem_limit_bytes=62 * 2**20),
        name="cross_block",
    )(firsts, grads, placement[None, :], placement[:, None], mixed1, flat(up1), flat(down1), flat(up0), flat(down0), *smalls, table)


def segment_backward_kernel(tile, qkv, d_first, cls_grad, seg_low, cls_out, project, output, d_qkv, d_branch, d_x, layer_out, sums_qkv, sums_out, d_mixed):
    width = d_first.shape[1]
    place = lax.broadcasted_iota(jnp.int32, (tile, 1), 0)
    grad, out = d_first[...], seg_low[...].astype(jnp.float32)
    step = pl.program_id(0)
    for s in range(tile // SEG_LEN):
        here = pl.ds(step * (tile // SEG_LEN) + s, 1)
        grad = jnp.where(place == s * SEG_LEN, cls_grad[here, :], grad)
        out = jnp.where(place == s * SEG_LEN, cls_out[here, :], out)
    layer_out[...] = out.astype(jnp.bfloat16)
    branch = grad.astype(jnp.bfloat16)
    d_branch[...] = branch
    d_mixed[...] = dot_nn(branch, output[...]).astype(jnp.bfloat16)
    attend_back(qkv, d_mixed, d_qkv, tile, SEG_LEN, width, None)
    d_x[...] = grad + dot_nn(d_qkv[...], project[...])

    @pl.when(step == 0)
    def _():
        sums_qkv[...] = jnp.zeros_like(sums_qkv)
        sums_out[...] = jnp.zeros_like(sums_out)

    sums_qkv[...] += jnp.broadcast_to(row_sums(d_qkv[...]), sums_qkv.shape)
    sums_out[...] += jnp.broadcast_to(row_sums(branch), sums_out.shape)


def segment_backward(qkv, d_first, cls_grad, seg_low, cls_out, project, output):
    rows, width = d_first.shape
    tile = 2 * SEG_LEN
    low, full = jnp.bfloat16, jnp.float32

    def cut(columns):
        return pl.BlockSpec((tile, columns), lambda i: (i, 0))

    return pl.pallas_call(
        functools.partial(segment_backward_kernel, tile),
        grid=(rows // tile,),
        in_specs=[
            cut(3 * width), cut(width), whole(cls_grad.shape), cut(width), whole(cls_out.shape), whole(project.shape), whole(output.shape),
        ],
        out_specs=[
            cut(3 * width), cut(width), cut(width), cut(width),
            pl.BlockSpec((8, 3 * width), lambda i: (0, 0)), pl.BlockSpec((8, width), lambda i: (0, 0)),
        ],
        out_shape=[
            jax.ShapeDtypeStruct((rows, 3 * width), low), jax.ShapeDtypeStruct((rows, width), low),
            jax.ShapeDtypeStruct((rows, width), full), jax.ShapeDtypeStruct((rows, width), low),
            jax.ShapeDtypeStruct((8, 3 * width), full), jax.ShapeDtypeStruct((8, width), full),
        ],
        scratch_shapes=[pltpu.VMEM((tile, width), jnp.bfloat16)],
        compiler_params=pltpu.CompilerParams(vmem_limit_bytes=60 * 2**20),
        name="segment_backward",
    )(qkv, d_first, cls_grad, seg_low, cls_out, project, output)


def sum_kernel(grid, chunk_list, nparts, *refs):
    given, outs = refs[:nparts], refs[nparts : 2 * nparts]
    held = refs[2 * nparts : 3 * nparts]
    lands = refs[3 * nparts : -3]
    send_sem, recv_sem, load_sem = refs[-3:]
    ndims = len(grid.dims)
    coords = grid.coords()
    loads = [pltpu.make_async_copy(given[a], held[a], load_sem.at[a]) for a in range(nparts)]
    for load in loads:
        load.start()
    grid.greet(coords)
    chunks, groups = [], {}
    for k, (a, first, count, colour) in enumerate(chunk_list):
        groups.setdefault(a, []).append(k)
        chunks.append((held[a], lands[k * ndims : (k + 1) * ndims], outs[a], first, count, colour))
    scatter = Scatter(grid, coords, chunks, send_sem, recv_sem)
    for tick in range(nparts + ndims):
        for a in range(nparts):
            stage = tick - a
            if not 0 <= stage <= ndims:
                continue
            if stage == 0:
                loads[a].wait()
            for k in groups[a]:
                if stage >= 1:
                    scatter.add(k, stage - 1)
                if stage < ndims:
                    scatter.start(k, stage)
    for k in range(len(chunks)):
        scatter.sent(k)


def sum_to_owners(grid, parts, cid):
    chunk_list = [(a, *h) for a, p in enumerate(parts) for h in halves(p.shape[1], p.dtype)]
    nparts = len(parts)
    shaped = [p.reshape(tuple(grid.dims) + p.shape[1:]) for p in parts]
    lands = []
    for a, first, count, colour in chunk_list:
        lands += Scatter.landing(grid, count, parts[a].shape[2], parts[a].dtype, colour)
    return pl.pallas_call(
        functools.partial(sum_kernel, grid, chunk_list, nparts),
        out_shape=[jax.ShapeDtypeStruct(p.shape[1:], jnp.float32) for p in parts],
        in_specs=[pl.BlockSpec(memory_space=pl.ANY)] * nparts,
        out_specs=[pl.BlockSpec(memory_space=pltpu.VMEM)] * nparts,
        scratch_shapes=[pltpu.VMEM(s.shape, s.dtype) for s in shaped] + lands + grid.sems(len(chunk_list)) + [pltpu.SemaphoreType.DMA((nparts,))],
        compiler_params=pltpu.CompilerParams(collective_id=cid, has_side_effects=True, vmem_limit_bytes=56 * 2**20),
        name="sum_to_owners",
    )(*shaped)


class Held:
    def __init__(self, value):
        self.value = value

    @property
    def shape(self):
        return self.value.shape

    @property
    def dtype(self):
        return self.value.dtype

    @staticmethod
    def plain(where):
        where = where if isinstance(where, tuple) else (where,)
        return tuple(slice(w.start, w.start + w.size) if isinstance(w, pl.Slice) else w for w in where)

    def __getitem__(self, where):
        return self.value[self.plain(where)]

    def __setitem__(self, where, value):
        self.value = self.value.at[self.plain(where)].set(value)


def cross_plain(grid, firsts, grads, placement, mixed1, up1, down1, up0, down0, smalls, table, sizes):
    slots, width = firsts.shape
    per_project, per_output, per_up, per_pair = sizes
    hidden_units = per_up * grid.n
    me = grid.flat()
    vec, vec_pair, vec_up = smalls

    def weights(b, up, down):
        return {
            "project_b": vec_pair[b], "output_b": vec[b, 0:1, :], "up_b": vec_up[b], "down_b": vec[b, 1:2, :],
            "gains": vec[b, 2:4, :], "shifts": vec[b, 4:6, :],
            "up": up.reshape(hidden_units, width), "down": down.reshape(hidden_units, width),
        }

    def blank(columns):
        return Held(jnp.zeros((slots, columns), jnp.bfloat16))

    def store():
        made = {k: blank(width) for k in ("mixed", "normed", "d_down", "d_mixed")}
        made.update({k: blank(hidden_units) for k in ("hidden", "slope", "d_inner")})
        made.update(qkv=blank(3 * width), d_qkv=blank(3 * width))
        return made

    def cut(matrix, size, axis=1):
        return lax.dynamic_slice_in_dim(matrix, me * size, size, axis)

    w0, w, r0, r = weights(0, up0, down0), weights(1, up1, down1), store(), store()
    parts = mixed1.reshape(grid.n, -1, width)
    w["project"] = parts[:, :per_project].reshape(3 * width, width)
    w["output"] = parts[:, per_project:].reshape(width, width)
    kept0 = feed_forward(firsts, w0, r0)
    seg_first = kept0[2] * w0["gains"][1:2, :] + w0["shifts"][1:2, :]
    doc, place = document_of(placement, slots // 2)
    picker = jnp.where(place[:, None] == jnp.arange(table.shape[0], dtype=jnp.int32)[None, :], 1.0, 0.0)
    x = seg_first + dot_nn(picker.astype(jnp.bfloat16), table)
    x_low = x.astype(jnp.bfloat16)
    allowed = doc[:, None] == doc[None, :]
    allowed = jnp.concatenate([allowed, allowed], 0)
    kept = forward_rows(x_low, x, w, r, slots, slots, allowed)
    out = kept[2] * w["gains"][1:2, :] + w["shifts"][1:2, :]
    d_first, sums = mlp_back(grads, *kept, w, r)
    branch = d_first.astype(jnp.bfloat16)
    r["d_mixed"][...] = dot_nn(branch, w["output"]).astype(jnp.bfloat16)
    attend_back(r["qkv"], r["d_mixed"], r["d_qkv"], slots, slots, width, allowed)
    d_x = d_first + dot_nn(r["d_qkv"][...], w["project"])
    d_first0, sums0 = mlp_back(d_x, *kept0, w0, r0)
    qkv_sums = row_sums(r["d_qkv"][...])
    pair = jnp.concatenate([qkv_sums[:, :width], qkv_sums[:, 2 * width :]], 1)

    def laid(rows, size):
        rows = cut(rows, size)
        return jnp.pad(rows, ((0, 8 - rows.shape[0]), (0, 128 - size)))

    own_small = jnp.concatenate(
        [
            laid(jnp.concatenate(list(sums[:5]) + [row_sums(branch)], 0), per_output), laid(sums[5], per_up), laid(pair, per_pair),
            laid(jnp.concatenate(list(sums0[:5]), 0), per_output), laid(sums0[5], per_up),
        ],
        0,
    )
    g_table = lax.dot_general(picker, cut(d_x, per_output), (((0,), (0,)), ((), ())), precision=highest)
    per_slots = slots // grid.n
    return (
        dot_tn(x_low, cut(r["d_qkv"][...], per_project)), dot_tn(r["mixed"][...], cut(branch, per_output)),
        dot_tn(r["normed"][...], cut(r["d_inner"][...], per_up)), dot_tn(cut(r["hidden"][...], per_up), r["d_down"][...]),
        dot_tn(cut(r0["d_inner"][...], per_up), r0["normed"][...]), dot_tn(cut(r0["hidden"][...], per_up), r0["d_down"][...]),
        own_small, g_table, cut(out, per_slots, 0), cut(d_first0, per_slots, 0),
    )


def shards(
    grid,
    tokens,
    cotangent,
    placement,
    project_weight,
    project_bias,
    output_weight,
    output_bias,
    up_weight,
    up_bias,
    down_weight,
    down_bias,
    norm_gain,
    norm_bias,
    position_table,
):
    n = grid.n
    seg_count, seg_len, width = tokens.shape
    slots, rows = placement.shape[0], seg_count * seg_len
    per_project, per_output = project_weight.shape[2], output_weight.shape[2]
    per_pair, per_up = project_bias.shape[1], up_bias.shape[1]
    sizes = (per_project, per_output, per_up, per_pair)
    low_tokens = tokens.reshape(rows, width)

    mixed0, up0, down0, *lines, vec, vec_pair, vec_up, table = gather_weights(
        grid,
        [project_weight, output_weight, up_weight, down_weight, project_bias, output_bias, up_bias, down_bias,
         norm_gain, norm_bias, position_table, cotangent],
        0,
    )
    smalls = [vec, vec_pair, vec_up]
    (qkv, mixed, normed, hidden, d_down, d_inner, d_first, seg_low, norm_sums, up_sums, project, output, all_first,
     mixed1, up1, down1, all_cot) = segment_forward(
        grid, low_tokens, cotangent.reshape(rows, width), mixed0, up0, down0, smalls, lines, per_project, 1
    )
    g_project, g_output, g_up, g_down, z_up, z_down, own_small, g_table, cross_own, cls_grad = (cross_block if slots <= 256 else cross_plain)(
        grid, all_first.reshape(slots, width), all_cot.reshape(slots, width), placement, mixed1, up1, down1, up0, down0,
        smalls, table, sizes,
    )
    d_qkv, d_branch, d_x, layer_out, sums_qkv, sums_out = segment_backward(
        qkv, d_first, cls_grad, seg_low, cross_own, project, output
    )
    grad_project, grad_output, grad_up, grad_down = [
        dot_tn(left, right).astype(jnp.bfloat16).reshape(n, -1, width)
        for left, right in ((d_qkv, low_tokens), (d_branch, mixed), (d_inner, normed), (hidden, d_down))
    ]

    def per_device(vector):
        return vector.reshape(vector.shape[:-1] + (n, -1))

    seg_small = jnp.concatenate(
        [
            per_device(jnp.concatenate([sums_qkv[0, :width], sums_qkv[0, 2 * width :]])), per_device(sums_out[0]),
            per_device(up_sums[0]), per_device(norm_sums[4]),
            per_device(norm_sums[:4]).transpose(1, 0, 2).reshape(n, -1),
        ],
        1,
    )
    small_size = seg_small.shape[1]
    small_width = -(-small_size // 128) * 128
    seg_small = jnp.pad(seg_small[:, None], ((0, 0), (0, 7), (0, small_width - small_size)))
    down_sum, up_sum, mixed_sum, small_sum = sum_to_owners(
        grid, [grad_down, grad_up, jnp.concatenate([grad_project, grad_output], 1), seg_small], 2
    )
    down_sum += z_down
    up_sum += z_up
    cuts, at = [], 0
    for size in (per_pair, per_output, per_up, per_output, 4 * per_output):
        cuts.append(small_sum[0, at : at + size])
        at += size
    pair_g = jnp.stack([cuts[0], own_small[16, :per_pair]])
    out_g = jnp.stack([cuts[1], own_small[5, :per_output]])
    up_g = jnp.stack([cuts[2] + own_small[32, :per_up], own_small[8, :per_up]])
    down_g = jnp.stack([cuts[3] + own_small[28, :per_output], own_small[4, :per_output]])
    norm_g = jnp.stack([cuts[4].reshape(4, per_output) + own_small[24:28, :per_output], own_small[0:4, :per_output]])
    return (
        layer_out.reshape(tokens.shape),
        d_x.reshape(tokens.shape),
        jnp.stack([mixed_sum[:per_project].T, g_project]),
        pair_g,
        jnp.stack([mixed_sum[per_project:].T, g_output]),
        out_g,
        jnp.stack([up_sum.T, g_up]),
        up_g,
        jnp.stack([down_sum, g_down]),
        down_g,
        norm_g[:, :2],
        norm_g[:, 2:],
        g_table,
    )


def solution(mesh):
    grid = Grid(mesh)
    rows, cols, last = P(AXES, None, None), P(None, AXES), P(None, None, AXES)
    middle = P(None, AXES, None)
    return jax.shard_map(
        functools.partial(shards, grid),
        mesh=mesh,
        in_specs=(
            rows, rows, P(), last, cols, last, cols, last, cols, middle, cols, last, last, cols,
        ),
        out_specs=(rows, rows, last, cols, last, cols, last, cols, middle, cols, last, last, cols),
        check_vma=False,
    )
```

```python
import functools
import math

import jax
import jax.numpy as jnp
from jax import lax
from jax.experimental import pallas as pl
from jax.experimental.pallas import tpu as pltpu
from jax.sharding import PartitionSpec as P

HEADS = 12
HEAD_DIM = 64
SEG_LEN = 128
LONG_SEGS = 64
SHORT_SEGS = 16
MESH = pl.DeviceIdType.MESH
AXES = ("dp", "fsdp")

highest = lax.Precision.HIGHEST
epsilon = 1e-06
masked_score = -1e30


class Grid:
    def __init__(self, mesh):
        self.dp, self.fsdp = mesh.shape["dp"], mesh.shape["fsdp"]
        twos = int(math.log2(self.dp))
        self.dims = (2,) * twos + (self.fsdp,)
        self.n = self.dp * self.fsdp
        self.last = len(self.dims) - 1
        self.most = max(self.dims) - 1
        middle = list(range(self.last - 1))
        self.orders = (
            [self.last] + middle[::-1] + [self.last - 1],
            [self.last] + middle + [self.last - 1],
        )

    def coords(self):
        dp, fs = lax.axis_index("dp"), lax.axis_index("fsdp")
        twos = self.last
        return tuple((dp // 2 ** (twos - 1 - i)) % 2 for i in range(twos)) + (fs,)

    def flat(self):
        return lax.axis_index("dp") * self.fsdp + lax.axis_index("fsdp")

    def peer(self, coords, dim, step):
        other = list(coords)
        other[dim] = lax.rem(coords[dim] + step, self.dims[dim])
        dp = 0
        for value in other[:-1]:
            dp = dp * 2 + value
        return (dp, other[-1]), other[dim]

    def greet(self, coords):
        self.meet(self.call(coords))

    def call(self, coords):
        barrier = pltpu.get_barrier_semaphore()
        count = 0
        for dim, size in enumerate(self.dims):
            for step in range(1, size):
                where, unused = self.peer(coords, dim, step)
                pl.semaphore_signal(barrier, inc=1, device_id=where, device_id_type=MESH)
                count += 1
        return count

    def meet(self, count):
        pl.semaphore_wait(pltpu.get_barrier_semaphore(), count)

    def sems(self, chunks):
        shape = (chunks, len(self.dims), self.most)
        return [pltpu.SemaphoreType.DMA(shape), pltpu.SemaphoreType.DMA(shape)]


def index_of(coords, free, ndims):
    return tuple(slice(None) if d in free else coords[d] for d in range(ndims))


def halves(rows, dtype):
    tile = 16 if dtype == jnp.bfloat16 else 8
    if rows % (2 * tile) == 0:
        return [(0, rows // 2, 0), (rows // 2, rows // 2, 1)]
    return [(0, rows, 0)]


class Gather:
    def __init__(self, grid, coords, chunks, send_sem, recv_sem, base=0):
        self.grid, self.coords, self.chunks = grid, coords, chunks
        self.send_sem, self.recv_sem, self.base = send_sem, recv_sem, base
        self.stages = len(grid.dims)

    def copies(self, k, stage):
        own, line, dest, first, rows, colour = self.chunks[k]
        grid, coords = self.grid, self.coords
        order = grid.orders[colour]
        dim = order[stage]
        cut = (pl.ds(first, rows),)
        if stage == 0:
            source = own.at[cut]
            target_ref = dest.at[coords + cut] if line is None else line.at[(coords[-1],) + cut]
        else:
            target_ref = dest.at[index_of(coords, order[:stage], len(grid.dims)) + cut]
            source = line.at[(slice(None),) + cut] if line is not None and stage == 1 else target_ref
        made = []
        for step in range(1, grid.dims[dim]):
            target, unused = grid.peer(coords, dim, step)
            made.append(
                pltpu.make_async_remote_copy(
                    source,
                    target_ref,
                    self.send_sem.at[self.base + k, stage, step - 1],
                    self.recv_sem.at[self.base + k, stage, step - 1],
                    device_id=target,
                    device_id_type=MESH,
                )
            )
        return made

    def start(self, k, stage):
        for copy in self.copies(k, stage):
            copy.start()

    def landed(self, k, stage):
        for copy in self.copies(k, stage):
            copy.wait_recv()

    def sent(self, k, first_stage, last_stage):
        for stage in range(first_stage, last_stage):
            for copy in self.copies(k, stage):
                copy.wait_send()


class Scatter:
    def __init__(self, grid, coords, chunks, send_sem, recv_sem, base=0):
        self.grid, self.coords, self.chunks = grid, coords, chunks
        self.send_sem, self.recv_sem, self.base = send_sem, recv_sem, base
        self.stages = len(grid.dims)

    @staticmethod
    def landing(grid, rows, width, dtype, colour):
        order = grid.orders[colour][::-1]
        made = []
        for stage, dim in enumerate(order):
            left = [grid.dims[d] for d in range(len(order)) if d in order[stage + 1 :]]
            made.append(pltpu.VMEM((grid.dims[dim] - 1, *left, rows, width), dtype))
        return made

    def copies(self, k, stage):
        held, lands, out, first, rows, colour = self.chunks[k]
        grid, coords = self.grid, self.coords
        order = grid.orders[colour][::-1]
        dim = order[stage]
        made = []
        for step in range(1, grid.dims[dim]):
            target, value = grid.peer(coords, dim, step)
            there = list(coords)
            there[dim] = value
            where = index_of(there, order[stage + 1 :], len(order)) + (pl.ds(first, rows),)
            made.append(
                pltpu.make_async_remote_copy(
                    held.at[where],
                    lands[stage].at[step - 1],
                    self.send_sem.at[self.base + k, stage, step - 1],
                    self.recv_sem.at[self.base + k, stage, step - 1],
                    device_id=target,
                    device_id_type=MESH,
                )
            )
        return made

    def start(self, k, stage):
        for copy in self.copies(k, stage):
            copy.start()

    def add(self, k, stage):
        for copy in self.copies(k, stage):
            copy.wait_recv()
        held, lands, out, first, rows, colour = self.chunks[k]
        grid, coords = self.grid, self.coords
        order = grid.orders[colour][::-1]
        land = lands[stage]
        where = index_of(coords, order[stage + 1 :], len(order)) + (pl.ds(first, rows),)
        total = held[where]
        final = stage == self.stages - 1
        if final:
            total = total.astype(jnp.float32)
        for step in range(grid.dims[order[stage]] - 1):
            total += land[step].astype(total.dtype)
        if final:
            out[pl.ds(first, rows)] = total
        else:
            held[where] = total

    def sent(self, k):
        for stage in range(self.stages):
            for copy in self.copies(k, stage):
                copy.wait_send()


def dot_nt(left, right):
    return lax.dot_general(
        left, right, (((1,), (1,)), ((), ())), preferred_element_type=jnp.float32
    )


def dot_nn(left, right):
    return lax.dot_general(
        left, right, (((1,), (0,)), ((), ())), preferred_element_type=jnp.float32
    )


def dot_tn(left, right):
    return lax.dot_general(
        left, right, (((0,), (0,)), ((), ())), preferred_element_type=jnp.float32
    )


def normalise(value):
    offset = value - jnp.mean(value, -1, keepdims=True)
    scale = lax.rsqrt(jnp.mean(offset * offset, -1, keepdims=True) + epsilon)
    return offset * scale, scale


def norm_back(grad, unit, scale, gain):
    pulled = grad * gain
    along = jnp.mean(pulled * unit, -1, keepdims=True)
    return scale * (pulled - jnp.mean(pulled, -1, keepdims=True) - unit * along)


def gelu_pair(x):
    bell = jnp.exp(-0.5 * x * x)
    t = 1.0 / (1.0 + (0.3275911 * 0.5**0.5) * jnp.abs(x))
    tail = t * (0.5 * 0.254829592 + t * (0.5 * -0.284496736 + t * (
        0.5 * 1.421413741 + t * (0.5 * -1.453152027 + t * (0.5 * 1.061405429)))))
    tail = tail * bell
    below = jnp.where(x < 0, tail, 1.0 - tail)
    return x * below, below + (x * 0.3989422804014327) * bell


def first_lanes():
    return lax.broadcasted_iota(jnp.int32, (1, 2 * HEAD_DIM), 1) < HEAD_DIM


def stack_heads(pair):
    zero = jnp.zeros_like(pair)
    left = first_lanes()
    return jnp.concatenate([jnp.where(left, pair, zero), jnp.where(left, zero, pair)], 0)


def unstack_heads(stacked):
    rows = stacked.shape[0] // 2
    return jnp.where(first_lanes(), stacked[:rows], stacked[rows:])


def pair_shares(query_stack, key_pair, allowed):
    scores = dot_nt(query_stack, key_pair)
    if allowed is not None:
        scores = jnp.where(allowed, scores, masked_score)
    raised = jnp.exp(scores - jnp.max(scores, -1, keepdims=True))
    return raised * (1.0 / jnp.sum(raised, -1, keepdims=True))


def attend_rows(qkv, mixed, rows, span, width, allowed):
    for start in range(0, rows, span):
        here = pl.ds(start, span)
        for p in range(width // (2 * HEAD_DIM)):
            at = p * 2 * HEAD_DIM
            query = stack_heads(qkv[here, pl.ds(at, 2 * HEAD_DIM)] * jnp.bfloat16(HEAD_DIM**-0.5))
            key = qkv[here, pl.ds(width + at, 2 * HEAD_DIM)]
            value = qkv[here, pl.ds(2 * width + at, 2 * HEAD_DIM)]
            shares = pair_shares(query, key, allowed)
            both = dot_nn(shares.astype(jnp.bfloat16), value)
            mixed[here, pl.ds(at, 2 * HEAD_DIM)] = unstack_heads(both).astype(jnp.bfloat16)


def attend_back(qkv, d_mixed, d_qkv, rows, span, width, allowed):
    scale = HEAD_DIM**-0.5
    for start in range(0, rows, span):
        here = pl.ds(start, span)
        for p in range(width // (2 * HEAD_DIM)):
            at = p * 2 * HEAD_DIM
            query = stack_heads(qkv[here, pl.ds(at, 2 * HEAD_DIM)] * jnp.bfloat16(scale))
            key = qkv[here, pl.ds(width + at, 2 * HEAD_DIM)]
            value = qkv[here, pl.ds(2 * width + at, 2 * HEAD_DIM)]
            grad = stack_heads(d_mixed[here, pl.ds(at, 2 * HEAD_DIM)])
            shares = pair_shares(query, key, allowed)
            d_shares = dot_nt(grad, value)
            delta = jnp.sum(shares * d_shares, -1, keepdims=True)
            d_scores = (shares * (d_shares - delta)).astype(jnp.bfloat16)
            d_query = unstack_heads(dot_nn(d_scores, key)) * scale
            d_key = dot_tn(d_scores, query)
            d_value = dot_tn(shares.astype(jnp.bfloat16), grad)
            d_qkv[here, pl.ds(at, 2 * HEAD_DIM)] = d_query.astype(jnp.bfloat16)
            d_qkv[here, pl.ds(width + at, 2 * HEAD_DIM)] = d_key.astype(jnp.bfloat16)
            d_qkv[here, pl.ds(2 * width + at, 2 * HEAD_DIM)] = d_value.astype(jnp.bfloat16)


def row_sums(value):
    return jnp.sum(value.astype(jnp.float32), 0, keepdims=True)


def whole(shape):
    return pl.BlockSpec(shape, lambda *i: (0,) * len(shape), pipeline_mode=pl.Buffered(1))


def select(rows, columns, first):
    row = lax.broadcasted_iota(jnp.int32, (rows, columns), 0)
    column = lax.broadcasted_iota(jnp.int32, (rows, columns), 1)
    return jnp.where(row == first + column, 1.0, 0.0).astype(jnp.bfloat16)


def spread_slots(rows_of_slots, n, per, size):
    columns = n * size
    step = min(columns, 768)
    out = []
    lane = lax.broadcasted_iota(jnp.int32, (128, 1), 0)
    slot = lax.broadcasted_iota(jnp.int32, (n * per, 1), 0) // per
    for c in range(0, columns, step):
        column = lax.broadcasted_iota(jnp.int32, (1, step), 1) + c
        ones = jnp.where(column % size == lane, 1.0, 0.0).astype(jnp.bfloat16)
        laid = dot_nn(rows_of_slots, ones)
        kept = jnp.where(slot == column // size, laid, 0.0)
        out.append(jnp.sum(kept.reshape(n, per, step), 0))
    return out[0] if len(out) == 1 else jnp.concatenate(out, 1)


SMALL_ROWS = 16


def misc_rows(per_output):
    return SMALL_ROWS + -(-per_output // 16) * 16


def weights_kernel(grid, sizes, *refs):
    width, per_project, per_output, per_up, per_pair, places_n = sizes
    n, ndims = grid.n, len(grid.dims)
    pw, ow, uw, dw, pb, ob, ub, db, ng, nb, pt, cot = refs[:12]
    mixed0, up0, down0, mixed1, up1, cot1, own_down1, vec, vec_pair, vec_up, table = refs[12:23]
    own_mixed, own_misc, misc_f, misc_all, own_cot, cot_head = refs[23:29]
    send_sem, recv_sem, local_sem = refs[29:]
    coords = grid.coords()
    me_line = coords[-1]
    cot_copy = pltpu.make_async_copy(cot.at[:, pl.ds(0, 8)], cot_head, local_sem.at[0])
    cot_copy.start()

    misc_f[...] = jnp.zeros_like(misc_f)
    at = 0
    for ref, size in ((pb, per_pair), (ob, per_output), (ub, per_up), (db, per_output)):
        misc_f[pl.ds(at, 2), pl.ds(0, size)] = ref[...].astype(jnp.float32)
        at += 2
    for ref in (ng, nb):
        for b in range(2):
            misc_f[pl.ds(at, 2), pl.ds(0, per_output)] = ref[b].astype(jnp.float32)
            at += 2
    misc_f[pl.ds(SMALL_ROWS, per_output), pl.ds(0, places_n)] = pt[...].astype(jnp.float32)
    own_misc[...] = misc_f[...].astype(jnp.bfloat16)

    def pack(b):
        rows = per_project + per_output
        own_mixed[b] = (
            dot_nn(place_rows(rows, per_project, 0), pw[b]) + dot_nn(place_rows(rows, per_output, per_project), ow[b])
        ).astype(jnp.bfloat16)

    def place_rows(rows, size, first):
        row = lax.broadcasted_iota(jnp.int32, (rows, size), 0)
        column = lax.broadcasted_iota(jnp.int32, (rows, size), 1)
        return jnp.where(row == first + column, 1.0, 0.0).astype(jnp.bfloat16)

    pack(0)
    grid.greet(coords)

    units, chunks = [], []

    def add(own, line, dest, cuts):
        for cut in cuts:
            chunks.append((own, line, dest, *cut))
        return list(range(len(chunks) - len(cuts), len(chunks)))

    mixed_rows = per_project + per_output
    units += [add(own_mixed.at[0], None, mixed0, u) for u in pairs(mixed_rows)]
    units[0] += add(own_misc, None, misc_all, [(0, misc_rows(per_output), 0)])
    up_units = len(units)
    units += [add(uw.at[0], None, up0, u) for u in pairs(per_up)]
    down_units = len(units)
    units += [add(dw.at[0], None, down0, u) for u in pairs(per_up)]
    line_units = [add(own_mixed.at[1], mixed1, None, [h]) for h in halves(mixed_rows, jnp.bfloat16)]
    line_units += [add(uw.at[1], up1, None, [h]) for h in halves(per_up, jnp.bfloat16)]
    line_units[0] += add(own_cot, cot1, None, [(0, own_cot.shape[0], 0)])
    gather = Gather(grid, coords, chunks, send_sem, recv_sem)

    def start(unit, stage):
        for k in unit:
            gather.start(k, stage)

    start(units[0], 0)
    pack(1)
    cot_copy.wait()
    for s in range(own_cot.shape[0]):
        own_cot[pl.ds(s, 1), :] = cot_head[s, 0:1, :]
    locals_ = [
        pltpu.make_async_copy(own_mixed.at[0], mixed0.at[coords], local_sem.at[0]),
        pltpu.make_async_copy(uw.at[0], up0.at[coords], local_sem.at[1]),
        pltpu.make_async_copy(dw.at[0], down0.at[coords], local_sem.at[2]),
        pltpu.make_async_copy(own_mixed.at[1], mixed1.at[me_line], local_sem.at[3]),
        pltpu.make_async_copy(uw.at[1], up1.at[me_line], local_sem.at[4]),
        pltpu.make_async_copy(dw.at[1], own_down1, local_sem.at[5]),
        pltpu.make_async_copy(own_cot, cot1.at[me_line], local_sem.at[6]),
    ]
    for copy in locals_:
        copy.start()
    misc_all[coords] = own_misc[...]
    for copy in locals_:
        copy.wait()

    def vectors():
        small = misc_all[..., 0:SMALL_ROWS, :].reshape(n * SMALL_ROWS, 128)
        singles = spread_slots(small, n, SMALL_ROWS, per_output)
        pairs = spread_slots(small, n, SMALL_ROWS, per_pair)
        ups = spread_slots(small, n, SMALL_ROWS, per_up)
        for b in range(2):
            vec[b, 0:1, :] = singles[2 + b : 3 + b]
            vec[b, 1:2, :] = singles[6 + b : 7 + b]
            vec[b, 2:4, :] = singles[8 + 2 * b : 10 + 2 * b]
            vec[b, 4:6, :] = singles[12 + 2 * b : 14 + 2 * b]
            vec[b, 6:8, :] = jnp.zeros((2, width), jnp.float32)
            vec_pair[b, :, 0:width] = pairs[b : b + 1, :width]
            vec_pair[b, :, width : 2 * width] = jnp.zeros((1, width), jnp.float32)
            vec_pair[b, :, 2 * width : 3 * width] = pairs[b : b + 1, width:]
            vec_up[b] = ups[4 + b : 5 + b]
        for d in range(n):
            where, rest = [], d
            for extent in grid.dims[::-1]:
                where.append(rest % extent)
                rest //= extent
            rows = misc_all[tuple(where[::-1]) + (pl.ds(SMALL_ROWS, misc_rows(per_output) - SMALL_ROWS),)].astype(jnp.float32)
            table[pl.ds(d * per_output, per_output), :] = rows[:per_output]

    count = len(units)
    line_ticks = {count - 6: line_units[:1], count - 4: line_units[1:2], count - 1: line_units[2:]} if count >= 7 else {0: line_units}
    for tick in range(1, count + ndims):
        for stage in range(1, ndims + 1):
            u = tick - stage
            if not 0 <= u < count:
                continue
            for k in units[u]:
                gather.landed(k, stage - 1)
                if stage < ndims:
                    gather.start(k, stage)
            if stage == 1:
                if u + 1 < count:
                    start(units[u + 1], 0)
                for unit in line_ticks.get(u, []):
                    start(unit, 0)
            if stage == ndims and u == 0:
                vectors()
    for unit in line_units:
        for k in unit:
            gather.landed(k, 0)
            gather.sent(k, 0, 1)
    for unit in units:
        for k in unit:
            gather.sent(k, 0, ndims)


def pairs(rows):
    if rows % 32:
        return [[(0, rows, 0)]]
    return [[(r, 16, 0), (r + 16, 16, 1)] for r in range(0, rows, 32)]


def gather_weights(grid, arrays, cid):
    project_weight, output_weight, up_weight, down_weight, project_bias = arrays[:5]
    per_project, per_output, per_up = project_weight.shape[1], output_weight.shape[1], up_weight.shape[1]
    width = project_weight.shape[2]
    per_pair = project_bias.shape[1]
    places_n = arrays[10].shape[1]
    segs = arrays[11].shape[0]
    n = grid.n
    low, full = jnp.bfloat16, jnp.float32
    mixed_rows = per_project + per_output
    small_rows = misc_rows(per_output)
    fs = grid.fsdp
    count = 2 + sum(len(u) for r in (mixed_rows, per_up, per_up) for u in pairs(r)) + sum(len(halves(r, low)) for r in (mixed_rows, per_up))
    vmem, anywhere = pl.BlockSpec(memory_space=pltpu.VMEM), pl.BlockSpec(memory_space=pl.ANY)

    def shape(s, d):
        return jax.ShapeDtypeStruct(s, d)

    return pl.pallas_call(
        functools.partial(weights_kernel, grid, (width, per_project, per_output, per_up, per_pair, places_n)),
        in_specs=[vmem] * 11 + [anywhere],
        out_specs=[anywhere] * 7 + [vmem] * 4,
        out_shape=[
            shape((*grid.dims, mixed_rows, width), low), shape((*grid.dims, per_up, width), low), shape((*grid.dims, per_up, width), low),
            shape((fs, mixed_rows, width), low), shape((fs, per_up, width), low), shape((fs, segs, width), full), shape((per_up, width), low),
            shape((2, 8, width), full), shape((2, 1, 3 * width), full), shape((2, 1, n * per_up), full), shape((width, 128), full),
        ],
        scratch_shapes=[
            pltpu.VMEM((2, mixed_rows, width), low),
            pltpu.VMEM((small_rows, 128), low), pltpu.VMEM((small_rows, 128), full), pltpu.VMEM((*grid.dims, small_rows, 128), low),
            pltpu.VMEM((segs, width), full), pltpu.VMEM((segs, 8, width), full),
        ]
        + grid.sems(count)
        + [pltpu.SemaphoreType.DMA((7,))],
        compiler_params=pltpu.CompilerParams(collective_id=cid, has_side_effects=True, vmem_limit_bytes=56 * 2**20),
        name="gather_weights",
    )(*arrays)


def forward_rows(x_low, x, w, r, rows, span, allowed, hook=lambda name: None):
    width = x.shape[1]
    step = width
    hook("project")
    for c in range(0, 3 * width, step):
        cut = pl.ds(c, step)
        r["qkv"][:, cut] = (dot_nt(x_low, w["project"][cut, :]) + w["project_b"][:, cut]).astype(jnp.bfloat16)
    attend_rows(r["qkv"], r["mixed"], rows, span, width, allowed)
    first = x + (dot_nt(r["mixed"][...], w["output"][...]) + w["output_b"])
    if "first" in r:
        r["first"](first)
    hook("first")
    unit_one, scale_one, unit_two, scale_two = feed_forward(first, w, r, hook)
    return unit_one, scale_one, unit_two, scale_two


def feed_forward(first, w, r, hook=lambda name: None):
    unit_one, scale_one = normalise(first)
    normed = unit_one * w["gains"][0:1, :] + w["shifts"][0:1, :]
    normed_low = normed.astype(jnp.bfloat16)
    r["normed"][...] = normed_low
    hidden_units = w["up"].shape[0]
    step = normed.shape[1]
    for c in range(0, hidden_units, step):
        cut = pl.ds(c, step)
        inner = dot_nt(normed_low, w["up"][cut, :]) + w["up_b"][:, cut]
        value, slope = gelu_pair(inner)
        r["hidden"][:, cut] = value.astype(jnp.bfloat16)
        r["slope"][:, cut] = slope.astype(r["slope"].dtype)
    hook("down")
    second = normed + (dot_nn(r["hidden"][...], w["down"][...]) + w["down_b"])
    unit_two, scale_two = normalise(second)
    return unit_one, scale_one, unit_two, scale_two


def mlp_back(grad, unit_one, scale_one, unit_two, scale_two, w, r, hook=lambda name: None):
    d_second = norm_back(grad, unit_two, scale_two, w["gains"][1:2, :])
    d_down = d_second.astype(jnp.bfloat16)
    r["d_down"][...] = d_down
    hidden_units = w["up"].shape[0]
    step = grad.shape[1]
    for c in range(0, hidden_units, step):
        cut = pl.ds(c, step)
        d_hidden = dot_nt(d_down, w["down"][cut, :])
        r["d_inner"][:, cut] = (d_hidden * r["slope"][:, cut].astype(jnp.float32)).astype(jnp.bfloat16)
    hook("up")
    d_normed = d_second + dot_nn(r["d_inner"][...], w["up"][...])
    d_first = norm_back(d_normed, unit_one, scale_one, w["gains"][0:1, :])
    sums = (
        row_sums(d_normed * unit_one), row_sums(grad * unit_two), row_sums(d_normed), row_sums(grad),
        row_sums(d_down), row_sums(r["d_inner"][...]),
    )
    return d_first, sums


def small_of(vec, vec_pair, vec_up, b):
    return {
        "project_b": vec_pair.at[b], "output_b": vec[b, 0:1, :], "up_b": vec_up.at[b], "down_b": vec[b, 1:2, :],
        "gains": vec[b, 2:4, :], "shifts": vec[b, 4:6, :],
    }


def unpack_mixed(grid, mixed, project, output, per_project):
    rows, width = mixed.shape[-2:]
    per_output = rows - per_project
    for d in range(grid.n):
        where, rest = [], d
        for size in grid.dims[::-1]:
            where.append(rest % size)
            rest //= size
        part = mixed[tuple(where[::-1])]
        project[pl.ds(d * per_project, per_project), :] = part[:per_project]
        output[pl.ds(d * per_output, per_output), :] = part[per_project:]


def spread(events, points):
    return [events[len(events) * p // points : len(events) * (p + 1) // points] for p in range(points)]


def segment_forward_kernel(grid, tile, steps, per_project, *refs):
    (tokens, grads, mixed0, up0, down0, vec, vec_pair, vec_up, line_mixed, line_up, line_cot, own_down) = refs[:12]
    names = ("qkv", "mixed", "d_first", "seg_low", "norm_sums", "up_sums")
    r = dict(zip(names, refs[12:18]))
    project_out, output_out, all_first, mixed1, up1, down1, all_cot, partial_up, partial_down = refs[18:27]
    r.update(zip(("slope", "normed", "hidden", "d_down", "d_inner"), refs[27:32]))
    held_mixed, project, output, up, down, own_first, sum_up, sum_down = refs[32:40]
    send_sem, recv_sem, local_sem = refs[40:]
    w = small_of(vec, vec_pair, vec_up, 0)
    w.update(project=project, output=output, up=up, down=down)
    width = tokens.shape[1]
    step = pl.program_id(0)
    last = steps - 1
    ndims = len(grid.dims)
    coords = grid.coords()
    loads = [pltpu.make_async_copy(*p, local_sem.at[i]) for i, p in enumerate(
        ((mixed0, held_mixed), (up0, up), (down0, down)))]
    stores = [pltpu.make_async_copy(*p, local_sem.at[3 + i]) for i, p in enumerate(
        ((project, project_out), (output, output_out)))]
    here = (coords[:-1]) + (slice(None),)
    lines = [pltpu.make_async_copy(a, b.at[here], local_sem.at[5 + i]) for i, (a, b) in enumerate(
        ((line_mixed, mixed1), (line_up, up1), (line_cot, all_cot)))]
    lines.append(pltpu.make_async_copy(own_down, down1.at[coords], local_sem.at[8]))
    keep_first = pltpu.make_async_copy(own_first, all_first.at[coords], local_sem.at[9])

    chunks, groups = [], []
    for own, line, dest, rows in (
        (None, line_mixed, mixed1, line_mixed.shape[1]), (None, line_up, up1, line_up.shape[1]), (own_down, None, down1, own_down.shape[0])
    ):
        cuts = halves(rows, jnp.bfloat16)
        groups.append(list(range(len(chunks), len(chunks) + len(cuts))))
        chunks += [(own, line, dest, *cut) for cut in cuts]
    groups[0].append(len(chunks))
    chunks.append((None, line_cot, all_cot, 0, line_cot.shape[1], 1))
    first_chunk = len(chunks)
    chunks.append((own_first, None, all_first, 0, own_first.shape[0], 0))
    gather = Gather(grid, coords, chunks, send_sem, recv_sem)

    ticks = ndims + 1

    def go(tick):
        if tick == 1:
            for copy in lines:
                copy.wait()
        for group in groups:
            late = chunks[group[0]][1] is None
            stage = tick if late else tick + 1
            for k in group:
                if stage > (0 if late else 1) and stage <= ndims:
                    gather.landed(k, stage - 1)
                if stage < ndims:
                    gather.start(k, stage)

    plan = {}
    for tick in range(1, ticks - 1):
        at = round((2 * steps - 1) * tick / (ticks - 2))
        if ndims == 4 and steps == 4:
            at = (1, 5, 7)[tick - 1]
        plan.setdefault(at, []).append(tick)

    def at_point(which):
        for at, some in plan.items():
            if at % 2 == which:

                @pl.when(step == at // 2)
                def _(some=some):
                    for tick in some:
                        go(tick)

    first_points = ["first", "down", "back", "up"]
    first_events = [[] for unused in first_points]
    stages = list(range(ndims))
    for i, stage in enumerate(stages):
        first_events[min(i, len(first_points) - 1)].append(stage)

    def first_point(name):
        @pl.when(step == last)
        def _():
            for stage in first_events[first_points.index(name)]:
                if stage == 0:
                    keep_first.start()
                else:
                    gather.landed(first_chunk, stage - 1)
                    if stage == 1:
                        keep_first.wait()
                gather.start(first_chunk, stage)

    @pl.when(step == 0)
    def _():
        for copy in loads:
            copy.start()
        grid.greet(coords)
        go(0)
        for copy in lines:
            copy.start()
        loads[0].wait()
        unpack_mixed(grid, held_mixed, project, output, per_project)
        for copy in stores:
            copy.start()

    def hook(name):
        if name == "first":
            first_point("first")

            @pl.when(step == 0)
            def _():
                for copy in loads[1:]:
                    copy.wait()

            at_point(0)
        if name == "down":
            first_point("down")
        if name == "up":
            first_point("up")

    def take_first(first):
        for s in range(tile // SEG_LEN):
            own_first[pl.ds(step * (tile // SEG_LEN) + s, 1), :] = first[s * SEG_LEN : s * SEG_LEN + 1]

    r["first"] = take_first
    x_low = tokens[...]
    x = x_low.astype(jnp.float32)
    unit_one, scale_one, unit_two, scale_two = forward_rows(x_low, x, w, r, tile, SEG_LEN, None, hook)
    seg_out = unit_two * w["gains"][1:2, :] + w["shifts"][1:2, :]
    r["seg_low"][...] = seg_out.astype(jnp.bfloat16)
    first_point("back")
    place = lax.broadcasted_iota(jnp.int32, (tile, 1), 0) % SEG_LEN
    grad = jnp.where(place == 0, 0.0, grads[...])
    d_first, sums = mlp_back(grad, unit_one, scale_one, unit_two, scale_two, w, r, hook)
    r["d_first"][...] = d_first
    gathered = jnp.concatenate(list(sums[:5]) + [jnp.zeros((3, width), jnp.float32)], 0)

    @pl.when(step == 0)
    def _():
        r["norm_sums"][...] = jnp.zeros_like(r["norm_sums"])
        r["up_sums"][...] = jnp.zeros_like(r["up_sums"])
        sum_up[...] = jnp.zeros_like(sum_up)
        sum_down[...] = jnp.zeros_like(sum_down)

    r["norm_sums"][...] += gathered
    r["up_sums"][...] += jnp.broadcast_to(sums[5], r["up_sums"].shape)
    for left, right, total in (("hidden", "d_down", sum_down), ("d_inner", "normed", sum_up)):
        for c in range(0, total.shape[0], width):
            total[pl.ds(c, width), :] += dot_tn(r[left][:, pl.ds(c, width)], r[right][...])
    at_point(1)

    @pl.when(step == last)
    def _():
        down[...] = sum_down[...].astype(jnp.bfloat16)
        up[...] = sum_up[...].astype(jnp.bfloat16)
        out = [pltpu.make_async_copy(*p, local_sem.at[i]) for i, p in enumerate(((down, partial_down), (up, partial_up)))]
        for copy in out:
            copy.start()
        go(ticks - 1)
        for g in range(len(groups)):
            for k in groups[g]:
                gather.sent(k, 1 if chunks[k][1] is not None else 0, ndims)
        gather.landed(first_chunk, ndims - 1)
        gather.sent(first_chunk, 0, ndims)
        for copy in stores + out:
            copy.wait()


def segment_forward(grid, tokens, grads, mixed0, up0, down0, smalls, lines, per_project, cid):
    rows, width = tokens.shape
    per_up = up0.shape[-2]
    mixed_rows = mixed0.shape[-2]
    hidden_units = per_up * grid.n
    tile = 2 * SEG_LEN
    steps = rows // tile
    segs = rows // SEG_LEN
    low, full = jnp.bfloat16, jnp.float32
    up0, down0 = up0.reshape(hidden_units, width), down0.reshape(hidden_units, width)
    count = 2 + sum(len(halves(r, low)) for r in (mixed_rows, per_up, per_up))
    vmem, anywhere = pl.BlockSpec(memory_space=pltpu.VMEM), pl.BlockSpec(memory_space=pl.ANY)

    def cut(columns):
        return pl.BlockSpec((tile, columns), lambda i: (i, 0))

    def shape(columns, dtype):
        return jax.ShapeDtypeStruct((rows, columns), dtype)

    return pl.pallas_call(
        functools.partial(segment_forward_kernel, grid, tile, steps, per_project),
        grid=(steps,),
        in_specs=[cut(width), cut(width)] + [anywhere] * 3 + [whole(s.shape) for s in (*smalls, *lines)],
        out_specs=[
            cut(3 * width), cut(width), cut(width), cut(width),
            pl.BlockSpec((8, width), lambda i: (0, 0)), pl.BlockSpec((8, hidden_units), lambda i: (0, 0)),
        ]
        + [anywhere] * 9,
        out_shape=[
            shape(3 * width, low), shape(width, low), shape(width, full), shape(width, low),
            jax.ShapeDtypeStruct((8, width), full), jax.ShapeDtypeStruct((8, hidden_units), full),
            jax.ShapeDtypeStruct((3 * width, width), low), jax.ShapeDtypeStruct((width, width), low),
            jax.ShapeDtypeStruct((*grid.dims, segs, width), full),
            jax.ShapeDtypeStruct((*grid.dims, mixed_rows, width), low),
            jax.ShapeDtypeStruct((*grid.dims, per_up, width), low), jax.ShapeDtypeStruct((*grid.dims, per_up, width), low),
            jax.ShapeDtypeStruct((*grid.dims, segs, width), full),
            jax.ShapeDtypeStruct((hidden_units, width), low), jax.ShapeDtypeStruct((hidden_units, width), low),
        ],
        scratch_shapes=[
            pltpu.VMEM((tile, hidden_units), low), pltpu.VMEM((tile, width), low), pltpu.VMEM((tile, hidden_units), low),
            pltpu.VMEM((tile, width), low), pltpu.VMEM((tile, hidden_units), low), pltpu.VMEM((*grid.dims, mixed_rows, width), low),
            pltpu.VMEM((3 * width, width), low), pltpu.VMEM((width, width), low),
            pltpu.VMEM((hidden_units, width), low), pltpu.VMEM((hidden_units, width), low), pltpu.VMEM((segs, width), full),
            pltpu.VMEM((hidden_units, width), full), pltpu.VMEM((hidden_units, width), full),
        ]
        + grid.sems(count)
        + [pltpu.SemaphoreType.DMA((10,))],
        compiler_params=pltpu.CompilerParams(collective_id=cid, has_side_effects=True, vmem_limit_bytes=60 * 2**20),
        name="segment_forward",
    )(tokens, grads, mixed0, up0, down0, *smalls, *lines)


def own_columns(value, first, size):
    return dot_nn(value, select(value.shape[1], size, first)).astype(jnp.bfloat16)


def own_sums(value, first, size):
    row = lax.broadcasted_iota(jnp.int32, (value.shape[1], size), 0)
    column = lax.broadcasted_iota(jnp.int32, (value.shape[1], size), 1)
    ones = jnp.where(row == first + column, 1.0, 0.0)
    return jnp.dot(value, ones, precision=highest, preferred_element_type=jnp.float32)


def document_of(placed, long_total):
    long_docs = long_total // LONG_SEGS
    is_long = placed < long_total
    rest = placed - long_total
    doc = jnp.where(is_long, placed // LONG_SEGS, long_docs + rest // SHORT_SEGS)
    return doc, jnp.where(is_long, placed % LONG_SEGS, rest % SHORT_SEGS)


def cross_kernel(grid, sizes, *refs):
    per_project, per_output, per_up, per_pair = sizes
    (firsts, grads, placed_row, placed_col, mixed1, up1, down1, up0, down0, vec, vec_pair, vec_up, table, partial) = refs[:14]
    g_project, g_output, g_up, g_down, z_up, down_sum, smalls, g_table, cross_own, d_first_own = refs[14:24]
    names = ("qkv", "slope", "d_mixed", "mixed", "normed", "hidden", "d_down", "d_inner", "d_qkv")
    r = dict(zip(names, refs[24:33]))
    held_mixed, project, output, up, down, z_up_w, z_down_w, z_slope, z_normed, z_hidden, z_d_down, z_d_inner, rows_f = refs[33:46]
    held, *lands, send_sem, recv_sem, local_sem = refs[46:]
    coords = grid.coords()
    reduce, ticks = summing(grid, coords, held, lands, down_sum, send_sem, recv_sem)
    load_partial = pltpu.make_async_copy(partial, held, local_sem.at[5])
    load_partial.start()
    loads = [pltpu.make_async_copy(*p, local_sem.at[i]) for i, p in enumerate(
        ((up0, z_up_w), (down0, z_down_w), (mixed1, held_mixed), (up1, up), (down1, down)))]
    for copy in loads:
        copy.start()
    expected = grid.call(coords)
    slots, width = firsts.shape
    places_n = LONG_SEGS
    me = grid.flat()
    per_slots = slots // grid.n

    w0 = small_of(vec, vec_pair, vec_up, 0)
    w0.update(up=z_up_w, down=z_down_w)
    r0 = {"normed": z_normed, "hidden": z_hidden, "slope": z_slope, "d_down": z_d_down, "d_inner": z_d_inner}

    def hook0(name):
        if name == "down":
            loads[1].wait()
            load_partial.wait()
            grid.meet(expected)
            reduce(0)

    loads[0].wait()
    kept0 = feed_forward(firsts[...], w0, r0, hook0)
    seg_first = kept0[2] * w0["gains"][1:2, :] + w0["shifts"][1:2, :]
    doc_row, unused = document_of(placed_row[...], slots // 2)
    doc_col, place_col = document_of(placed_col[...], slots // 2)
    picker = place_col == lax.broadcasted_iota(jnp.int32, (slots, places_n), 1)
    picker_f = jnp.where(picker, 1.0, 0.0)
    x = seg_first + dot_nt(picker_f.astype(jnp.bfloat16), table[:, 0:places_n].astype(jnp.bfloat16))

    w = small_of(vec, vec_pair, vec_up, 1)
    w.update(project=project, output=output, up=up, down=down)
    loads[2].wait()
    unpack_mixed(grid, held_mixed, project, output, per_project)
    x_low = x.astype(jnp.bfloat16)
    allowed = doc_col == doc_row
    allowed = jnp.concatenate([allowed, allowed], 0)
    reduce(1)

    def hook(name):
        if name == "first":
            loads[3].wait()
            reduce(2)
        if name == "down":
            loads[4].wait()

    kept = forward_rows(x_low, x, w, r, slots, slots, allowed, hook)
    mine = pl.ds(pl.multiple_of(me * per_slots, per_slots), per_slots)
    rows_f[...] = kept[2] * w["gains"][1:2, :] + w["shifts"][1:2, :]
    cross_own[...] = rows_f[mine, :]
    reduce(3)
    d_first, sums = mlp_back(grads[...], *kept, w, r)
    reduce(4)
    branch = d_first.astype(jnp.bfloat16)
    r["d_mixed"][...] = dot_nn(branch, output[...]).astype(jnp.bfloat16)
    attend_back(r["qkv"], r["d_mixed"], r["d_qkv"], slots, slots, width, allowed)
    d_x = d_first + dot_nn(r["d_qkv"][...], project[...])
    reduce(5)

    g_project[...] = dot_tn(own_columns(r["d_qkv"][...], me * per_project, per_project), x_low)
    g_output[...] = dot_tn(own_columns(branch, me * per_output, per_output), r["mixed"][...])
    g_up[...] = dot_tn(own_columns(r["d_inner"][...], me * per_up, per_up), r["normed"][...])
    g_down[...] = dot_tn(own_columns(r["hidden"][...], me * per_up, per_up), r["d_down"][...])
    smalls[...] = jnp.zeros_like(smalls)
    norm_rows = jnp.concatenate(list(sums[:5]) + [row_sums(branch), jnp.zeros((2, width), jnp.float32)], 0)
    smalls[0:8, 0:per_output] = own_sums(norm_rows, me * per_output, per_output)
    smalls[8:16, 0:per_up] = own_sums(jnp.broadcast_to(sums[5], (8, sums[5].shape[1])), me * per_up, per_up)
    qkv_sums = row_sums(r["d_qkv"][...])
    pair = jnp.concatenate([qkv_sums[:, :width], qkv_sums[:, 2 * width :]], 1)
    smalls[16:24, 0:per_pair] = own_sums(jnp.broadcast_to(pair, (8, 2 * width)), me * per_pair, per_pair)
    g_table[...] = lax.dot_general(
        own_sums(d_x, me * per_output, per_output), picker_f, (((0,), (0,)), ((), ())),
        precision=highest, preferred_element_type=jnp.float32,
    )

    d_first0, sums = mlp_back(d_x, *kept0, w0, r0)
    rows_f[...] = d_first0
    d_first_own[...] = rows_f[mine, :]
    z_up[...] = dot_tn(own_columns(z_d_inner[...], me * per_up, per_up), z_normed[...])
    z_down = dot_tn(own_columns(z_hidden[...], me * per_up, per_up), z_d_down[...])
    norm_rows = jnp.concatenate(list(sums[:5]) + [jnp.zeros((3, width), jnp.float32)], 0)
    smalls[24:32, 0:per_output] = own_sums(norm_rows, me * per_output, per_output)
    smalls[32:40, 0:per_up] = own_sums(jnp.broadcast_to(sums[5], (8, sums[5].shape[1])), me * per_up, per_up)
    for tick in range(6, ticks):
        reduce(tick)
    down_sum[...] += z_down
    reduce(None)


def summing(grid, coords, held, lands, out, send_sem, recv_sem):
    ndims = len(grid.dims)
    units = pairs(held.shape[-2])
    cuts = [cut for unit in units for cut in unit]
    chunks = [(held, lands[k * ndims : (k + 1) * ndims], out, *cut) for k, cut in enumerate(cuts)]
    scatter = Scatter(grid, coords, chunks, send_sem, recv_sem)
    per = len(units[0])

    def reduce(tick):
        if tick is None:
            for k in range(len(chunks)):
                scatter.sent(k)
            return
        for stage in range(ndims + 1):
            u = tick - stage
            if not 0 <= u < len(units):
                continue
            for k in range(u * per, (u + 1) * per):
                if stage > 0:
                    scatter.add(k, stage - 1)
                if stage < ndims:
                    scatter.start(k, stage)

    return reduce, len(units) + ndims


def summing_scratch(grid, rows, width):
    low = jnp.bfloat16
    cuts = [cut for unit in pairs(rows) for cut in unit]
    lands = [land for cut in cuts for land in Scatter.landing(grid, cut[1], width, low, cut[2])]
    return [pltpu.VMEM((*grid.dims, rows, width), low)] + lands + grid.sems(len(cuts))


def cross_block(grid, firsts, grads, placement, mixed1, up1, down1, up0, down0, smalls, table, sizes, partial, cid):
    slots, width = firsts.shape
    per_project, per_output, per_up, per_pair = sizes
    hidden_units = per_up * grid.n
    low, full = jnp.bfloat16, jnp.float32
    per_slots = slots // grid.n
    flat = lambda ref: ref.reshape(hidden_units, width)
    vmem, anywhere = pl.BlockSpec(memory_space=pltpu.VMEM), pl.BlockSpec(memory_space=pl.ANY)
    outs = [
        (per_project, width), (per_output, width), (per_up, width), (per_up, width), (per_up, width), (per_up, width),
        (40, 128), (per_output, LONG_SEGS), (per_slots, width), (per_slots, width),
    ]

    def held(*shape, dtype=low):
        return pltpu.VMEM(shape, dtype)

    return pl.pallas_call(
        functools.partial(cross_kernel, grid, sizes),
        in_specs=[vmem] * 4 + [anywhere] * 5 + [vmem] * 4 + [anywhere],
        out_specs=[vmem] * len(outs),
        out_shape=[jax.ShapeDtypeStruct(s, full) for s in outs],
        scratch_shapes=[
            held(slots, 3 * width), held(slots, hidden_units), held(slots, width), held(slots, width), held(slots, width),
            held(slots, hidden_units), held(slots, width), held(slots, hidden_units), held(slots, 3 * width),
            held(*mixed1.shape), held(3 * width, width), held(width, width), held(hidden_units, width), held(hidden_units, width),
            held(hidden_units, width), held(hidden_units, width), held(slots, hidden_units), held(slots, width),
            held(slots, hidden_units), held(slots, width), held(slots, hidden_units), held(slots, width, dtype=full),
            *summing_scratch(grid, per_up, width),
            pltpu.SemaphoreType.DMA((6,)),
        ],
        compiler_params=pltpu.CompilerParams(collective_id=cid, has_side_effects=True, vmem_limit_bytes=63 * 2**20),
        name="cross_block",
    )(firsts, grads, placement[None, :], placement[:, None], mixed1, flat(up1), flat(down1), flat(up0), flat(down0), *smalls, table, partial)


def segment_backward_kernel(grid, tile, steps, *refs):
    qkv, d_first, cls_grad, seg_low, cls_out, project, output, partial, cls_part = refs[:9]
    d_qkv, d_branch, d_x, layer_out, sums_qkv, sums_out, up_sum, d_mixed, held = refs[9:18]
    *lands, send_sem, recv_sem, local_sem = refs[18:]
    width = d_first.shape[1]
    step = pl.program_id(0)
    coords = grid.coords()
    reduce, ticks = summing(grid, coords, held, lands, up_sum, send_sem, recv_sem)
    plan = {}
    for tick in range(ticks - 1):
        plan.setdefault(min(2 * steps - 1, tick + 1), []).append(tick)

    def at_point(which):
        for at, stages in plan.items():
            if at % 2 == which:

                @pl.when(step == at // 2)
                def _(stages=stages):
                    for stage in stages:
                        if stage == 0:
                            load.wait()
                        reduce(stage)

    load = pltpu.make_async_copy(partial, held, local_sem.at[0])

    @pl.when(step == 0)
    def _():
        load.start()
        grid.greet(coords)
        sums_qkv[...] = jnp.zeros_like(sums_qkv)
        sums_out[...] = jnp.zeros_like(sums_out)

    at_point(0)
    place = lax.broadcasted_iota(jnp.int32, (tile, 1), 0)
    grad, out = d_first[...], seg_low[...].astype(jnp.float32)
    for s in range(tile // SEG_LEN):
        here = pl.ds(step * (tile // SEG_LEN) + s, 1)
        grad = jnp.where(place == s * SEG_LEN, cls_grad[here, :], grad)
        out = jnp.where(place == s * SEG_LEN, cls_out[here, :], out)
    layer_out[...] = out.astype(jnp.bfloat16)
    branch = grad.astype(jnp.bfloat16)
    d_branch[...] = branch
    d_mixed[...] = dot_nn(branch, output[...]).astype(jnp.bfloat16)
    attend_back(qkv, d_mixed, d_qkv, tile, SEG_LEN, width, None)
    at_point(1)
    d_x[...] = grad + dot_nn(d_qkv[...], project[...])
    sums_qkv[...] += jnp.broadcast_to(row_sums(d_qkv[...]), sums_qkv.shape)
    sums_out[...] += jnp.broadcast_to(row_sums(branch), sums_out.shape)

    @pl.when(step == steps - 1)
    def _():
        reduce(ticks - 1)
        up_sum[...] += cls_part[...]
        reduce(None)


def segment_backward(grid, qkv, d_first, cls_grad, seg_low, cls_out, project, output, partial, cls_part, cid):
    rows, width = d_first.shape
    tile = 2 * SEG_LEN
    low, full = jnp.bfloat16, jnp.float32
    per_up = partial.shape[-2]

    def cut(columns):
        return pl.BlockSpec((tile, columns), lambda i: (i, 0))

    return pl.pallas_call(
        functools.partial(segment_backward_kernel, grid, tile, rows // tile),
        grid=(rows // tile,),
        in_specs=[
            cut(3 * width), cut(width), whole(cls_grad.shape), cut(width), whole(cls_out.shape), whole(project.shape), whole(output.shape),
            pl.BlockSpec(memory_space=pl.ANY), whole(cls_part.shape),
        ],
        out_specs=[
            cut(3 * width), cut(width), cut(width), cut(width),
            pl.BlockSpec((8, 3 * width), lambda i: (0, 0)), pl.BlockSpec((8, width), lambda i: (0, 0)),
            pl.BlockSpec((per_up, width), lambda i: (0, 0)),
        ],
        out_shape=[
            jax.ShapeDtypeStruct((rows, 3 * width), low), jax.ShapeDtypeStruct((rows, width), low),
            jax.ShapeDtypeStruct((rows, width), full), jax.ShapeDtypeStruct((rows, width), low),
            jax.ShapeDtypeStruct((8, 3 * width), full), jax.ShapeDtypeStruct((8, width), full),
            jax.ShapeDtypeStruct((per_up, width), full),
        ],
        scratch_shapes=[
            pltpu.VMEM((tile, width), jnp.bfloat16), *summing_scratch(grid, per_up, width), pltpu.SemaphoreType.DMA((1,)),
        ],
        compiler_params=pltpu.CompilerParams(collective_id=cid, has_side_effects=True, vmem_limit_bytes=60 * 2**20),
        name="segment_backward",
    )(qkv, d_first, cls_grad, seg_low, cls_out, project, output, partial, cls_part)


def sum_kernel(grid, chunk_list, nparts, *refs):
    given, outs = refs[:nparts], refs[nparts : 2 * nparts]
    held = refs[2 * nparts : 3 * nparts]
    lands = refs[3 * nparts : -3]
    send_sem, recv_sem, load_sem = refs[-3:]
    ndims = len(grid.dims)
    coords = grid.coords()
    loads = [pltpu.make_async_copy(given[a], held[a], load_sem.at[a]) for a in range(nparts)]
    for load in loads:
        load.start()
    grid.greet(coords)
    chunks = [
        (held[a], lands[k * ndims : (k + 1) * ndims], outs[a], first, count, colour)
        for k, (a, first, count, colour, unit) in enumerate(chunk_list)
    ]
    scatter = Scatter(grid, coords, chunks, send_sem, recv_sem)
    loaded = set()
    units = sorted({c[4] for c in chunk_list})
    for tick in range(len(units) + ndims):
        for stage in range(ndims + 1):
            u = tick - stage
            if not 0 <= u < len(units):
                continue
            for k, (a, first, count, colour, unit) in enumerate(chunk_list):
                if unit != units[u]:
                    continue
                if a not in loaded:
                    loaded.add(a)
                    loads[a].wait()
                if stage >= 1:
                    scatter.add(k, stage - 1)
                if stage < ndims:
                    scatter.start(k, stage)
    for k in range(len(chunks)):
        scatter.sent(k)


def sum_to_owners(grid, parts, cid):
    chunk_list = []
    for a, p in enumerate(parts):
        for unit, cuts in enumerate(pairs(p.shape[1]) if p.dtype == jnp.bfloat16 else [halves(p.shape[1], p.dtype)]):
            chunk_list += [(a, *cut, unit) for cut in cuts]
    nparts = len(parts)
    shaped = [p.reshape(tuple(grid.dims) + p.shape[1:]) for p in parts]
    lands = []
    for a, first, count, colour, unit in chunk_list:
        lands += Scatter.landing(grid, count, parts[a].shape[2], parts[a].dtype, colour)
    return pl.pallas_call(
        functools.partial(sum_kernel, grid, chunk_list, nparts),
        out_shape=[jax.ShapeDtypeStruct(p.shape[1:], jnp.float32) for p in parts],
        in_specs=[pl.BlockSpec(memory_space=pl.ANY)] * nparts,
        out_specs=[pl.BlockSpec(memory_space=pltpu.VMEM)] * nparts,
        scratch_shapes=[pltpu.VMEM(s.shape, s.dtype) for s in shaped] + lands + grid.sems(len(chunk_list)) + [pltpu.SemaphoreType.DMA((nparts,))],
        compiler_params=pltpu.CompilerParams(collective_id=cid, has_side_effects=True, vmem_limit_bytes=56 * 2**20),
        name="sum_to_owners",
    )(*shaped)


class Held:
    def __init__(self, value):
        self.value = value

    @property
    def shape(self):
        return self.value.shape

    @property
    def dtype(self):
        return self.value.dtype

    @staticmethod
    def plain(where):
        where = where if isinstance(where, tuple) else (where,)
        return tuple(slice(w.start, w.start + w.size) if isinstance(w, pl.Slice) else w for w in where)

    def __getitem__(self, where):
        return self.value[self.plain(where)]

    def __setitem__(self, where, value):
        self.value = self.value.at[self.plain(where)].set(value)


def cross_plain(grid, firsts, grads, placement, mixed1, up1, down1, up0, down0, smalls, table, sizes, partial, cid):
    slots, width = firsts.shape
    per_project, per_output, per_up, per_pair = sizes
    hidden_units = per_up * grid.n
    me = grid.flat()
    vec, vec_pair, vec_up = smalls

    def weights(b, up, down):
        return {
            "project_b": vec_pair[b], "output_b": vec[b, 0:1, :], "up_b": vec_up[b], "down_b": vec[b, 1:2, :],
            "gains": vec[b, 2:4, :], "shifts": vec[b, 4:6, :],
            "up": up.reshape(hidden_units, width), "down": down.reshape(hidden_units, width),
        }

    def blank(columns):
        return Held(jnp.zeros((slots, columns), jnp.bfloat16))

    def store():
        made = {k: blank(width) for k in ("mixed", "normed", "d_down", "d_mixed")}
        made.update({k: blank(hidden_units) for k in ("hidden", "slope", "d_inner")})
        made.update(qkv=blank(3 * width), d_qkv=blank(3 * width))
        return made

    def cut(matrix, size, axis=1):
        return lax.dynamic_slice_in_dim(matrix, me * size, size, axis)

    w0, w, r0, r = weights(0, up0, down0), weights(1, up1, down1), store(), store()
    parts = mixed1.reshape(grid.n, -1, width)
    w["project"] = parts[:, :per_project].reshape(3 * width, width)
    w["output"] = parts[:, per_project:].reshape(width, width)
    kept0 = feed_forward(firsts, w0, r0)
    seg_first = kept0[2] * w0["gains"][1:2, :] + w0["shifts"][1:2, :]
    doc, place = document_of(placement, slots // 2)
    picker = jnp.where(place[:, None] == jnp.arange(LONG_SEGS, dtype=jnp.int32)[None, :], 1.0, 0.0)
    x = seg_first + dot_nt(picker.astype(jnp.bfloat16), table[:, :LONG_SEGS].astype(jnp.bfloat16))
    x_low = x.astype(jnp.bfloat16)
    allowed = doc[:, None] == doc[None, :]
    allowed = jnp.concatenate([allowed, allowed], 0)
    kept = forward_rows(x_low, x, w, r, slots, slots, allowed)
    out = kept[2] * w["gains"][1:2, :] + w["shifts"][1:2, :]
    d_first, sums = mlp_back(grads, *kept, w, r)
    branch = d_first.astype(jnp.bfloat16)
    r["d_mixed"][...] = dot_nn(branch, w["output"]).astype(jnp.bfloat16)
    attend_back(r["qkv"], r["d_mixed"], r["d_qkv"], slots, slots, width, allowed)
    d_x = d_first + dot_nn(r["d_qkv"][...], w["project"])
    d_first0, sums0 = mlp_back(d_x, *kept0, w0, r0)
    qkv_sums = row_sums(r["d_qkv"][...])
    pair = jnp.concatenate([qkv_sums[:, :width], qkv_sums[:, 2 * width :]], 1)

    def laid(rows, size):
        rows = cut(rows, size)
        return jnp.pad(rows, ((0, 8 - rows.shape[0]), (0, 128 - size)))

    own_small = jnp.concatenate(
        [
            laid(jnp.concatenate(list(sums[:5]) + [row_sums(branch)], 0), per_output), laid(sums[5], per_up), laid(pair, per_pair),
            laid(jnp.concatenate(list(sums0[:5]), 0), per_output), laid(sums0[5], per_up),
        ],
        0,
    )
    g_table = lax.dot_general(cut(d_x, per_output), picker, (((0,), (0,)), ((), ())), precision=highest)
    per_slots = slots // grid.n
    return (
        dot_tn(cut(r["d_qkv"][...], per_project), x_low), dot_tn(cut(branch, per_output), r["mixed"][...]),
        dot_tn(cut(r["d_inner"][...], per_up), r["normed"][...]), dot_tn(cut(r["hidden"][...], per_up), r["d_down"][...]),
        dot_tn(cut(r0["d_inner"][...], per_up), r0["normed"][...]), dot_tn(cut(r0["hidden"][...], per_up), r0["d_down"][...]) + sum_to_owners(grid, [partial.reshape(grid.n, per_up, width)], cid)[0],
        own_small, g_table, cut(out, per_slots, 0), cut(d_first0, per_slots, 0),
    )


def shards(
    grid,
    tokens,
    cotangent,
    placement,
    project_weight,
    project_bias,
    output_weight,
    output_bias,
    up_weight,
    up_bias,
    down_weight,
    down_bias,
    norm_gain,
    norm_bias,
    position_table,
):
    n = grid.n
    seg_count, seg_len, width = tokens.shape
    slots, rows = placement.shape[0], seg_count * seg_len
    per_project, per_output = project_weight.shape[2], output_weight.shape[2]
    per_pair, per_up = project_bias.shape[1], up_bias.shape[1]
    sizes = (per_project, per_output, per_up, per_pair)
    low_tokens = tokens.reshape(rows, width)

    mixed0, up0, down0, *lines, vec, vec_pair, vec_up, table = gather_weights(
        grid,
        [*(jnp.swapaxes(w, 1, 2) for w in (project_weight, output_weight, up_weight)), down_weight,
         project_bias, output_bias, up_bias, down_bias, norm_gain, norm_bias, position_table.T, cotangent],
        0,
    )
    smalls = [vec, vec_pair, vec_up]
    (qkv, mixed, d_first, seg_low, norm_sums, up_sums, project, output, all_first,
     mixed1, up1, down1, all_cot, partial_up, partial_down) = segment_forward(
        grid, low_tokens, cotangent.reshape(rows, width), mixed0, up0, down0, smalls, lines, per_project, 1
    )
    partial_up, partial_down = [p.reshape(*grid.dims, per_up, width) for p in (partial_up, partial_down)]
    g_project, g_output, g_up, g_down, z_up, down_sum, own_small, g_table, cross_own, cls_grad = (cross_block if slots <= 256 else cross_plain)(
        grid, all_first.reshape(slots, width), all_cot.reshape(slots, width), placement, mixed1, up1, down1, up0, down0,
        smalls, table, sizes, partial_down, 2,
    )
    d_qkv, d_branch, d_x, layer_out, sums_qkv, sums_out, up_sum = segment_backward(
        grid, qkv, d_first, cls_grad, seg_low, cross_own, project, output, partial_up, z_up, 3
    )
    grad_project, grad_output = [
        dot_tn(left, right).astype(jnp.bfloat16).reshape(n, -1, width)
        for left, right in ((d_qkv, low_tokens), (d_branch, mixed))
    ]

    def per_device(vector):
        return vector.reshape(vector.shape[:-1] + (n, -1))

    seg_small = jnp.concatenate(
        [
            per_device(jnp.concatenate([sums_qkv[0, :width], sums_qkv[0, 2 * width :]])), per_device(sums_out[0]),
            per_device(up_sums[0]), per_device(norm_sums[4]),
            per_device(norm_sums[:4]).transpose(1, 0, 2).reshape(n, -1),
        ],
        1,
    )
    small_size = seg_small.shape[1]
    small_width = -(-small_size // 128) * 128
    seg_small = jnp.pad(seg_small[:, None], ((0, 0), (0, 7), (0, small_width - small_size)))
    mixed_sum, small_sum = sum_to_owners(grid, [jnp.concatenate([grad_project, grad_output], 1), seg_small], 4)
    cuts, at = [], 0
    for size in (per_pair, per_output, per_up, per_output, 4 * per_output):
        cuts.append(small_sum[0, at : at + size])
        at += size
    pair_g = jnp.stack([cuts[0], own_small[16, :per_pair]])
    out_g = jnp.stack([cuts[1], own_small[5, :per_output]])
    up_g = jnp.stack([cuts[2] + own_small[32, :per_up], own_small[8, :per_up]])
    down_g = jnp.stack([cuts[3] + own_small[28, :per_output], own_small[4, :per_output]])
    norm_g = jnp.stack([cuts[4].reshape(4, per_output) + own_small[24:28, :per_output], own_small[0:4, :per_output]])
    return (
        layer_out.reshape(tokens.shape),
        d_x.reshape(tokens.shape),
        jnp.swapaxes(jnp.stack([mixed_sum[:per_project], g_project]), 1, 2),
        pair_g,
        jnp.swapaxes(jnp.stack([mixed_sum[per_project:], g_output]), 1, 2),
        out_g,
        jnp.swapaxes(jnp.stack([up_sum, g_up]), 1, 2),
        up_g,
        jnp.stack([down_sum, g_down]),
        down_g,
        norm_g[:, :2],
        norm_g[:, 2:],
        g_table.T,
    )


def solution(mesh):
    grid = Grid(mesh)
    rows, cols, last = P(AXES, None, None), P(None, AXES), P(None, None, AXES)
    middle = P(None, AXES, None)
    return jax.shard_map(
        functools.partial(shards, grid),
        mesh=mesh,
        in_specs=(
            rows, rows, P(), last, cols, last, cols, last, cols, middle, cols, last, last, cols,
        ),
        out_specs=(rows, rows, last, cols, last, cols, last, cols, middle, cols, last, last, cols),
        check_vma=False,
    )
```

```python
import functools
import math

import jax
import jax.numpy as jnp
from jax import lax
from jax.experimental import pallas as pl
from jax.experimental.pallas import tpu as pltpu
from jax.sharding import PartitionSpec as P

HEADS = 12
HEAD_DIM = 64
SEG_LEN = 128
LONG_SEGS = 64
SHORT_SEGS = 16
MESH = pl.DeviceIdType.MESH
AXES = ("dp", "fsdp")

highest = lax.Precision.HIGHEST
epsilon = 1e-06
masked_score = -1e30


class Grid:
    def __init__(self, mesh):
        self.dp, self.fsdp = mesh.shape["dp"], mesh.shape["fsdp"]
        twos = int(math.log2(self.dp))
        self.dims = (2,) * twos + (self.fsdp,)
        self.n = self.dp * self.fsdp
        self.last = len(self.dims) - 1
        self.most = max(self.dims) - 1
        middle = list(range(self.last - 1))
        self.orders = (
            [self.last] + middle[::-1] + [self.last - 1],
            [self.last] + middle + [self.last - 1],
        )

    def coords(self):
        dp, fs = lax.axis_index("dp"), lax.axis_index("fsdp")
        twos = self.last
        return tuple((dp // 2 ** (twos - 1 - i)) % 2 for i in range(twos)) + (fs,)

    def flat(self):
        return lax.axis_index("dp") * self.fsdp + lax.axis_index("fsdp")

    def peer(self, coords, dim, step):
        other = list(coords)
        other[dim] = lax.rem(coords[dim] + step, self.dims[dim])
        dp = 0
        for value in other[:-1]:
            dp = dp * 2 + value
        return (dp, other[-1]), other[dim]

    def greet(self, coords):
        self.meet(self.call(coords))

    def call(self, coords):
        barrier = pltpu.get_barrier_semaphore()
        count = 0
        for dim, size in enumerate(self.dims):
            for step in range(1, size):
                where, unused = self.peer(coords, dim, step)
                pl.semaphore_signal(barrier, inc=1, device_id=where, device_id_type=MESH)
                count += 1
        return count

    def meet(self, count):
        pl.semaphore_wait(pltpu.get_barrier_semaphore(), count)

    def sems(self, chunks):
        shape = (chunks, len(self.dims), self.most)
        return [pltpu.SemaphoreType.DMA(shape), pltpu.SemaphoreType.DMA(shape)]


def index_of(coords, free, ndims):
    return tuple(slice(None) if d in free else coords[d] for d in range(ndims))


def halves(rows, dtype):
    tile = 16 if dtype == jnp.bfloat16 else 8
    if rows % (2 * tile) == 0:
        return [(0, rows // 2, 0), (rows // 2, rows // 2, 1)]
    return [(0, rows, 0)]


class Gather:
    def __init__(self, grid, coords, chunks, send_sem, recv_sem, base=0):
        self.grid, self.coords, self.chunks = grid, coords, chunks
        self.send_sem, self.recv_sem, self.base = send_sem, recv_sem, base
        self.stages = len(grid.dims)

    def copies(self, k, stage):
        own, line, dest, first, rows, colour = self.chunks[k]
        grid, coords = self.grid, self.coords
        order = grid.orders[colour]
        dim = order[stage]
        cut = (pl.ds(first, rows),)
        if stage == 0:
            source = own.at[cut]
            target_ref = dest.at[coords + cut] if line is None else line.at[(coords[-1],) + cut]
        else:
            target_ref = dest.at[index_of(coords, order[:stage], len(grid.dims)) + cut]
            source = line.at[(slice(None),) + cut] if line is not None and stage == 1 else target_ref
        made = []
        for step in range(1, grid.dims[dim]):
            target, unused = grid.peer(coords, dim, step)
            made.append(
                pltpu.make_async_remote_copy(
                    source,
                    target_ref,
                    self.send_sem.at[self.base + k, stage, step - 1],
                    self.recv_sem.at[self.base + k, stage, step - 1],
                    device_id=target,
                    device_id_type=MESH,
                )
            )
        return made

    def start(self, k, stage):
        for copy in self.copies(k, stage):
            copy.start()

    def landed(self, k, stage):
        for copy in self.copies(k, stage):
            copy.wait_recv()

    def sent(self, k, first_stage, last_stage):
        for stage in range(first_stage, last_stage):
            for copy in self.copies(k, stage):
                copy.wait_send()


class Scatter:
    def __init__(self, grid, coords, chunks, send_sem, recv_sem, base=0):
        self.grid, self.coords, self.chunks = grid, coords, chunks
        self.send_sem, self.recv_sem, self.base = send_sem, recv_sem, base
        self.stages = len(grid.dims)

    @staticmethod
    def landing(grid, rows, width, dtype, colour):
        order = grid.orders[colour][::-1]
        made = []
        for stage, dim in enumerate(order):
            left = [grid.dims[d] for d in range(len(order)) if d in order[stage + 1 :]]
            made.append(pltpu.VMEM((grid.dims[dim] - 1, *left, rows, width), dtype))
        return made

    def copies(self, k, stage):
        held, lands, out, first, rows, colour = self.chunks[k]
        grid, coords = self.grid, self.coords
        order = grid.orders[colour][::-1]
        dim = order[stage]
        made = []
        for step in range(1, grid.dims[dim]):
            target, value = grid.peer(coords, dim, step)
            there = list(coords)
            there[dim] = value
            where = index_of(there, order[stage + 1 :], len(order)) + (pl.ds(first, rows),)
            made.append(
                pltpu.make_async_remote_copy(
                    held.at[where],
                    lands[stage].at[step - 1],
                    self.send_sem.at[self.base + k, stage, step - 1],
                    self.recv_sem.at[self.base + k, stage, step - 1],
                    device_id=target,
                    device_id_type=MESH,
                )
            )
        return made

    def start(self, k, stage):
        for copy in self.copies(k, stage):
            copy.start()

    def add(self, k, stage):
        for copy in self.copies(k, stage):
            copy.wait_recv()
        held, lands, out, first, rows, colour = self.chunks[k]
        grid, coords = self.grid, self.coords
        order = grid.orders[colour][::-1]
        land = lands[stage]
        where = index_of(coords, order[stage + 1 :], len(order)) + (pl.ds(first, rows),)
        total = held[where]
        final = stage == self.stages - 1
        if final:
            total = total.astype(jnp.float32)
        for step in range(grid.dims[order[stage]] - 1):
            total += land[step].astype(total.dtype)
        if final:
            out[pl.ds(first, rows)] = total
        else:
            held[where] = total

    def sent(self, k):
        for stage in range(self.stages):
            for copy in self.copies(k, stage):
                copy.wait_send()


def dot_nt(left, right):
    return lax.dot_general(
        left, right, (((1,), (1,)), ((), ())), preferred_element_type=jnp.float32
    )


def dot_nn(left, right):
    return lax.dot_general(
        left, right, (((1,), (0,)), ((), ())), preferred_element_type=jnp.float32
    )


def dot_tn(left, right):
    return lax.dot_general(
        left, right, (((0,), (0,)), ((), ())), preferred_element_type=jnp.float32
    )


def normalise(value):
    offset = value - jnp.mean(value, -1, keepdims=True)
    scale = lax.rsqrt(jnp.mean(offset * offset, -1, keepdims=True) + epsilon)
    return offset * scale, scale


def norm_back(grad, unit, scale, gain):
    pulled = grad * gain
    along = jnp.mean(pulled * unit, -1, keepdims=True)
    return scale * (pulled - jnp.mean(pulled, -1, keepdims=True) - unit * along)


def gelu_pair(x):
    bell = jnp.exp(-0.5 * x * x)
    t = 1.0 / (1.0 + (0.3275911 * 0.5**0.5) * jnp.abs(x))
    tail = t * (0.5 * 0.254829592 + t * (0.5 * -0.284496736 + t * (
        0.5 * 1.421413741 + t * (0.5 * -1.453152027 + t * (0.5 * 1.061405429)))))
    tail = tail * bell
    below = jnp.where(x < 0, tail, 1.0 - tail)
    return x * below, below + (x * 0.3989422804014327) * bell


def first_lanes():
    return lax.broadcasted_iota(jnp.int32, (1, 2 * HEAD_DIM), 1) < HEAD_DIM


def stack_heads(pair):
    zero = jnp.zeros_like(pair)
    left = first_lanes()
    return jnp.concatenate([jnp.where(left, pair, zero), jnp.where(left, zero, pair)], 0)


def unstack_heads(stacked):
    rows = stacked.shape[0] // 2
    return jnp.where(first_lanes(), stacked[:rows], stacked[rows:])


def pair_shares(query_stack, key_pair, allowed):
    scores = dot_nt(query_stack, key_pair)
    if allowed is not None:
        scores = jnp.where(allowed, scores, masked_score)
    raised = jnp.exp(scores - jnp.max(scores, -1, keepdims=True))
    return raised * (1.0 / jnp.sum(raised, -1, keepdims=True))


def attend_rows(qkv, mixed, rows, span, width, allowed):
    for start in range(0, rows, span):
        here = pl.ds(start, span)
        for p in range(width // (2 * HEAD_DIM)):
            at = p * 2 * HEAD_DIM
            query = stack_heads(qkv[here, pl.ds(at, 2 * HEAD_DIM)] * jnp.bfloat16(HEAD_DIM**-0.5))
            key = qkv[here, pl.ds(width + at, 2 * HEAD_DIM)]
            value = qkv[here, pl.ds(2 * width + at, 2 * HEAD_DIM)]
            shares = pair_shares(query, key, allowed)
            both = dot_nn(shares.astype(jnp.bfloat16), value)
            mixed[here, pl.ds(at, 2 * HEAD_DIM)] = unstack_heads(both).astype(jnp.bfloat16)


def attend_back(qkv, d_mixed, d_qkv, rows, span, width, allowed):
    scale = HEAD_DIM**-0.5
    for start in range(0, rows, span):
        here = pl.ds(start, span)
        for p in range(width // (2 * HEAD_DIM)):
            at = p * 2 * HEAD_DIM
            query = stack_heads(qkv[here, pl.ds(at, 2 * HEAD_DIM)] * jnp.bfloat16(scale))
            key = qkv[here, pl.ds(width + at, 2 * HEAD_DIM)]
            value = qkv[here, pl.ds(2 * width + at, 2 * HEAD_DIM)]
            grad = stack_heads(d_mixed[here, pl.ds(at, 2 * HEAD_DIM)])
            shares = pair_shares(query, key, allowed)
            d_shares = dot_nt(grad, value)
            delta = jnp.sum(shares * d_shares, -1, keepdims=True)
            d_scores = (shares * (d_shares - delta)).astype(jnp.bfloat16)
            d_query = unstack_heads(dot_nn(d_scores, key)) * scale
            d_key = dot_tn(d_scores, query)
            d_value = dot_tn(shares.astype(jnp.bfloat16), grad)
            d_qkv[here, pl.ds(at, 2 * HEAD_DIM)] = d_query.astype(jnp.bfloat16)
            d_qkv[here, pl.ds(width + at, 2 * HEAD_DIM)] = d_key.astype(jnp.bfloat16)
            d_qkv[here, pl.ds(2 * width + at, 2 * HEAD_DIM)] = d_value.astype(jnp.bfloat16)


def row_sums(value):
    return jnp.sum(value.astype(jnp.float32), 0, keepdims=True)


def whole(shape):
    return pl.BlockSpec(shape, lambda *i: (0,) * len(shape), pipeline_mode=pl.Buffered(1))


def select(rows, columns, first):
    row = lax.broadcasted_iota(jnp.int32, (rows, columns), 0)
    column = lax.broadcasted_iota(jnp.int32, (rows, columns), 1)
    return jnp.where(row == first + column, 1.0, 0.0).astype(jnp.bfloat16)


def spread_slots(rows_of_slots, n, per, size):
    columns = n * size
    step = min(columns, 768)
    out = []
    lane = lax.broadcasted_iota(jnp.int32, (128, 1), 0)
    slot = lax.broadcasted_iota(jnp.int32, (n * per, 1), 0) // per
    for c in range(0, columns, step):
        column = lax.broadcasted_iota(jnp.int32, (1, step), 1) + c
        ones = jnp.where(column % size == lane, 1.0, 0.0).astype(jnp.bfloat16)
        laid = dot_nn(rows_of_slots, ones)
        kept = jnp.where(slot == column // size, laid, 0.0)
        out.append(jnp.sum(kept.reshape(n, per, step), 0))
    return out[0] if len(out) == 1 else jnp.concatenate(out, 1)


SMALL_ROWS = 16


def misc_rows(per_output):
    return SMALL_ROWS + -(-per_output // 16) * 16


def weights_kernel(grid, sizes, *refs):
    width, per_project, per_output, per_up, per_pair, places_n = sizes
    n, ndims = grid.n, len(grid.dims)
    pw, ow, uw, dw, pb, ob, ub, db, ng, nb, pt, cot = refs[:12]
    mixed0, up0, down0, mixed1, up1, cot1, own_down1, vec, vec_pair, vec_up, table = refs[12:23]
    own_mixed, own_misc, misc_f, misc_all, own_cot, cot_head = refs[23:29]
    send_sem, recv_sem, local_sem = refs[29:]
    coords = grid.coords()
    me_line = coords[-1]
    cot_copy = pltpu.make_async_copy(cot.at[:, pl.ds(0, 8)], cot_head, local_sem.at[0])
    cot_copy.start()

    misc_f[...] = jnp.zeros_like(misc_f)
    at = 0
    for ref, size in ((pb, per_pair), (ob, per_output), (ub, per_up), (db, per_output)):
        misc_f[pl.ds(at, 2), pl.ds(0, size)] = ref[...].astype(jnp.float32)
        at += 2
    for ref in (ng, nb):
        for b in range(2):
            misc_f[pl.ds(at, 2), pl.ds(0, per_output)] = ref[b].astype(jnp.float32)
            at += 2
    misc_f[pl.ds(SMALL_ROWS, per_output), pl.ds(0, places_n)] = pt[...].astype(jnp.float32)
    own_misc[...] = misc_f[...].astype(jnp.bfloat16)

    def pack(b):
        rows = per_project + per_output
        own_mixed[b] = (
            dot_nn(place_rows(rows, per_project, 0), pw[b]) + dot_nn(place_rows(rows, per_output, per_project), ow[b])
        ).astype(jnp.bfloat16)

    def place_rows(rows, size, first):
        row = lax.broadcasted_iota(jnp.int32, (rows, size), 0)
        column = lax.broadcasted_iota(jnp.int32, (rows, size), 1)
        return jnp.where(row == first + column, 1.0, 0.0).astype(jnp.bfloat16)

    pack(0)
    grid.greet(coords)

    units, chunks = [], []

    def add(own, line, dest, cuts):
        for cut in cuts:
            chunks.append((own, line, dest, *cut))
        return list(range(len(chunks) - len(cuts), len(chunks)))

    mixed_rows = per_project + per_output
    units += [add(own_mixed.at[0], None, mixed0, u) for u in pairs(mixed_rows)]
    units[0] += add(own_misc, None, misc_all, [(0, misc_rows(per_output), 0)])
    up_units = len(units)
    units += [add(uw.at[0], None, up0, u) for u in pairs(per_up)]
    down_units = len(units)
    units += [add(dw.at[0], None, down0, u) for u in pairs(per_up)]
    line_units = [add(own_mixed.at[1], mixed1, None, [h]) for h in halves(mixed_rows, jnp.bfloat16)]
    line_units += [add(uw.at[1], up1, None, [h]) for h in halves(per_up, jnp.bfloat16)]
    line_units[0] += add(own_cot, cot1, None, [(0, own_cot.shape[0], 0)])
    gather = Gather(grid, coords, chunks, send_sem, recv_sem)

    def start(unit, stage):
        for k in unit:
            gather.start(k, stage)

    start(units[0], 0)
    pack(1)
    cot_copy.wait()
    for s in range(own_cot.shape[0]):
        own_cot[pl.ds(s, 1), :] = cot_head[s, 0:1, :]
    locals_ = [
        pltpu.make_async_copy(own_mixed.at[0], mixed0.at[coords], local_sem.at[0]),
        pltpu.make_async_copy(uw.at[0], up0.at[coords], local_sem.at[1]),
        pltpu.make_async_copy(dw.at[0], down0.at[coords], local_sem.at[2]),
        pltpu.make_async_copy(own_mixed.at[1], mixed1.at[me_line], local_sem.at[3]),
        pltpu.make_async_copy(uw.at[1], up1.at[me_line], local_sem.at[4]),
        pltpu.make_async_copy(dw.at[1], own_down1, local_sem.at[5]),
        pltpu.make_async_copy(own_cot, cot1.at[me_line], local_sem.at[6]),
    ]
    for copy in locals_:
        copy.start()
    misc_all[coords] = own_misc[...]
    for copy in locals_:
        copy.wait()

    def vectors():
        small = misc_all[..., 0:SMALL_ROWS, :].reshape(n * SMALL_ROWS, 128)
        singles = spread_slots(small, n, SMALL_ROWS, per_output)
        pairs = spread_slots(small, n, SMALL_ROWS, per_pair)
        ups = spread_slots(small, n, SMALL_ROWS, per_up)
        for b in range(2):
            vec[b, 0:1, :] = singles[2 + b : 3 + b]
            vec[b, 1:2, :] = singles[6 + b : 7 + b]
            vec[b, 2:4, :] = singles[8 + 2 * b : 10 + 2 * b]
            vec[b, 4:6, :] = singles[12 + 2 * b : 14 + 2 * b]
            vec[b, 6:8, :] = jnp.zeros((2, width), jnp.float32)
            vec_pair[b, :, 0:width] = pairs[b : b + 1, :width]
            vec_pair[b, :, width : 2 * width] = jnp.zeros((1, width), jnp.float32)
            vec_pair[b, :, 2 * width : 3 * width] = pairs[b : b + 1, width:]
            vec_up[b] = ups[4 + b : 5 + b]
        for d in range(n):
            where, rest = [], d
            for extent in grid.dims[::-1]:
                where.append(rest % extent)
                rest //= extent
            rows = misc_all[tuple(where[::-1]) + (pl.ds(SMALL_ROWS, misc_rows(per_output) - SMALL_ROWS),)].astype(jnp.float32)
            table[pl.ds(d * per_output, per_output), :] = rows[:per_output]

    count = len(units)
    line_ticks = {count - 6: line_units[:1], count - 4: line_units[1:2], count - 1: line_units[2:]} if count >= 7 else {0: line_units}
    for tick in range(1, count + ndims):
        for stage in range(1, ndims + 1):
            u = tick - stage
            if not 0 <= u < count:
                continue
            for k in units[u]:
                gather.landed(k, stage - 1)
                if stage < ndims:
                    gather.start(k, stage)
            if stage == 1:
                if u + 1 < count:
                    start(units[u + 1], 0)
                for unit in line_ticks.get(u, []):
                    start(unit, 0)
            if stage == ndims and u == 0:
                vectors()
    for unit in line_units:
        for k in unit:
            gather.landed(k, 0)
            gather.sent(k, 0, 1)
    for unit in units:
        for k in unit:
            gather.sent(k, 0, ndims)


def pairs(rows):
    if rows % 32:
        return [[(0, rows, 0)]]
    return [[(r, 16, 0), (r + 16, 16, 1)] for r in range(0, rows, 32)]


def gather_weights(grid, arrays, cid):
    project_weight, output_weight, up_weight, down_weight, project_bias = arrays[:5]
    per_project, per_output, per_up = project_weight.shape[1], output_weight.shape[1], up_weight.shape[1]
    width = project_weight.shape[2]
    per_pair = project_bias.shape[1]
    places_n = arrays[10].shape[1]
    segs = arrays[11].shape[0]
    n = grid.n
    low, full = jnp.bfloat16, jnp.float32
    mixed_rows = per_project + per_output
    small_rows = misc_rows(per_output)
    fs = grid.fsdp
    count = 2 + sum(len(u) for r in (mixed_rows, per_up, per_up) for u in pairs(r)) + sum(len(halves(r, low)) for r in (mixed_rows, per_up))
    vmem, anywhere = pl.BlockSpec(memory_space=pltpu.VMEM), pl.BlockSpec(memory_space=pl.ANY)

    def shape(s, d):
        return jax.ShapeDtypeStruct(s, d)

    return pl.pallas_call(
        functools.partial(weights_kernel, grid, (width, per_project, per_output, per_up, per_pair, places_n)),
        in_specs=[vmem] * 11 + [anywhere],
        out_specs=[anywhere] * 7 + [vmem] * 4,
        out_shape=[
            shape((*grid.dims, mixed_rows, width), low), shape((*grid.dims, per_up, width), low), shape((*grid.dims, per_up, width), low),
            shape((fs, mixed_rows, width), low), shape((fs, per_up, width), low), shape((fs, segs, width), full), shape((per_up, width), low),
            shape((2, 8, width), full), shape((2, 1, 3 * width), full), shape((2, 1, n * per_up), full), shape((width, 128), full),
        ],
        scratch_shapes=[
            pltpu.VMEM((2, mixed_rows, width), low),
            pltpu.VMEM((small_rows, 128), low), pltpu.VMEM((small_rows, 128), full), pltpu.VMEM((*grid.dims, small_rows, 128), low),
            pltpu.VMEM((segs, width), full), pltpu.VMEM((segs, 8, width), full),
        ]
        + grid.sems(count)
        + [pltpu.SemaphoreType.DMA((7,))],
        compiler_params=pltpu.CompilerParams(collective_id=cid, has_side_effects=True, vmem_limit_bytes=56 * 2**20),
        name="gather_weights",
    )(*arrays)


def forward_rows(x_low, x, w, r, rows, span, allowed, hook=lambda name: None):
    width = x.shape[1]
    step = width
    hook("project")
    for c in range(0, 3 * width, step):
        cut = pl.ds(c, step)
        r["qkv"][:, cut] = (dot_nt(x_low, w["project"][cut, :]) + w["project_b"][:, cut]).astype(jnp.bfloat16)
    attend_rows(r["qkv"], r["mixed"], rows, span, width, allowed)
    first = x + (dot_nt(r["mixed"][...], w["output"][...]) + w["output_b"])
    if "first" in r:
        r["first"](first)
    hook("first")
    unit_one, scale_one, unit_two, scale_two = feed_forward(first, w, r, hook)
    return unit_one, scale_one, unit_two, scale_two


def feed_forward(first, w, r, hook=lambda name: None):
    unit_one, scale_one = normalise(first)
    normed = unit_one * w["gains"][0:1, :] + w["shifts"][0:1, :]
    normed_low = normed.astype(jnp.bfloat16)
    r["normed"][...] = normed_low
    hidden_units = w["up"].shape[0]
    step = normed.shape[1]
    for c in range(0, hidden_units, step):
        cut = pl.ds(c, step)
        inner = dot_nt(normed_low, w["up"][cut, :]) + w["up_b"][:, cut]
        value, slope = gelu_pair(inner)
        r["hidden"][:, cut] = value.astype(jnp.bfloat16)
        r["slope"][:, cut] = slope.astype(r["slope"].dtype)
    hook("down")
    second = normed + (dot_nn(r["hidden"][...], w["down"][...]) + w["down_b"])
    unit_two, scale_two = normalise(second)
    return unit_one, scale_one, unit_two, scale_two


def mlp_back(grad, unit_one, scale_one, unit_two, scale_two, w, r, hook=lambda name: None):
    d_second = norm_back(grad, unit_two, scale_two, w["gains"][1:2, :])
    d_down = d_second.astype(jnp.bfloat16)
    r["d_down"][...] = d_down
    hidden_units = w["up"].shape[0]
    step = grad.shape[1]
    for c in range(0, hidden_units, step):
        cut = pl.ds(c, step)
        d_hidden = dot_nt(d_down, w["down"][cut, :])
        r["d_inner"][:, cut] = (d_hidden * r["slope"][:, cut].astype(jnp.float32)).astype(jnp.bfloat16)
    hook("up")
    d_normed = d_second + dot_nn(r["d_inner"][...], w["up"][...])
    d_first = norm_back(d_normed, unit_one, scale_one, w["gains"][0:1, :])
    sums = (
        row_sums(d_normed * unit_one), row_sums(grad * unit_two), row_sums(d_normed), row_sums(grad),
        row_sums(d_down), row_sums(r["d_inner"][...]),
    )
    return d_first, sums


def small_of(vec, vec_pair, vec_up, b):
    return {
        "project_b": vec_pair.at[b], "output_b": vec[b, 0:1, :], "up_b": vec_up.at[b], "down_b": vec[b, 1:2, :],
        "gains": vec[b, 2:4, :], "shifts": vec[b, 4:6, :],
    }


def unpack_mixed(grid, mixed, project, output, per_project):
    rows, width = mixed.shape[-2:]
    per_output = rows - per_project
    for d in range(grid.n):
        where, rest = [], d
        for size in grid.dims[::-1]:
            where.append(rest % size)
            rest //= size
        part = mixed[tuple(where[::-1])]
        project[pl.ds(d * per_project, per_project), :] = part[:per_project]
        output[pl.ds(d * per_output, per_output), :] = part[per_project:]


def spread(events, points):
    return [events[len(events) * p // points : len(events) * (p + 1) // points] for p in range(points)]


def segment_forward_kernel(grid, tile, steps, per_project, *refs):
    (tokens, grads, mixed0, up0, down0, vec, vec_pair, vec_up, line_mixed, line_up, line_cot, own_down) = refs[:12]
    names = ("qkv", "mixed", "d_first", "seg_low", "norm_sums", "up_sums")
    r = dict(zip(names, refs[12:18]))
    project_out, output_out, all_first, mixed1, up1, down1, all_cot, partial_up, partial_down = refs[18:27]
    r.update(zip(("slope", "normed", "hidden", "d_down", "d_inner"), refs[27:32]))
    held_mixed, project, output, up, down, own_first, sum_up, sum_down = refs[32:40]
    send_sem, recv_sem, local_sem = refs[40:]
    w = small_of(vec, vec_pair, vec_up, 0)
    w.update(project=project, output=output, up=up, down=down)
    width = tokens.shape[1]
    step = pl.program_id(0)
    last = steps - 1
    ndims = len(grid.dims)
    coords = grid.coords()
    loads = [pltpu.make_async_copy(*p, local_sem.at[i]) for i, p in enumerate(
        ((mixed0, held_mixed), (up0, up), (down0, down)))]
    stores = [pltpu.make_async_copy(*p, local_sem.at[3 + i]) for i, p in enumerate(
        ((project, project_out), (output, output_out)))]
    here = (coords[:-1]) + (slice(None),)
    lines = [pltpu.make_async_copy(a, b.at[here], local_sem.at[5 + i]) for i, (a, b) in enumerate(
        ((line_mixed, mixed1), (line_up, up1), (line_cot, all_cot)))]
    lines.append(pltpu.make_async_copy(own_down, down1.at[coords], local_sem.at[8]))
    keep_first = pltpu.make_async_copy(own_first, all_first.at[coords], local_sem.at[9])

    chunks, groups = [], []
    for own, line, dest, rows in (
        (None, line_mixed, mixed1, line_mixed.shape[1]), (None, line_up, up1, line_up.shape[1]), (own_down, None, down1, own_down.shape[0])
    ):
        cuts = halves(rows, jnp.bfloat16)
        groups.append(list(range(len(chunks), len(chunks) + len(cuts))))
        chunks += [(own, line, dest, *cut) for cut in cuts]
    groups[0].append(len(chunks))
    chunks.append((None, line_cot, all_cot, 0, line_cot.shape[1], 1))
    first_chunk = len(chunks)
    chunks.append((own_first, None, all_first, 0, own_first.shape[0], 0))
    gather = Gather(grid, coords, chunks, send_sem, recv_sem)

    ticks = ndims + 1

    def go(tick):
        if tick == 1:
            for copy in lines:
                copy.wait()
        for group in groups:
            late = chunks[group[0]][1] is None
            stage = tick if late else tick + 1
            for k in group:
                if stage > (0 if late else 1) and stage <= ndims:
                    gather.landed(k, stage - 1)
                if stage < ndims:
                    gather.start(k, stage)

    plan = {}
    for tick in range(1, ticks - 1):
        at = round((2 * steps - 1) * tick / (ticks - 2))
        if ndims == 4 and steps == 4:
            at = (1, 5, 7)[tick - 1]
        plan.setdefault(at, []).append(tick)

    def at_point(which):
        for at, some in plan.items():
            if at % 2 == which:

                @pl.when(step == at // 2)
                def _(some=some):
                    for tick in some:
                        go(tick)

    first_points = ["first", "back", "tail", "end"]
    first_events = [[] for unused in first_points]
    stages = list(range(ndims))
    for i, stage in enumerate(stages):
        first_events[min(i, len(first_points) - 1)].append(stage)

    def first_point(name):
        @pl.when(step == last)
        def _():
            for stage in first_events[first_points.index(name)]:
                if stage == 0:
                    keep_first.start()
                else:
                    gather.landed(first_chunk, stage - 1)
                    if stage == 1:
                        keep_first.wait()
                gather.start(first_chunk, stage)

    @pl.when(step == 0)
    def _():
        for copy in loads:
            copy.start()
        grid.greet(coords)
        go(0)
        for copy in lines:
            copy.start()
        loads[0].wait()
        unpack_mixed(grid, held_mixed, project, output, per_project)
        for copy in stores:
            copy.start()

    def hook(name):
        if name == "first":
            first_point("first")

            @pl.when(step == 0)
            def _():
                for copy in loads[1:]:
                    copy.wait()

            at_point(0)

    def take_first(first):
        for s in range(tile // SEG_LEN):
            own_first[pl.ds(step * (tile // SEG_LEN) + s, 1), :] = first[s * SEG_LEN : s * SEG_LEN + 1]

    r["first"] = take_first
    x_low = tokens[...]
    x = x_low.astype(jnp.float32)
    unit_one, scale_one, unit_two, scale_two = forward_rows(x_low, x, w, r, tile, SEG_LEN, None, hook)
    seg_out = unit_two * w["gains"][1:2, :] + w["shifts"][1:2, :]
    r["seg_low"][...] = seg_out.astype(jnp.bfloat16)
    first_point("back")
    place = lax.broadcasted_iota(jnp.int32, (tile, 1), 0) % SEG_LEN
    grad = jnp.where(place == 0, 0.0, grads[...])
    d_first, sums = mlp_back(grad, unit_one, scale_one, unit_two, scale_two, w, r, hook)
    r["d_first"][...] = d_first
    gathered = jnp.concatenate(list(sums[:5]) + [jnp.zeros((3, width), jnp.float32)], 0)

    @pl.when(step == 0)
    def _():
        r["norm_sums"][...] = jnp.zeros_like(r["norm_sums"])
        r["up_sums"][...] = jnp.zeros_like(r["up_sums"])
        sum_up[...] = jnp.zeros_like(sum_up)
        sum_down[...] = jnp.zeros_like(sum_down)

    r["norm_sums"][...] += gathered
    r["up_sums"][...] += jnp.broadcast_to(sums[5], r["up_sums"].shape)
    first_point("tail")
    for left, right, total in (("hidden", "d_down", sum_down), ("d_inner", "normed", sum_up)):
        for c in range(0, total.shape[0], width):
            total[pl.ds(c, width), :] += dot_tn(r[left][:, pl.ds(c, width)], r[right][...])
    first_point("end")
    at_point(1)

    @pl.when(step == last)
    def _():
        down[...] = sum_down[...].astype(jnp.bfloat16)
        up[...] = sum_up[...].astype(jnp.bfloat16)
        out = [pltpu.make_async_copy(*p, local_sem.at[i]) for i, p in enumerate(((down, partial_down), (up, partial_up)))]
        for copy in out:
            copy.start()
        go(ticks - 1)
        for g in range(len(groups)):
            for k in groups[g]:
                gather.sent(k, 1 if chunks[k][1] is not None else 0, ndims)
        gather.landed(first_chunk, ndims - 1)
        gather.sent(first_chunk, 0, ndims)
        for copy in stores + out:
            copy.wait()


def segment_forward(grid, tokens, grads, mixed0, up0, down0, smalls, lines, per_project, cid):
    rows, width = tokens.shape
    per_up = up0.shape[-2]
    mixed_rows = mixed0.shape[-2]
    hidden_units = per_up * grid.n
    tile = 2 * SEG_LEN
    steps = rows // tile
    segs = rows // SEG_LEN
    low, full = jnp.bfloat16, jnp.float32
    up0, down0 = up0.reshape(hidden_units, width), down0.reshape(hidden_units, width)
    count = 2 + sum(len(halves(r, low)) for r in (mixed_rows, per_up, per_up))
    vmem, anywhere = pl.BlockSpec(memory_space=pltpu.VMEM), pl.BlockSpec(memory_space=pl.ANY)

    def cut(columns):
        return pl.BlockSpec((tile, columns), lambda i: (i, 0))

    def shape(columns, dtype):
        return jax.ShapeDtypeStruct((rows, columns), dtype)

    return pl.pallas_call(
        functools.partial(segment_forward_kernel, grid, tile, steps, per_project),
        grid=(steps,),
        in_specs=[cut(width), cut(width)] + [anywhere] * 3 + [whole(s.shape) for s in (*smalls, *lines)],
        out_specs=[
            cut(3 * width), cut(width), cut(width), cut(width),
            pl.BlockSpec((8, width), lambda i: (0, 0)), pl.BlockSpec((8, hidden_units), lambda i: (0, 0)),
        ]
        + [anywhere] * 9,
        out_shape=[
            shape(3 * width, low), shape(width, low), shape(width, full), shape(width, low),
            jax.ShapeDtypeStruct((8, width), full), jax.ShapeDtypeStruct((8, hidden_units), full),
            jax.ShapeDtypeStruct((3 * width, width), low), jax.ShapeDtypeStruct((width, width), low),
            jax.ShapeDtypeStruct((*grid.dims, segs, width), full),
            jax.ShapeDtypeStruct((*grid.dims, mixed_rows, width), low),
            jax.ShapeDtypeStruct((*grid.dims, per_up, width), low), jax.ShapeDtypeStruct((*grid.dims, per_up, width), low),
            jax.ShapeDtypeStruct((*grid.dims, segs, width), full),
            jax.ShapeDtypeStruct((hidden_units, width), low), jax.ShapeDtypeStruct((hidden_units, width), low),
        ],
        scratch_shapes=[
            pltpu.VMEM((tile, hidden_units), low), pltpu.VMEM((tile, width), low), pltpu.VMEM((tile, hidden_units), low),
            pltpu.VMEM((tile, width), low), pltpu.VMEM((tile, hidden_units), low), pltpu.VMEM((*grid.dims, mixed_rows, width), low),
            pltpu.VMEM((3 * width, width), low), pltpu.VMEM((width, width), low),
            pltpu.VMEM((hidden_units, width), low), pltpu.VMEM((hidden_units, width), low), pltpu.VMEM((segs, width), full),
            pltpu.VMEM((hidden_units, width), full), pltpu.VMEM((hidden_units, width), full),
        ]
        + grid.sems(count)
        + [pltpu.SemaphoreType.DMA((10,))],
        compiler_params=pltpu.CompilerParams(collective_id=cid, has_side_effects=True, vmem_limit_bytes=60 * 2**20),
        name="segment_forward",
    )(tokens, grads, mixed0, up0, down0, *smalls, *lines)


def own_columns(value, first, size):
    return dot_nn(value, select(value.shape[1], size, first)).astype(jnp.bfloat16)


def own_sums(value, first, size):
    row = lax.broadcasted_iota(jnp.int32, (value.shape[1], size), 0)
    column = lax.broadcasted_iota(jnp.int32, (value.shape[1], size), 1)
    ones = jnp.where(row == first + column, 1.0, 0.0)
    return jnp.dot(value, ones, precision=highest, preferred_element_type=jnp.float32)


def document_of(placed, long_total):
    long_docs = long_total // LONG_SEGS
    is_long = placed < long_total
    rest = placed - long_total
    doc = jnp.where(is_long, placed // LONG_SEGS, long_docs + rest // SHORT_SEGS)
    return doc, jnp.where(is_long, placed % LONG_SEGS, rest % SHORT_SEGS)


def cross_kernel(grid, sizes, *refs):
    per_project, per_output, per_up, per_pair = sizes
    (firsts, grads, placed_row, placed_col, mixed1, up1, down1, up0, down0, vec, vec_pair, vec_up, table, partial) = refs[:14]
    g_project, g_output, g_up, g_down, z_up, down_sum, smalls, g_table, cross_own, d_first_own = refs[14:24]
    names = ("qkv", "slope", "d_mixed", "mixed", "normed", "hidden", "d_down", "d_inner", "d_qkv")
    r = dict(zip(names, refs[24:33]))
    held_mixed, project, output, up, down, z_up_w, z_down_w, z_slope, z_normed, z_hidden, z_d_down, z_d_inner, rows_f = refs[33:46]
    held, *lands, send_sem, recv_sem, local_sem = refs[46:]
    coords = grid.coords()
    reduce, ticks = summing(grid, coords, held, lands, down_sum, send_sem, recv_sem)
    load_partial = pltpu.make_async_copy(partial, held, local_sem.at[5])
    load_partial.start()
    loads = [pltpu.make_async_copy(*p, local_sem.at[i]) for i, p in enumerate(
        ((up0, z_up_w), (down0, z_down_w), (mixed1, held_mixed), (up1, up), (down1, down)))]
    for copy in loads:
        copy.start()
    expected = grid.call(coords)
    slots, width = firsts.shape
    places_n = LONG_SEGS
    me = grid.flat()
    per_slots = slots // grid.n

    w0 = small_of(vec, vec_pair, vec_up, 0)
    w0.update(up=z_up_w, down=z_down_w)
    r0 = {"normed": z_normed, "hidden": z_hidden, "slope": z_slope, "d_down": z_d_down, "d_inner": z_d_inner}

    def hook0(name):
        if name == "down":
            loads[1].wait()
            load_partial.wait()
            grid.meet(expected)
            reduce(0)

    loads[0].wait()
    kept0 = feed_forward(firsts[...], w0, r0, hook0)
    seg_first = kept0[2] * w0["gains"][1:2, :] + w0["shifts"][1:2, :]
    doc_row, unused = document_of(placed_row[...], slots // 2)
    doc_col, place_col = document_of(placed_col[...], slots // 2)
    picker = place_col == lax.broadcasted_iota(jnp.int32, (slots, places_n), 1)
    picker_f = jnp.where(picker, 1.0, 0.0)
    x = seg_first + dot_nt(picker_f.astype(jnp.bfloat16), table[:, 0:places_n].astype(jnp.bfloat16))

    w = small_of(vec, vec_pair, vec_up, 1)
    w.update(project=project, output=output, up=up, down=down)
    loads[2].wait()
    unpack_mixed(grid, held_mixed, project, output, per_project)
    x_low = x.astype(jnp.bfloat16)
    allowed = doc_col == doc_row
    allowed = jnp.concatenate([allowed, allowed], 0)
    reduce(1)

    def hook(name):
        if name == "first":
            loads[3].wait()
        if name == "down":
            loads[4].wait()

    kept = forward_rows(x_low, x, w, r, slots, slots, allowed, hook)
    mine = pl.ds(pl.multiple_of(me * per_slots, per_slots), per_slots)
    rows_f[...] = kept[2] * w["gains"][1:2, :] + w["shifts"][1:2, :]
    cross_own[...] = rows_f[mine, :]
    d_first, sums = mlp_back(grads[...], *kept, w, r)
    reduce(2)
    branch = d_first.astype(jnp.bfloat16)
    r["d_mixed"][...] = dot_nn(branch, output[...]).astype(jnp.bfloat16)
    attend_back(r["qkv"], r["d_mixed"], r["d_qkv"], slots, slots, width, allowed)
    d_x = d_first + dot_nn(r["d_qkv"][...], project[...])
    reduce(3)

    g_project[...] = dot_tn(own_columns(r["d_qkv"][...], me * per_project, per_project), x_low)
    g_output[...] = dot_tn(own_columns(branch, me * per_output, per_output), r["mixed"][...])
    g_up[...] = dot_tn(own_columns(r["d_inner"][...], me * per_up, per_up), r["normed"][...])
    g_down[...] = dot_tn(own_columns(r["hidden"][...], me * per_up, per_up), r["d_down"][...])
    smalls[...] = jnp.zeros_like(smalls)
    norm_rows = jnp.concatenate(list(sums[:5]) + [row_sums(branch), jnp.zeros((2, width), jnp.float32)], 0)
    smalls[0:8, 0:per_output] = own_sums(norm_rows, me * per_output, per_output)
    up_rows = jnp.broadcast_to(sums[5], (8, sums[5].shape[1]))
    smalls[6:7, 0:per_up] = own_sums(up_rows, me * per_up, per_up)[0:1]
    qkv_sums = row_sums(r["d_qkv"][...])
    pair = jnp.concatenate([qkv_sums[:, :width], qkv_sums[:, 2 * width :]], 1)
    smalls[7:8, 0:per_pair] = own_sums(jnp.broadcast_to(pair, (8, 2 * width)), me * per_pair, per_pair)[0:1]
    g_table[...] = lax.dot_general(
        own_sums(d_x, me * per_output, per_output), picker_f, (((0,), (0,)), ((), ())),
        precision=highest, preferred_element_type=jnp.float32,
    )

    d_first0, sums = mlp_back(d_x, *kept0, w0, r0)
    rows_f[...] = d_first0
    d_first_own[...] = rows_f[mine, :]
    z_up[...] = dot_tn(own_columns(z_d_inner[...], me * per_up, per_up), z_normed[...])
    z_down = dot_tn(own_columns(z_hidden[...], me * per_up, per_up), z_d_down[...])
    norm_rows = jnp.concatenate(list(sums[:5]) + [jnp.zeros((3, width), jnp.float32)], 0)
    smalls[8:16, 0:per_output] = own_sums(norm_rows, me * per_output, per_output)
    up_rows = jnp.broadcast_to(sums[5], (8, sums[5].shape[1]))
    smalls[14:15, 0:per_up] = own_sums(up_rows, me * per_up, per_up)[0:1]
    for tick in range(4, ticks):
        reduce(tick)
    down_sum[...] += z_down
    reduce(None)


def summing(grid, coords, held, lands, out, send_sem, recv_sem):
    ndims = len(grid.dims)
    units = [halves(held.shape[-2], held.dtype)]
    cuts = [cut for unit in units for cut in unit]
    chunks = [(held, lands[k * ndims : (k + 1) * ndims], out, *cut) for k, cut in enumerate(cuts)]
    scatter = Scatter(grid, coords, chunks, send_sem, recv_sem)
    per = len(units[0])

    def reduce(tick):
        if tick is None:
            for k in range(len(chunks)):
                scatter.sent(k)
            return
        for stage in range(ndims + 1):
            u = tick - stage
            if not 0 <= u < len(units):
                continue
            for k in range(u * per, (u + 1) * per):
                if stage > 0:
                    scatter.add(k, stage - 1)
                if stage < ndims:
                    scatter.start(k, stage)

    return reduce, len(units) + ndims


def summing_scratch(grid, rows, width):
    low = jnp.bfloat16
    cuts = halves(rows, low)
    lands = [land for cut in cuts for land in Scatter.landing(grid, cut[1], width, low, cut[2])]
    return [pltpu.VMEM((*grid.dims, rows, width), low)] + lands + grid.sems(len(cuts))


def cross_block(grid, firsts, grads, placement, mixed1, up1, down1, up0, down0, smalls, table, sizes, partial, cid):
    slots, width = firsts.shape
    per_project, per_output, per_up, per_pair = sizes
    hidden_units = per_up * grid.n
    low, full = jnp.bfloat16, jnp.float32
    per_slots = slots // grid.n
    flat = lambda ref: ref.reshape(hidden_units, width)
    vmem, anywhere = pl.BlockSpec(memory_space=pltpu.VMEM), pl.BlockSpec(memory_space=pl.ANY)
    outs = [
        (per_project, width), (per_output, width), (per_up, width), (per_up, width), (per_up, width), (per_up, width),
        (16, 128), (per_output, LONG_SEGS), (per_slots, width), (per_slots, width),
    ]

    def held(*shape, dtype=low):
        return pltpu.VMEM(shape, dtype)

    return pl.pallas_call(
        functools.partial(cross_kernel, grid, sizes),
        in_specs=[vmem] * 4 + [anywhere] * 5 + [vmem] * 4 + [anywhere],
        out_specs=[vmem] * len(outs),
        out_shape=[jax.ShapeDtypeStruct(s, full) for s in outs],
        scratch_shapes=[
            held(slots, 3 * width), held(slots, hidden_units), held(slots, width), held(slots, width), held(slots, width),
            held(slots, hidden_units), held(slots, width), held(slots, hidden_units), held(slots, 3 * width),
            held(*mixed1.shape), held(3 * width, width), held(width, width), held(hidden_units, width), held(hidden_units, width),
            held(hidden_units, width), held(hidden_units, width), held(slots, hidden_units), held(slots, width),
            held(slots, hidden_units), held(slots, width), held(slots, hidden_units), held(slots, width, dtype=full),
            *summing_scratch(grid, per_up, width),
            pltpu.SemaphoreType.DMA((6,)),
        ],
        compiler_params=pltpu.CompilerParams(collective_id=cid, has_side_effects=True, vmem_limit_bytes=63 * 2**20),
        name="cross_block",
    )(firsts, grads, placement[None, :], placement[:, None], mixed1, flat(up1), flat(down1), flat(up0), flat(down0), *smalls, table, partial)


def segment_backward_kernel(grid, tile, steps, per_project, *refs):
    qkv, d_first, cls_grad, seg_low, cls_out, mixed, tokens, project, output, partial, cls_part = refs[:11]
    d_x, layer_out, sums_qkv, sums_out, up_sum, partial_mixed = refs[11:17]
    d_mixed, d_qkv, d_branch, sum_project, sum_output, packed, held = refs[17:24]
    *lands, send_sem, recv_sem, local_sem = refs[24:]
    width = d_first.shape[1]
    per_output = packed.shape[-2] - per_project
    step = pl.program_id(0)
    coords = grid.coords()
    reduce, ticks = summing(grid, coords, held, lands, up_sum, send_sem, recv_sem)
    plan = {}
    for tick in range(1, ticks - 1):
        at = (2, 5, 6)[tick - 1] if ticks == 5 and steps == 4 else min(2 * steps - 1, tick + 1)
        plan.setdefault(at, []).append(tick)

    def at_point(which):
        for at, some in plan.items():
            if at % 2 == which:

                @pl.when(step == at // 2)
                def _(some=some):
                    for tick in some:
                        reduce(tick)

    @pl.when(step == 0)
    def _():
        load = pltpu.make_async_copy(partial, held, local_sem.at[0])
        load.start()
        for total in (sums_qkv, sums_out, sum_project, sum_output):
            total[...] = jnp.zeros_like(total)
        grid.greet(coords)
        load.wait()
        reduce(0)

    at_point(0)
    place = lax.broadcasted_iota(jnp.int32, (tile, 1), 0)
    grad, out = d_first[...], seg_low[...].astype(jnp.float32)
    for s in range(tile // SEG_LEN):
        here = pl.ds(step * (tile // SEG_LEN) + s, 1)
        grad = jnp.where(place == s * SEG_LEN, cls_grad[here, :], grad)
        out = jnp.where(place == s * SEG_LEN, cls_out[here, :], out)
    layer_out[...] = out.astype(jnp.bfloat16)
    branch = grad.astype(jnp.bfloat16)
    d_branch[...] = branch
    d_mixed[...] = dot_nn(branch, output[...]).astype(jnp.bfloat16)
    attend_back(qkv, d_mixed, d_qkv, tile, SEG_LEN, width, None)
    at_point(1)
    d_x[...] = grad + dot_nn(d_qkv[...], project[...])
    sums_qkv[...] += jnp.broadcast_to(row_sums(d_qkv[...]), sums_qkv.shape)
    sums_out[...] += jnp.broadcast_to(row_sums(branch), sums_out.shape)
    sum_output[...] += dot_tn(d_branch[...], mixed[...])
    for c in range(0, 3 * width, width):
        sum_project[pl.ds(c, width), :] += dot_tn(d_qkv[:, pl.ds(c, width)], tokens[...])

    @pl.when(step == steps - 1)
    def _():
        for d in range(grid.n):
            where, rest = [], d
            for size in grid.dims[::-1]:
                where.append(rest % size)
                rest //= size
            rows = [sum_project[pl.ds(d * per_project, per_project), :], sum_output[pl.ds(d * per_output, per_output), :]]
            packed[tuple(where[::-1])] = jnp.concatenate(rows, 0).astype(jnp.bfloat16)
        store = pltpu.make_async_copy(packed, partial_mixed, local_sem.at[0])
        store.start()
        reduce(ticks - 1)
        up_sum[...] += cls_part[...]
        reduce(None)
        store.wait()


def segment_backward(grid, qkv, d_first, cls_grad, seg_low, cls_out, mixed, tokens, project, output, partial, cls_part, per_project, cid):
    rows, width = d_first.shape
    tile = 2 * SEG_LEN
    low, full = jnp.bfloat16, jnp.float32
    per_up = partial.shape[-2]
    mixed_rows = 4 * width // grid.n
    anywhere = pl.BlockSpec(memory_space=pl.ANY)

    def cut(columns):
        return pl.BlockSpec((tile, columns), lambda i: (i, 0))

    return pl.pallas_call(
        functools.partial(segment_backward_kernel, grid, tile, rows // tile, per_project),
        grid=(rows // tile,),
        in_specs=[
            cut(3 * width), cut(width), whole(cls_grad.shape), cut(width), whole(cls_out.shape), cut(width), cut(width),
            whole(project.shape), whole(output.shape), anywhere, whole(cls_part.shape),
        ],
        out_specs=[
            cut(width), cut(width), pl.BlockSpec((8, 3 * width), lambda i: (0, 0)), pl.BlockSpec((8, width), lambda i: (0, 0)),
            pl.BlockSpec((per_up, width), lambda i: (0, 0)), anywhere,
        ],
        out_shape=[
            jax.ShapeDtypeStruct((rows, width), full), jax.ShapeDtypeStruct((rows, width), low),
            jax.ShapeDtypeStruct((8, 3 * width), full), jax.ShapeDtypeStruct((8, width), full),
            jax.ShapeDtypeStruct((per_up, width), full), jax.ShapeDtypeStruct((*grid.dims, mixed_rows, width), low),
        ],
        scratch_shapes=[
            pltpu.VMEM((tile, width), low), pltpu.VMEM((tile, 3 * width), low), pltpu.VMEM((tile, width), low),
            pltpu.VMEM((3 * width, width), full), pltpu.VMEM((width, width), full), pltpu.VMEM((*grid.dims, mixed_rows, width), low),
            *summing_scratch(grid, per_up, width), pltpu.SemaphoreType.DMA((1,)),
        ],
        compiler_params=pltpu.CompilerParams(collective_id=cid, has_side_effects=True, vmem_limit_bytes=60 * 2**20),
        name="segment_backward",
    )(qkv, d_first, cls_grad, seg_low, cls_out, mixed, tokens, project, output, partial, cls_part)


def sum_kernel(grid, chunk_list, nparts, *refs):
    given, outs = refs[:nparts], refs[nparts : 2 * nparts]
    held = refs[2 * nparts : 3 * nparts]
    lands = refs[3 * nparts : -3]
    send_sem, recv_sem, load_sem = refs[-3:]
    ndims = len(grid.dims)
    coords = grid.coords()
    loads = [pltpu.make_async_copy(given[a], held[a], load_sem.at[a]) for a in range(nparts)]
    for load in loads:
        load.start()
    grid.greet(coords)
    chunks = [
        (held[a], lands[k * ndims : (k + 1) * ndims], outs[a], first, count, colour)
        for k, (a, first, count, colour, unit) in enumerate(chunk_list)
    ]
    scatter = Scatter(grid, coords, chunks, send_sem, recv_sem)
    loaded = set()
    units = sorted({c[4] for c in chunk_list})
    for tick in range(len(units) + ndims):
        for stage in range(ndims + 1):
            u = tick - stage
            if not 0 <= u < len(units):
                continue
            for k, (a, first, count, colour, unit) in enumerate(chunk_list):
                if unit != units[u]:
                    continue
                if a not in loaded:
                    loaded.add(a)
                    loads[a].wait()
                if stage >= 1:
                    scatter.add(k, stage - 1)
                if stage < ndims:
                    scatter.start(k, stage)
    for k in range(len(chunks)):
        scatter.sent(k)


def sum_to_owners(grid, parts, cid):
    chunk_list = []
    for a, p in enumerate(parts):
        for unit, cuts in enumerate(pairs(p.shape[1]) if p.dtype == jnp.bfloat16 else [halves(p.shape[1], p.dtype)]):
            chunk_list += [(a, *cut, unit) for cut in cuts]
    nparts = len(parts)
    shaped = [p.reshape(tuple(grid.dims) + p.shape[1:]) for p in parts]
    lands = []
    for a, first, count, colour, unit in chunk_list:
        lands += Scatter.landing(grid, count, parts[a].shape[2], parts[a].dtype, colour)
    return pl.pallas_call(
        functools.partial(sum_kernel, grid, chunk_list, nparts),
        out_shape=[jax.ShapeDtypeStruct(p.shape[1:], jnp.float32) for p in parts],
        in_specs=[pl.BlockSpec(memory_space=pl.ANY)] * nparts,
        out_specs=[pl.BlockSpec(memory_space=pltpu.VMEM)] * nparts,
        scratch_shapes=[pltpu.VMEM(s.shape, s.dtype) for s in shaped] + lands + grid.sems(len(chunk_list)) + [pltpu.SemaphoreType.DMA((nparts,))],
        compiler_params=pltpu.CompilerParams(collective_id=cid, has_side_effects=True, vmem_limit_bytes=56 * 2**20),
        name="sum_to_owners",
    )(*shaped)


class Held:
    def __init__(self, value):
        self.value = value

    @property
    def shape(self):
        return self.value.shape

    @property
    def dtype(self):
        return self.value.dtype

    @staticmethod
    def plain(where):
        where = where if isinstance(where, tuple) else (where,)
        return tuple(slice(w.start, w.start + w.size) if isinstance(w, pl.Slice) else w for w in where)

    def __getitem__(self, where):
        return self.value[self.plain(where)]

    def __setitem__(self, where, value):
        self.value = self.value.at[self.plain(where)].set(value)


def cross_plain(grid, firsts, grads, placement, mixed1, up1, down1, up0, down0, smalls, table, sizes, partial, cid):
    slots, width = firsts.shape
    per_project, per_output, per_up, per_pair = sizes
    hidden_units = per_up * grid.n
    me = grid.flat()
    vec, vec_pair, vec_up = smalls

    def weights(b, up, down):
        return {
            "project_b": vec_pair[b], "output_b": vec[b, 0:1, :], "up_b": vec_up[b], "down_b": vec[b, 1:2, :],
            "gains": vec[b, 2:4, :], "shifts": vec[b, 4:6, :],
            "up": up.reshape(hidden_units, width), "down": down.reshape(hidden_units, width),
        }

    def blank(columns):
        return Held(jnp.zeros((slots, columns), jnp.bfloat16))

    def store():
        made = {k: blank(width) for k in ("mixed", "normed", "d_down", "d_mixed")}
        made.update({k: blank(hidden_units) for k in ("hidden", "slope", "d_inner")})
        made.update(qkv=blank(3 * width), d_qkv=blank(3 * width))
        return made

    def cut(matrix, size, axis=1):
        return lax.dynamic_slice_in_dim(matrix, me * size, size, axis)

    w0, w, r0, r = weights(0, up0, down0), weights(1, up1, down1), store(), store()
    parts = mixed1.reshape(grid.n, -1, width)
    w["project"] = parts[:, :per_project].reshape(3 * width, width)
    w["output"] = parts[:, per_project:].reshape(width, width)
    kept0 = feed_forward(firsts, w0, r0)
    seg_first = kept0[2] * w0["gains"][1:2, :] + w0["shifts"][1:2, :]
    doc, place = document_of(placement, slots // 2)
    picker = jnp.where(place[:, None] == jnp.arange(LONG_SEGS, dtype=jnp.int32)[None, :], 1.0, 0.0)
    x = seg_first + dot_nt(picker.astype(jnp.bfloat16), table[:, :LONG_SEGS].astype(jnp.bfloat16))
    x_low = x.astype(jnp.bfloat16)
    allowed = doc[:, None] == doc[None, :]
    allowed = jnp.concatenate([allowed, allowed], 0)
    kept = forward_rows(x_low, x, w, r, slots, slots, allowed)
    out = kept[2] * w["gains"][1:2, :] + w["shifts"][1:2, :]
    d_first, sums = mlp_back(grads, *kept, w, r)
    branch = d_first.astype(jnp.bfloat16)
    r["d_mixed"][...] = dot_nn(branch, w["output"]).astype(jnp.bfloat16)
    attend_back(r["qkv"], r["d_mixed"], r["d_qkv"], slots, slots, width, allowed)
    d_x = d_first + dot_nn(r["d_qkv"][...], w["project"])
    d_first0, sums0 = mlp_back(d_x, *kept0, w0, r0)
    qkv_sums = row_sums(r["d_qkv"][...])
    pair = jnp.concatenate([qkv_sums[:, :width], qkv_sums[:, 2 * width :]], 1)

    def laid(rows, size):
        return jnp.pad(cut(rows, size), ((0, 0), (0, 128 - size)))

    none = jnp.zeros((1, 128), jnp.float32)
    own_small = jnp.concatenate(
        [
            laid(jnp.concatenate(list(sums[:5]) + [row_sums(branch)], 0), per_output), laid(sums[5], per_up), laid(pair, per_pair),
            laid(jnp.concatenate(list(sums0[:5]), 0), per_output), none, laid(sums0[5], per_up), none,
        ],
        0,
    )
    g_table = lax.dot_general(cut(d_x, per_output), picker, (((0,), (0,)), ((), ())), precision=highest)
    per_slots = slots // grid.n
    return (
        dot_tn(cut(r["d_qkv"][...], per_project), x_low), dot_tn(cut(branch, per_output), r["mixed"][...]),
        dot_tn(cut(r["d_inner"][...], per_up), r["normed"][...]), dot_tn(cut(r["hidden"][...], per_up), r["d_down"][...]),
        dot_tn(cut(r0["d_inner"][...], per_up), r0["normed"][...]), dot_tn(cut(r0["hidden"][...], per_up), r0["d_down"][...]) + sum_to_owners(grid, [partial.reshape(grid.n, per_up, width)], cid)[0],
        own_small, g_table, cut(out, per_slots, 0), cut(d_first0, per_slots, 0),
    )


def shards(
    grid,
    tokens,
    cotangent,
    placement,
    project_weight,
    project_bias,
    output_weight,
    output_bias,
    up_weight,
    up_bias,
    down_weight,
    down_bias,
    norm_gain,
    norm_bias,
    position_table,
):
    n = grid.n
    seg_count, seg_len, width = tokens.shape
    slots, rows = placement.shape[0], seg_count * seg_len
    per_project, per_output = project_weight.shape[2], output_weight.shape[2]
    per_pair, per_up = project_bias.shape[1], up_bias.shape[1]
    sizes = (per_project, per_output, per_up, per_pair)
    low_tokens = tokens.reshape(rows, width)

    mixed0, up0, down0, *lines, vec, vec_pair, vec_up, table = gather_weights(
        grid,
        [*(jnp.swapaxes(w, 1, 2) for w in (project_weight, output_weight, up_weight)), down_weight,
         project_bias, output_bias, up_bias, down_bias, norm_gain, norm_bias, position_table.T, cotangent],
        0,
    )
    smalls = [vec, vec_pair, vec_up]
    (qkv, mixed, d_first, seg_low, norm_sums, up_sums, project, output, all_first,
     mixed1, up1, down1, all_cot, partial_up, partial_down) = segment_forward(
        grid, low_tokens, cotangent.reshape(rows, width), mixed0, up0, down0, smalls, lines, per_project, 1
    )
    partial_up, partial_down = [p.reshape(*grid.dims, per_up, width) for p in (partial_up, partial_down)]
    g_project, g_output, g_up, g_down, z_up, down_sum, own_small, g_table, cross_own, cls_grad = (cross_block if slots <= 256 else cross_plain)(
        grid, all_first.reshape(slots, width), all_cot.reshape(slots, width), placement, mixed1, up1, down1, up0, down0,
        smalls, table, sizes, partial_down, 2,
    )
    d_x, layer_out, sums_qkv, sums_out, up_sum, partial_mixed = segment_backward(
        grid, qkv, d_first, cls_grad, seg_low, cross_own, mixed, low_tokens, project, output, partial_up, z_up, per_project, 3
    )

    def per_device(rows):
        cut = rows.reshape(rows.shape[0], n, -1).transpose(1, 0, 2)
        return jnp.pad(cut, ((0, 0), (0, 0), (0, 128 - cut.shape[2])))

    seg_small = jnp.concatenate(
        [
            per_device(jnp.concatenate([norm_sums[:5], sums_out[:1]], 0)), per_device(up_sums[:1]),
            per_device(jnp.concatenate([sums_qkv[:1, :width], sums_qkv[:1, 2 * width :]], 1)),
        ],
        1,
    )
    mixed_sum, small_sum = sum_to_owners(grid, [partial_mixed.reshape(n, -1, width), seg_small], 4)
    both = jnp.stack([small_sum + own_small[8:], own_small[:8]])
    return (
        layer_out.reshape(tokens.shape),
        d_x.reshape(tokens.shape),
        jnp.swapaxes(jnp.stack([mixed_sum[:per_project], g_project]), 1, 2),
        both[:, 7, :per_pair],
        jnp.swapaxes(jnp.stack([mixed_sum[per_project:], g_output]), 1, 2),
        both[:, 5, :per_output],
        jnp.swapaxes(jnp.stack([up_sum, g_up]), 1, 2),
        both[:, 6, :per_up],
        jnp.stack([down_sum, g_down]),
        both[:, 4, :per_output],
        both[:, 0:2, :per_output],
        both[:, 2:4, :per_output],
        g_table.T,
    )


def solution(mesh):
    grid = Grid(mesh)
    rows, cols, last = P(AXES, None, None), P(None, AXES), P(None, None, AXES)
    middle = P(None, AXES, None)
    return jax.shard_map(
        functools.partial(shards, grid),
        mesh=mesh,
        in_specs=(
            rows, rows, P(), last, cols, last, cols, last, cols, middle, cols, last, last, cols,
        ),
        out_specs=(rows, rows, last, cols, last, cols, last, cols, middle, cols, last, last, cols),
        check_vma=False,
    )
```

```python
import functools
import math

import jax
import jax.numpy as jnp
from jax import lax
from jax.experimental import pallas as pl
from jax.experimental.pallas import tpu as pltpu
from jax.sharding import PartitionSpec as P

HEADS = 12
HEAD_DIM = 64
SEG_LEN = 128
LONG_SEGS = 64
SHORT_SEGS = 16
MESH = pl.DeviceIdType.MESH
AXES = ("dp", "fsdp")

highest = lax.Precision.HIGHEST
epsilon = 1e-06
masked_score = -1e30


class Grid:
    def __init__(self, mesh):
        self.dp, self.fsdp = mesh.shape["dp"], mesh.shape["fsdp"]
        twos = int(math.log2(self.dp))
        self.dims = (2,) * twos + (self.fsdp,)
        self.n = self.dp * self.fsdp
        self.last = len(self.dims) - 1
        self.most = max(self.dims) - 1
        middle = list(range(self.last - 1))
        self.orders = (
            [self.last] + middle[::-1] + [self.last - 1],
            [self.last] + middle + [self.last - 1],
        )

    def coords(self):
        dp, fs = lax.axis_index("dp"), lax.axis_index("fsdp")
        twos = self.last
        return tuple((dp // 2 ** (twos - 1 - i)) % 2 for i in range(twos)) + (fs,)

    def flat(self):
        return lax.axis_index("dp") * self.fsdp + lax.axis_index("fsdp")

    def peer(self, coords, dim, step):
        other = list(coords)
        other[dim] = lax.rem(coords[dim] + step, self.dims[dim])
        dp = 0
        for value in other[:-1]:
            dp = dp * 2 + value
        return (dp, other[-1]), other[dim]

    def greet(self, coords):
        self.meet(self.call(coords))

    def call(self, coords):
        barrier = pltpu.get_barrier_semaphore()
        count = 0
        for dim, size in enumerate(self.dims):
            for step in range(1, size):
                where, unused = self.peer(coords, dim, step)
                pl.semaphore_signal(barrier, inc=1, device_id=where, device_id_type=MESH)
                count += 1
        return count

    def meet(self, count):
        pl.semaphore_wait(pltpu.get_barrier_semaphore(), count)

    def sems(self, chunks):
        shape = (chunks, len(self.dims), self.most)
        return [pltpu.SemaphoreType.DMA(shape), pltpu.SemaphoreType.DMA(shape)]


def index_of(coords, free, ndims):
    return tuple(slice(None) if d in free else coords[d] for d in range(ndims))


def halves(rows, dtype):
    tile = 16 if dtype == jnp.bfloat16 else 8
    if rows % (2 * tile) == 0:
        return [(0, rows // 2, 0), (rows // 2, rows // 2, 1)]
    return [(0, rows, 0)]


class Gather:
    def __init__(self, grid, coords, chunks, send_sem, recv_sem, base=0):
        self.grid, self.coords, self.chunks = grid, coords, chunks
        self.send_sem, self.recv_sem, self.base = send_sem, recv_sem, base
        self.stages = len(grid.dims)

    def copies(self, k, stage):
        own, line, dest, first, rows, colour = self.chunks[k]
        grid, coords = self.grid, self.coords
        order = grid.orders[colour]
        dim = order[stage]
        cut = (pl.ds(first, rows),)
        if stage == 0:
            source = own.at[cut]
            target_ref = dest.at[coords + cut] if line is None else line.at[(coords[-1],) + cut]
        else:
            target_ref = dest.at[index_of(coords, order[:stage], len(grid.dims)) + cut]
            source = line.at[(slice(None),) + cut] if line is not None and stage == 1 else target_ref
        made = []
        for step in range(1, grid.dims[dim]):
            target, unused = grid.peer(coords, dim, step)
            made.append(
                pltpu.make_async_remote_copy(
                    source,
                    target_ref,
                    self.send_sem.at[self.base + k, stage, step - 1],
                    self.recv_sem.at[self.base + k, stage, step - 1],
                    device_id=target,
                    device_id_type=MESH,
                )
            )
        return made

    def start(self, k, stage):
        for copy in self.copies(k, stage):
            copy.start()

    def landed(self, k, stage):
        for copy in self.copies(k, stage):
            copy.wait_recv()

    def sent(self, k, first_stage, last_stage):
        for stage in range(first_stage, last_stage):
            for copy in self.copies(k, stage):
                copy.wait_send()


class Scatter:
    def __init__(self, grid, coords, chunks, send_sem, recv_sem, base=0):
        self.grid, self.coords, self.chunks = grid, coords, chunks
        self.send_sem, self.recv_sem, self.base = send_sem, recv_sem, base
        self.stages = len(grid.dims)

    @staticmethod
    def landing(grid, rows, width, dtype, colour):
        order = grid.orders[colour][::-1]
        made = []
        for stage, dim in enumerate(order):
            left = [grid.dims[d] for d in range(len(order)) if d in order[stage + 1 :]]
            made.append(pltpu.VMEM((grid.dims[dim] - 1, *left, rows, width), dtype))
        return made

    def copies(self, k, stage):
        held, lands, out, first, rows, colour = self.chunks[k]
        grid, coords = self.grid, self.coords
        order = grid.orders[colour][::-1]
        dim = order[stage]
        made = []
        for step in range(1, grid.dims[dim]):
            target, value = grid.peer(coords, dim, step)
            there = list(coords)
            there[dim] = value
            where = index_of(there, order[stage + 1 :], len(order)) + (pl.ds(first, rows),)
            made.append(
                pltpu.make_async_remote_copy(
                    held.at[where],
                    lands[stage].at[step - 1],
                    self.send_sem.at[self.base + k, stage, step - 1],
                    self.recv_sem.at[self.base + k, stage, step - 1],
                    device_id=target,
                    device_id_type=MESH,
                )
            )
        return made

    def start(self, k, stage):
        for copy in self.copies(k, stage):
            copy.start()

    def add(self, k, stage):
        for copy in self.copies(k, stage):
            copy.wait_recv()
        held, lands, out, first, rows, colour = self.chunks[k]
        grid, coords = self.grid, self.coords
        order = grid.orders[colour][::-1]
        land = lands[stage]
        where = index_of(coords, order[stage + 1 :], len(order)) + (pl.ds(first, rows),)
        total = held[where]
        final = stage == self.stages - 1
        if final:
            total = total.astype(jnp.float32)
        for step in range(grid.dims[order[stage]] - 1):
            total += land[step].astype(total.dtype)
        if final:
            out[pl.ds(first, rows)] = total
        else:
            held[where] = total

    def sent(self, k, stages):
        for stage in range(stages):
            for copy in self.copies(k, stage):
                copy.wait_send()


def dot_nt(left, right):
    return lax.dot_general(
        left, right, (((1,), (1,)), ((), ())), preferred_element_type=jnp.float32
    )


def dot_nn(left, right):
    return lax.dot_general(
        left, right, (((1,), (0,)), ((), ())), preferred_element_type=jnp.float32
    )


def dot_tn(left, right):
    return lax.dot_general(
        left, right, (((0,), (0,)), ((), ())), preferred_element_type=jnp.float32
    )


def normalise(value):
    offset = value - jnp.mean(value, -1, keepdims=True)
    scale = lax.rsqrt(jnp.mean(offset * offset, -1, keepdims=True) + epsilon)
    return offset * scale, scale


def norm_back(grad, unit, scale, gain):
    pulled = grad * gain
    along = jnp.mean(pulled * unit, -1, keepdims=True)
    return scale * (pulled - jnp.mean(pulled, -1, keepdims=True) - unit * along)


def gelu_pair(x):
    bell = jnp.exp(-0.5 * x * x)
    t = 1.0 / (1.0 + (0.3275911 * 0.5**0.5) * jnp.abs(x))
    tail = t * (0.5 * 0.254829592 + t * (0.5 * -0.284496736 + t * (
        0.5 * 1.421413741 + t * (0.5 * -1.453152027 + t * (0.5 * 1.061405429)))))
    tail = tail * bell
    below = jnp.where(x < 0, tail, 1.0 - tail)
    return x * below, below + (x * 0.3989422804014327) * bell


def first_lanes():
    return lax.broadcasted_iota(jnp.int32, (1, 2 * HEAD_DIM), 1) < HEAD_DIM


def stack_heads(pair):
    zero = jnp.zeros_like(pair)
    left = first_lanes()
    return jnp.concatenate([jnp.where(left, pair, zero), jnp.where(left, zero, pair)], 0)


def unstack_heads(stacked):
    rows = stacked.shape[0] // 2
    return jnp.where(first_lanes(), stacked[:rows], stacked[rows:])


def pair_shares(query_stack, key_pair, allowed):
    scores = dot_nt(query_stack, key_pair)
    if allowed is not None:
        scores = jnp.where(allowed, scores, masked_score)
    raised = jnp.exp(scores - jnp.max(scores, -1, keepdims=True))
    return raised * (1.0 / jnp.sum(raised, -1, keepdims=True))


def attend_rows(qkv, mixed, rows, span, width, allowed):
    for start in range(0, rows, span):
        here = pl.ds(start, span)
        for p in range(width // (2 * HEAD_DIM)):
            at = p * 2 * HEAD_DIM
            query = stack_heads(qkv[here, pl.ds(at, 2 * HEAD_DIM)] * jnp.bfloat16(HEAD_DIM**-0.5))
            key = qkv[here, pl.ds(width + at, 2 * HEAD_DIM)]
            value = qkv[here, pl.ds(2 * width + at, 2 * HEAD_DIM)]
            shares = pair_shares(query, key, allowed)
            both = dot_nn(shares.astype(jnp.bfloat16), value)
            mixed[here, pl.ds(at, 2 * HEAD_DIM)] = unstack_heads(both).astype(jnp.bfloat16)


def attend_back(qkv, d_mixed, d_qkv, rows, span, width, allowed):
    scale = HEAD_DIM**-0.5
    for start in range(0, rows, span):
        here = pl.ds(start, span)
        for p in range(width // (2 * HEAD_DIM)):
            at = p * 2 * HEAD_DIM
            query = stack_heads(qkv[here, pl.ds(at, 2 * HEAD_DIM)] * jnp.bfloat16(scale))
            key = qkv[here, pl.ds(width + at, 2 * HEAD_DIM)]
            value = qkv[here, pl.ds(2 * width + at, 2 * HEAD_DIM)]
            grad = stack_heads(d_mixed[here, pl.ds(at, 2 * HEAD_DIM)])
            shares = pair_shares(query, key, allowed)
            d_shares = dot_nt(grad, value)
            delta = jnp.sum(shares * d_shares, -1, keepdims=True)
            d_scores = (shares * (d_shares - delta)).astype(jnp.bfloat16)
            d_query = unstack_heads(dot_nn(d_scores, key)) * scale
            d_key = dot_tn(d_scores, query)
            d_value = dot_tn(shares.astype(jnp.bfloat16), grad)
            d_qkv[here, pl.ds(at, 2 * HEAD_DIM)] = d_query.astype(jnp.bfloat16)
            d_qkv[here, pl.ds(width + at, 2 * HEAD_DIM)] = d_key.astype(jnp.bfloat16)
            d_qkv[here, pl.ds(2 * width + at, 2 * HEAD_DIM)] = d_value.astype(jnp.bfloat16)


def row_sums(value):
    return jnp.sum(value.astype(jnp.float32), 0, keepdims=True)


def whole(shape):
    return pl.BlockSpec(shape, lambda *i: (0,) * len(shape), pipeline_mode=pl.Buffered(1))


def select(rows, columns, first):
    row = lax.broadcasted_iota(jnp.int32, (rows, columns), 0)
    column = lax.broadcasted_iota(jnp.int32, (rows, columns), 1)
    return jnp.where(row == first + column, 1.0, 0.0).astype(jnp.bfloat16)


def spread_slots(rows_of_slots, n, per, size):
    columns = n * size
    step = min(columns, 768)
    out = []
    lane = lax.broadcasted_iota(jnp.int32, (128, 1), 0)
    slot = lax.broadcasted_iota(jnp.int32, (n * per, 1), 0) // per
    for c in range(0, columns, step):
        column = lax.broadcasted_iota(jnp.int32, (1, step), 1) + c
        ones = jnp.where(column % size == lane, 1.0, 0.0).astype(jnp.bfloat16)
        laid = dot_nn(rows_of_slots, ones)
        kept = jnp.where(slot == column // size, laid, 0.0)
        out.append(jnp.sum(kept.reshape(n, per, step), 0))
    return out[0] if len(out) == 1 else jnp.concatenate(out, 1)


SMALL_ROWS = 16


def misc_rows(per_output):
    return SMALL_ROWS + -(-per_output // 16) * 16


def weights_kernel(grid, sizes, *refs):
    width, per_project, per_output, per_up, per_pair, places_n = sizes
    n, ndims = grid.n, len(grid.dims)
    pw, ow, uw, dw, pb, ob, ub, db, ng, nb, pt, cot = refs[:12]
    mixed0, up0, down0, mixed1, up1, cot1, own_down1, vec, vec_pair, vec_up, table = refs[12:23]
    own_mixed, own_misc, misc_f, misc_all, own_cot, cot_head = refs[23:29]
    send_sem, recv_sem, local_sem = refs[29:]
    coords = grid.coords()
    me_line = coords[-1]
    cot_copy = pltpu.make_async_copy(cot.at[:, pl.ds(0, 8)], cot_head, local_sem.at[0])
    cot_copy.start()

    misc_f[...] = jnp.zeros_like(misc_f)
    at = 0
    for ref, size in ((pb, per_pair), (ob, per_output), (ub, per_up), (db, per_output)):
        misc_f[pl.ds(at, 2), pl.ds(0, size)] = ref[...].astype(jnp.float32)
        at += 2
    for ref in (ng, nb):
        for b in range(2):
            misc_f[pl.ds(at, 2), pl.ds(0, per_output)] = ref[b].astype(jnp.float32)
            at += 2
    misc_f[pl.ds(SMALL_ROWS, per_output), pl.ds(0, places_n)] = pt[...].astype(jnp.float32)
    own_misc[...] = misc_f[...].astype(jnp.bfloat16)

    def pack(b):
        rows = per_project + per_output
        own_mixed[b] = (
            dot_nn(place_rows(rows, per_project, 0), pw[b]) + dot_nn(place_rows(rows, per_output, per_project), ow[b])
        ).astype(jnp.bfloat16)

    def place_rows(rows, size, first):
        row = lax.broadcasted_iota(jnp.int32, (rows, size), 0)
        column = lax.broadcasted_iota(jnp.int32, (rows, size), 1)
        return jnp.where(row == first + column, 1.0, 0.0).astype(jnp.bfloat16)

    pack(0)
    grid.greet(coords)

    units, chunks = [], []

    def add(own, line, dest, cuts):
        for cut in cuts:
            chunks.append((own, line, dest, *cut))
        return list(range(len(chunks) - len(cuts), len(chunks)))

    mixed_rows = per_project + per_output
    units += [add(own_mixed.at[0], None, mixed0, u) for u in pairs(mixed_rows)]
    units[0] += add(own_misc, None, misc_all, [(0, misc_rows(per_output), 0)])
    up_units = len(units)
    units += [add(uw.at[0], None, up0, u) for u in pairs(per_up)]
    down_units = len(units)
    units += [add(dw.at[0], None, down0, u) for u in pairs(per_up)]
    line_units = [add(own_mixed.at[1], mixed1, None, [h]) for h in halves(mixed_rows, jnp.bfloat16)]
    line_units += [add(uw.at[1], up1, None, [h]) for h in halves(per_up, jnp.bfloat16)]
    line_units[0] += add(own_cot, cot1, None, [(0, own_cot.shape[0], 0)])
    gather = Gather(grid, coords, chunks, send_sem, recv_sem)

    def start(unit, stage):
        for k in unit:
            gather.start(k, stage)

    start(units[0], 0)
    pack(1)
    cot_copy.wait()
    for s in range(own_cot.shape[0]):
        own_cot[pl.ds(s, 1), :] = cot_head[s, 0:1, :]
    locals_ = [
        pltpu.make_async_copy(own_mixed.at[0], mixed0.at[coords], local_sem.at[0]),
        pltpu.make_async_copy(uw.at[0], up0.at[coords], local_sem.at[1]),
        pltpu.make_async_copy(dw.at[0], down0.at[coords], local_sem.at[2]),
        pltpu.make_async_copy(own_mixed.at[1], mixed1.at[me_line], local_sem.at[3]),
        pltpu.make_async_copy(uw.at[1], up1.at[me_line], local_sem.at[4]),
        pltpu.make_async_copy(dw.at[1], own_down1, local_sem.at[5]),
        pltpu.make_async_copy(own_cot, cot1.at[me_line], local_sem.at[6]),
    ]
    for copy in locals_:
        copy.start()
    misc_all[coords] = own_misc[...]
    for copy in locals_:
        copy.wait()

    def vectors():
        small = misc_all[..., 0:SMALL_ROWS, :].reshape(n * SMALL_ROWS, 128)
        singles = spread_slots(small, n, SMALL_ROWS, per_output)
        pairs = spread_slots(small, n, SMALL_ROWS, per_pair)
        ups = spread_slots(small, n, SMALL_ROWS, per_up)
        for b in range(2):
            vec[b, 0:1, :] = singles[2 + b : 3 + b]
            vec[b, 1:2, :] = singles[6 + b : 7 + b]
            vec[b, 2:4, :] = singles[8 + 2 * b : 10 + 2 * b]
            vec[b, 4:6, :] = singles[12 + 2 * b : 14 + 2 * b]
            vec[b, 6:8, :] = jnp.zeros((2, width), jnp.float32)
            vec_pair[b, :, 0:width] = pairs[b : b + 1, :width]
            vec_pair[b, :, width : 2 * width] = jnp.zeros((1, width), jnp.float32)
            vec_pair[b, :, 2 * width : 3 * width] = pairs[b : b + 1, width:]
            vec_up[b] = ups[4 + b : 5 + b]
        for d in range(n):
            where, rest = [], d
            for extent in grid.dims[::-1]:
                where.append(rest % extent)
                rest //= extent
            rows = misc_all[tuple(where[::-1]) + (pl.ds(SMALL_ROWS, misc_rows(per_output) - SMALL_ROWS),)].astype(jnp.float32)
            table[pl.ds(d * per_output, per_output), :] = rows[:per_output]

    count = len(units)
    line_ticks = {count - 6: line_units[:1], count - 4: line_units[1:2], count - 1: line_units[2:]} if count >= 7 else {0: line_units}
    for tick in range(1, count + ndims):
        for stage in range(1, ndims + 1):
            u = tick - stage
            if not 0 <= u < count:
                continue
            for k in units[u]:
                gather.landed(k, stage - 1)
                if stage < ndims:
                    gather.start(k, stage)
            if stage == 1:
                if u + 1 < count:
                    start(units[u + 1], 0)
                for unit in line_ticks.get(u, []):
                    start(unit, 0)
            if stage == ndims and u == 0:
                vectors()
    for unit in line_units:
        for k in unit:
            gather.landed(k, 0)
            gather.sent(k, 0, 1)
    for unit in units:
        for k in unit:
            gather.sent(k, 0, ndims)


def pairs(rows):
    if rows % 32:
        return [[(0, rows, 0)]]
    return [[(r, 16, 0), (r + 16, 16, 1)] for r in range(0, rows, 32)]


def gather_weights(grid, arrays, cid):
    project_weight, output_weight, up_weight, down_weight, project_bias = arrays[:5]
    per_project, per_output, per_up = project_weight.shape[1], output_weight.shape[1], up_weight.shape[1]
    width = project_weight.shape[2]
    per_pair = project_bias.shape[1]
    places_n = arrays[10].shape[1]
    segs = arrays[11].shape[0]
    n = grid.n
    low, full = jnp.bfloat16, jnp.float32
    mixed_rows = per_project + per_output
    small_rows = misc_rows(per_output)
    fs = grid.fsdp
    count = 2 + sum(len(u) for r in (mixed_rows, per_up, per_up) for u in pairs(r)) + sum(len(halves(r, low)) for r in (mixed_rows, per_up))
    vmem, anywhere = pl.BlockSpec(memory_space=pltpu.VMEM), pl.BlockSpec(memory_space=pl.ANY)

    def shape(s, d):
        return jax.ShapeDtypeStruct(s, d)

    return pl.pallas_call(
        functools.partial(weights_kernel, grid, (width, per_project, per_output, per_up, per_pair, places_n)),
        in_specs=[vmem] * 11 + [anywhere],
        out_specs=[anywhere] * 7 + [vmem] * 4,
        out_shape=[
            shape((*grid.dims, mixed_rows, width), low), shape((*grid.dims, per_up, width), low), shape((*grid.dims, per_up, width), low),
            shape((fs, mixed_rows, width), low), shape((fs, per_up, width), low), shape((fs, segs, width), full), shape((per_up, width), low),
            shape((2, 8, width), full), shape((2, 1, 3 * width), full), shape((2, 1, n * per_up), full), shape((width, 128), full),
        ],
        scratch_shapes=[
            pltpu.VMEM((2, mixed_rows, width), low),
            pltpu.VMEM((small_rows, 128), low), pltpu.VMEM((small_rows, 128), full), pltpu.VMEM((*grid.dims, small_rows, 128), low),
            pltpu.VMEM((segs, width), full), pltpu.VMEM((segs, 8, width), full),
        ]
        + grid.sems(count)
        + [pltpu.SemaphoreType.DMA((7,))],
        compiler_params=pltpu.CompilerParams(collective_id=cid, has_side_effects=True, vmem_limit_bytes=56 * 2**20),
        name="gather_weights",
    )(*arrays)


def forward_rows(x_low, x, w, r, rows, span, allowed, hook=lambda name: None):
    width = x.shape[1]
    step = width
    hook("project")
    for c in range(0, 3 * width, step):
        cut = pl.ds(c, step)
        r["qkv"][:, cut] = (dot_nt(x_low, w["project"][cut, :]) + w["project_b"][:, cut]).astype(jnp.bfloat16)
    attend_rows(r["qkv"], r["mixed"], rows, span, width, allowed)
    first = x + (dot_nt(r["mixed"][...], w["output"][...]) + w["output_b"])
    if "first" in r:
        r["first"](first)
    hook("first")
    unit_one, scale_one, unit_two, scale_two = feed_forward(first, w, r, hook)
    return unit_one, scale_one, unit_two, scale_two


def feed_forward(first, w, r, hook=lambda name: None):
    unit_one, scale_one = normalise(first)
    normed = unit_one * w["gains"][0:1, :] + w["shifts"][0:1, :]
    normed_low = normed.astype(jnp.bfloat16)
    r["normed"][...] = normed_low
    hidden_units = w["up"].shape[0]
    step = normed.shape[1]
    for c in range(0, hidden_units, step):
        cut = pl.ds(c, step)
        inner = dot_nt(normed_low, w["up"][cut, :]) + w["up_b"][:, cut]
        value, slope = gelu_pair(inner)
        r["hidden"][:, cut] = value.astype(jnp.bfloat16)
        r["slope"][:, cut] = slope.astype(r["slope"].dtype)
    hook("down")
    second = normed + (dot_nn(r["hidden"][...], w["down"][...]) + w["down_b"])
    unit_two, scale_two = normalise(second)
    return unit_one, scale_one, unit_two, scale_two


def mlp_back(grad, unit_one, scale_one, unit_two, scale_two, w, r, hook=lambda name: None):
    d_second = norm_back(grad, unit_two, scale_two, w["gains"][1:2, :])
    d_down = d_second.astype(jnp.bfloat16)
    r["d_down"][...] = d_down
    hidden_units = w["up"].shape[0]
    step = grad.shape[1]
    for c in range(0, hidden_units, step):
        cut = pl.ds(c, step)
        d_hidden = dot_nt(d_down, w["down"][cut, :])
        r["d_inner"][:, cut] = (d_hidden * r["slope"][:, cut].astype(jnp.float32)).astype(jnp.bfloat16)
    hook("up")
    d_normed = d_second + dot_nn(r["d_inner"][...], w["up"][...])
    d_first = norm_back(d_normed, unit_one, scale_one, w["gains"][0:1, :])
    sums = (
        row_sums(d_normed * unit_one), row_sums(grad * unit_two), row_sums(d_normed), row_sums(grad),
        row_sums(d_down), row_sums(r["d_inner"][...]),
    )
    return d_first, sums


def small_of(vec, vec_pair, vec_up, b):
    return {
        "project_b": vec_pair.at[b], "output_b": vec[b, 0:1, :], "up_b": vec_up.at[b], "down_b": vec[b, 1:2, :],
        "gains": vec[b, 2:4, :], "shifts": vec[b, 4:6, :],
    }


def unpack_mixed(grid, mixed, project, output, per_project):
    rows, width = mixed.shape[-2:]
    per_output = rows - per_project
    for d in range(grid.n):
        where, rest = [], d
        for size in grid.dims[::-1]:
            where.append(rest % size)
            rest //= size
        part = mixed[tuple(where[::-1])]
        project[pl.ds(d * per_project, per_project), :] = part[:per_project]
        output[pl.ds(d * per_output, per_output), :] = part[per_project:]


def spread(events, points):
    return [events[len(events) * p // points : len(events) * (p + 1) // points] for p in range(points)]


def segment_forward_kernel(grid, tile, steps, per_project, *refs):
    (tokens, grads, mixed0, up0, down0, vec, vec_pair, vec_up, line_mixed, line_up, line_cot, own_down) = refs[:12]
    names = ("qkv", "mixed", "d_first", "seg_low", "norm_sums", "up_sums")
    r = dict(zip(names, refs[12:18]))
    project_out, output_out, all_first, mixed1, up1, down1, all_cot, partial_up, partial_down = refs[18:27]
    r.update(zip(("slope", "normed", "hidden", "d_down", "d_inner"), refs[27:32]))
    held_mixed, project, output, up, down, own_first, sum_up, sum_down = refs[32:40]
    send_sem, recv_sem, local_sem = refs[40:]
    w = small_of(vec, vec_pair, vec_up, 0)
    w.update(project=project, output=output, up=up, down=down)
    width = tokens.shape[1]
    step = pl.program_id(0)
    last = steps - 1
    ndims = len(grid.dims)
    coords = grid.coords()
    loads = [pltpu.make_async_copy(*p, local_sem.at[i]) for i, p in enumerate(
        ((mixed0, held_mixed), (up0, up), (down0, down)))]
    stores = [pltpu.make_async_copy(*p, local_sem.at[3 + i]) for i, p in enumerate(
        ((project, project_out), (output, output_out)))]
    here = (coords[:-1]) + (slice(None),)
    lines = [pltpu.make_async_copy(a, b.at[here], local_sem.at[5 + i]) for i, (a, b) in enumerate(
        ((line_mixed, mixed1), (line_up, up1), (line_cot, all_cot)))]
    lines.append(pltpu.make_async_copy(own_down, down1.at[coords], local_sem.at[8]))
    keep_first = pltpu.make_async_copy(own_first, all_first.at[coords], local_sem.at[9])

    chunks, groups = [], []
    for own, line, dest, rows in (
        (None, line_mixed, mixed1, line_mixed.shape[1]), (None, line_up, up1, line_up.shape[1]), (own_down, None, down1, own_down.shape[0])
    ):
        cuts = halves(rows, jnp.bfloat16)
        groups.append(list(range(len(chunks), len(chunks) + len(cuts))))
        chunks += [(own, line, dest, *cut) for cut in cuts]
    groups[0].append(len(chunks))
    chunks.append((None, line_cot, all_cot, 0, line_cot.shape[1], 1))
    first_chunk = len(chunks)
    chunks.append((own_first, None, all_first, 0, own_first.shape[0], 0))
    gather = Gather(grid, coords, chunks, send_sem, recv_sem)

    ticks = ndims + 1

    def go(tick):
        if tick == 1:
            for copy in lines:
                copy.wait()
        for group in groups:
            late = chunks[group[0]][1] is None
            stage = tick if late else tick + 1
            for k in group:
                if stage > (0 if late else 1) and stage <= ndims:
                    gather.landed(k, stage - 1)
                if stage < ndims:
                    gather.start(k, stage)

    plan = {}
    for tick in range(1, ticks - 1):
        at = round((2 * steps - 1) * tick / (ticks - 2))
        if ndims == 4 and steps == 4:
            at = (1, 5, 7)[tick - 1]
        plan.setdefault(at, []).append(tick)

    def at_point(which):
        for at, some in plan.items():
            if at % 2 == which:

                @pl.when(step == at // 2)
                def _(some=some):
                    for tick in some:
                        go(tick)

    first_points = ["first", "back", "tail", "end"]
    first_events = [[] for unused in first_points]
    stages = list(range(ndims))
    for i, stage in enumerate(stages):
        first_events[min(i, len(first_points) - 1)].append(stage)

    def first_point(name):
        @pl.when(step == last)
        def _():
            for stage in first_events[first_points.index(name)]:
                if stage == 0:
                    keep_first.start()
                else:
                    gather.landed(first_chunk, stage - 1)
                    if stage == 1:
                        keep_first.wait()
                gather.start(first_chunk, stage)

    @pl.when(step == 0)
    def _():
        for copy in loads:
            copy.start()
        grid.greet(coords)
        go(0)
        for copy in lines:
            copy.start()
        loads[0].wait()
        unpack_mixed(grid, held_mixed, project, output, per_project)
        for copy in stores:
            copy.start()

    def hook(name):
        if name == "first":
            first_point("first")

            @pl.when(step == 0)
            def _():
                for copy in loads[1:]:
                    copy.wait()

            at_point(0)

    def take_first(first):
        for s in range(tile // SEG_LEN):
            own_first[pl.ds(step * (tile // SEG_LEN) + s, 1), :] = first[s * SEG_LEN : s * SEG_LEN + 1]

    r["first"] = take_first
    x_low = tokens[...]
    x = x_low.astype(jnp.float32)
    unit_one, scale_one, unit_two, scale_two = forward_rows(x_low, x, w, r, tile, SEG_LEN, None, hook)
    seg_out = unit_two * w["gains"][1:2, :] + w["shifts"][1:2, :]
    r["seg_low"][...] = seg_out.astype(jnp.bfloat16)
    first_point("back")
    place = lax.broadcasted_iota(jnp.int32, (tile, 1), 0) % SEG_LEN
    grad = jnp.where(place == 0, 0.0, grads[...])
    d_first, sums = mlp_back(grad, unit_one, scale_one, unit_two, scale_two, w, r, hook)
    r["d_first"][...] = d_first
    gathered = jnp.concatenate(list(sums[:5]) + [jnp.zeros((3, width), jnp.float32)], 0)

    @pl.when(step == 0)
    def _():
        r["norm_sums"][...] = jnp.zeros_like(r["norm_sums"])
        r["up_sums"][...] = jnp.zeros_like(r["up_sums"])
        sum_up[...] = jnp.zeros_like(sum_up)
        sum_down[...] = jnp.zeros_like(sum_down)

    r["norm_sums"][...] += gathered
    r["up_sums"][...] += jnp.broadcast_to(sums[5], r["up_sums"].shape)
    first_point("tail")
    for left, right, total in (("hidden", "d_down", sum_down), ("d_inner", "normed", sum_up)):
        for c in range(0, total.shape[0], width):
            total[pl.ds(c, width), :] += dot_tn(r[left][:, pl.ds(c, width)], r[right][...])
    first_point("end")
    at_point(1)

    @pl.when(step == last)
    def _():
        down[...] = sum_down[...].astype(jnp.bfloat16)
        up[...] = sum_up[...].astype(jnp.bfloat16)
        out = [pltpu.make_async_copy(*p, local_sem.at[i]) for i, p in enumerate(((down, partial_down), (up, partial_up)))]
        for copy in out:
            copy.start()
        go(ticks - 1)
        for g in range(len(groups)):
            for k in groups[g]:
                gather.sent(k, 1 if chunks[k][1] is not None else 0, ndims)
        gather.landed(first_chunk, ndims - 1)
        gather.sent(first_chunk, 0, ndims)
        for copy in stores + out:
            copy.wait()


def segment_forward(grid, tokens, grads, mixed0, up0, down0, smalls, lines, per_project, cid):
    rows, width = tokens.shape
    per_up = up0.shape[-2]
    mixed_rows = mixed0.shape[-2]
    hidden_units = per_up * grid.n
    tile = 2 * SEG_LEN
    steps = rows // tile
    segs = rows // SEG_LEN
    low, full = jnp.bfloat16, jnp.float32
    up0, down0 = up0.reshape(hidden_units, width), down0.reshape(hidden_units, width)
    count = 2 + sum(len(halves(r, low)) for r in (mixed_rows, per_up, per_up))
    vmem, anywhere = pl.BlockSpec(memory_space=pltpu.VMEM), pl.BlockSpec(memory_space=pl.ANY)

    def cut(columns):
        return pl.BlockSpec((tile, columns), lambda i: (i, 0))

    def shape(columns, dtype):
        return jax.ShapeDtypeStruct((rows, columns), dtype)

    return pl.pallas_call(
        functools.partial(segment_forward_kernel, grid, tile, steps, per_project),
        grid=(steps,),
        in_specs=[cut(width), cut(width)] + [anywhere] * 3 + [whole(s.shape) for s in (*smalls, *lines)],
        out_specs=[
            cut(3 * width), cut(width), cut(width), cut(width),
            pl.BlockSpec((8, width), lambda i: (0, 0)), pl.BlockSpec((8, hidden_units), lambda i: (0, 0)),
        ]
        + [anywhere] * 9,
        out_shape=[
            shape(3 * width, low), shape(width, low), shape(width, full), shape(width, low),
            jax.ShapeDtypeStruct((8, width), full), jax.ShapeDtypeStruct((8, hidden_units), full),
            jax.ShapeDtypeStruct((3 * width, width), low), jax.ShapeDtypeStruct((width, width), low),
            jax.ShapeDtypeStruct((*grid.dims, segs, width), full),
            jax.ShapeDtypeStruct((*grid.dims, mixed_rows, width), low),
            jax.ShapeDtypeStruct((*grid.dims, per_up, width), low), jax.ShapeDtypeStruct((*grid.dims, per_up, width), low),
            jax.ShapeDtypeStruct((*grid.dims, segs, width), full),
            jax.ShapeDtypeStruct((hidden_units, width), low), jax.ShapeDtypeStruct((hidden_units, width), low),
        ],
        scratch_shapes=[
            pltpu.VMEM((tile, hidden_units), low), pltpu.VMEM((tile, width), low), pltpu.VMEM((tile, hidden_units), low),
            pltpu.VMEM((tile, width), low), pltpu.VMEM((tile, hidden_units), low), pltpu.VMEM((*grid.dims, mixed_rows, width), low),
            pltpu.VMEM((3 * width, width), low), pltpu.VMEM((width, width), low),
            pltpu.VMEM((hidden_units, width), low), pltpu.VMEM((hidden_units, width), low), pltpu.VMEM((segs, width), full),
            pltpu.VMEM((hidden_units, width), full), pltpu.VMEM((hidden_units, width), full),
        ]
        + grid.sems(count)
        + [pltpu.SemaphoreType.DMA((10,))],
        compiler_params=pltpu.CompilerParams(collective_id=cid, has_side_effects=True, vmem_limit_bytes=60 * 2**20),
        name="segment_forward",
    )(tokens, grads, mixed0, up0, down0, *smalls, *lines)


def own_columns(value, first, size):
    return dot_nn(value, select(value.shape[1], size, first)).astype(jnp.bfloat16)


def own_sums(value, first, size):
    row = lax.broadcasted_iota(jnp.int32, (value.shape[1], size), 0)
    column = lax.broadcasted_iota(jnp.int32, (value.shape[1], size), 1)
    ones = jnp.where(row == first + column, 1.0, 0.0)
    return jnp.dot(value, ones, precision=highest, preferred_element_type=jnp.float32)


def document_of(placed, long_total):
    long_docs = long_total // LONG_SEGS
    is_long = placed < long_total
    rest = placed - long_total
    doc = jnp.where(is_long, placed // LONG_SEGS, long_docs + rest // SHORT_SEGS)
    return doc, jnp.where(is_long, placed % LONG_SEGS, rest % SHORT_SEGS)


def cross_kernel(grid, sizes, *refs):
    per_project, per_output, per_up, per_pair = sizes
    (firsts, grads, placed_row, placed_col, mixed1, up1, down1, up0, down0, vec, vec_pair, vec_up, table, partial) = refs[:14]
    g_project, g_output, g_up, g_down, z_up, z_down, smalls, g_table, cross_own, d_first_own, line_down = refs[14:25]
    names = ("qkv", "slope", "d_mixed", "mixed", "normed", "hidden", "d_down", "d_inner", "d_qkv")
    r = dict(zip(names, refs[25:34]))
    held_mixed, project, output, up, down, z_up_w, z_down_w, z_slope, z_normed, z_hidden, z_d_down, z_d_inner, rows_f = refs[34:47]
    held, *lands, send_sem, recv_sem, local_sem = refs[47:]
    coords = grid.coords()
    reduce, ticks = summing(grid, coords, held, lands, None, send_sem, recv_sem, 1)
    load_partial = pltpu.make_async_copy(partial, held, local_sem.at[5])
    load_partial.start()
    loads = [pltpu.make_async_copy(*p, local_sem.at[i]) for i, p in enumerate(
        ((up0, z_up_w), (down0, z_down_w), (mixed1, held_mixed), (up1, up), (down1, down)))]
    for copy in loads:
        copy.start()
    expected = grid.call(coords)
    slots, width = firsts.shape
    places_n = LONG_SEGS
    me = grid.flat()
    per_slots = slots // grid.n

    w0 = small_of(vec, vec_pair, vec_up, 0)
    w0.update(up=z_up_w, down=z_down_w)
    r0 = {"normed": z_normed, "hidden": z_hidden, "slope": z_slope, "d_down": z_d_down, "d_inner": z_d_inner}

    def hook0(name):
        if name == "down":
            loads[1].wait()
            load_partial.wait()
            grid.meet(expected)
            reduce(0)

    loads[0].wait()
    kept0 = feed_forward(firsts[...], w0, r0, hook0)
    seg_first = kept0[2] * w0["gains"][1:2, :] + w0["shifts"][1:2, :]
    doc_row, unused = document_of(placed_row[...], slots // 2)
    doc_col, place_col = document_of(placed_col[...], slots // 2)
    picker = place_col == lax.broadcasted_iota(jnp.int32, (slots, places_n), 1)
    picker_f = jnp.where(picker, 1.0, 0.0)
    x = seg_first + dot_nt(picker_f.astype(jnp.bfloat16), table[:, 0:places_n].astype(jnp.bfloat16))

    w = small_of(vec, vec_pair, vec_up, 1)
    w.update(project=project, output=output, up=up, down=down)
    loads[2].wait()
    unpack_mixed(grid, held_mixed, project, output, per_project)
    x_low = x.astype(jnp.bfloat16)
    allowed = doc_col == doc_row
    allowed = jnp.concatenate([allowed, allowed], 0)
    reduce(1)

    def hook(name):
        if name == "first":
            loads[3].wait()
        if name == "down":
            loads[4].wait()

    kept = forward_rows(x_low, x, w, r, slots, slots, allowed, hook)
    mine = pl.ds(pl.multiple_of(me * per_slots, per_slots), per_slots)
    rows_f[...] = kept[2] * w["gains"][1:2, :] + w["shifts"][1:2, :]
    cross_own[...] = rows_f[mine, :]
    d_first, sums = mlp_back(grads[...], *kept, w, r)
    reduce(2)
    branch = d_first.astype(jnp.bfloat16)
    r["d_mixed"][...] = dot_nn(branch, output[...]).astype(jnp.bfloat16)
    attend_back(r["qkv"], r["d_mixed"], r["d_qkv"], slots, slots, width, allowed)
    d_x = d_first + dot_nn(r["d_qkv"][...], project[...])
    for tick in range(3, ticks):
        reduce(tick)
    store = pltpu.make_async_copy(held.at[coords[:-1]], line_down, local_sem.at[5])
    store.start()

    g_project[...] = dot_tn(own_columns(r["d_qkv"][...], me * per_project, per_project), x_low)
    g_output[...] = dot_tn(own_columns(branch, me * per_output, per_output), r["mixed"][...])
    g_up[...] = dot_tn(own_columns(r["d_inner"][...], me * per_up, per_up), r["normed"][...])
    g_down[...] = dot_tn(own_columns(r["hidden"][...], me * per_up, per_up), r["d_down"][...])
    smalls[...] = jnp.zeros_like(smalls)
    norm_rows = jnp.concatenate(list(sums[:5]) + [row_sums(branch), jnp.zeros((2, width), jnp.float32)], 0)
    smalls[0:8, 0:per_output] = own_sums(norm_rows, me * per_output, per_output)
    up_rows = jnp.broadcast_to(sums[5], (8, sums[5].shape[1]))
    smalls[6:7, 0:per_up] = own_sums(up_rows, me * per_up, per_up)[0:1]
    qkv_sums = row_sums(r["d_qkv"][...])
    pair = jnp.concatenate([qkv_sums[:, :width], qkv_sums[:, 2 * width :]], 1)
    smalls[7:8, 0:per_pair] = own_sums(jnp.broadcast_to(pair, (8, 2 * width)), me * per_pair, per_pair)[0:1]
    g_table[...] = lax.dot_general(
        own_sums(d_x, me * per_output, per_output), picker_f, (((0,), (0,)), ((), ())),
        precision=highest, preferred_element_type=jnp.float32,
    )

    d_first0, sums = mlp_back(d_x, *kept0, w0, r0)
    rows_f[...] = d_first0
    d_first_own[...] = rows_f[mine, :]
    z_up[...] = dot_tn(own_columns(z_d_inner[...], me * per_up, per_up), z_normed[...])
    z_down[...] = dot_tn(own_columns(z_hidden[...], me * per_up, per_up), z_d_down[...])
    norm_rows = jnp.concatenate(list(sums[:5]) + [jnp.zeros((3, width), jnp.float32)], 0)
    smalls[8:16, 0:per_output] = own_sums(norm_rows, me * per_output, per_output)
    up_rows = jnp.broadcast_to(sums[5], (8, sums[5].shape[1]))
    smalls[14:15, 0:per_up] = own_sums(up_rows, me * per_up, per_up)[0:1]
    store.wait()
    reduce(None)


def summing(grid, coords, held, lands, out, send_sem, recv_sem, short=0):
    ndims = len(grid.dims) - short
    units = [halves(held.shape[-2], held.dtype)]
    cuts = [cut for unit in units for cut in unit]
    whole_dims = len(grid.dims)
    chunks = [(held, lands[k * whole_dims : (k + 1) * whole_dims], out, *cut) for k, cut in enumerate(cuts)]
    scatter = Scatter(grid, coords, chunks, send_sem, recv_sem)
    per = len(units[0])

    def reduce(tick):
        if tick is None:
            for k in range(len(chunks)):
                scatter.sent(k, ndims)
            return
        for stage in range(ndims + 1):
            u = tick - stage
            if not 0 <= u < len(units):
                continue
            for k in range(u * per, (u + 1) * per):
                if stage > 0:
                    scatter.add(k, stage - 1)
                if stage < ndims:
                    scatter.start(k, stage)

    return reduce, len(units) + ndims


def summing_scratch(grid, rows, width):
    low = jnp.bfloat16
    cuts = halves(rows, low)
    lands = [land for cut in cuts for land in Scatter.landing(grid, cut[1], width, low, cut[2])]
    return [pltpu.VMEM((*grid.dims, rows, width), low)] + lands + grid.sems(len(cuts))


def cross_block(grid, firsts, grads, placement, mixed1, up1, down1, up0, down0, smalls, table, sizes, partial, cid):
    slots, width = firsts.shape
    per_project, per_output, per_up, per_pair = sizes
    hidden_units = per_up * grid.n
    low, full = jnp.bfloat16, jnp.float32
    per_slots = slots // grid.n
    flat = lambda ref: ref.reshape(hidden_units, width)
    vmem, anywhere = pl.BlockSpec(memory_space=pltpu.VMEM), pl.BlockSpec(memory_space=pl.ANY)
    outs = [
        (per_project, width), (per_output, width), (per_up, width), (per_up, width), (per_up, width), (per_up, width),
        (16, 128), (per_output, LONG_SEGS), (per_slots, width), (per_slots, width),
    ]

    def held(*shape, dtype=low):
        return pltpu.VMEM(shape, dtype)

    return pl.pallas_call(
        functools.partial(cross_kernel, grid, sizes),
        in_specs=[vmem] * 4 + [anywhere] * 5 + [vmem] * 4 + [anywhere],
        out_specs=[vmem] * len(outs) + [anywhere],
        out_shape=[jax.ShapeDtypeStruct(s, full) for s in outs] + [jax.ShapeDtypeStruct((grid.fsdp, per_up, width), low)],
        scratch_shapes=[
            held(slots, 3 * width), held(slots, hidden_units), held(slots, width), held(slots, width), held(slots, width),
            held(slots, hidden_units), held(slots, width), held(slots, hidden_units), held(slots, 3 * width),
            held(*mixed1.shape), held(3 * width, width), held(width, width), held(hidden_units, width), held(hidden_units, width),
            held(hidden_units, width), held(hidden_units, width), held(slots, hidden_units), held(slots, width),
            held(slots, hidden_units), held(slots, width), held(slots, hidden_units), held(slots, width, dtype=full),
            *summing_scratch(grid, per_up, width),
            pltpu.SemaphoreType.DMA((6,)),
        ],
        compiler_params=pltpu.CompilerParams(collective_id=cid, has_side_effects=True, vmem_limit_bytes=63 * 2**20),
        name="cross_block",
    )(firsts, grads, placement[None, :], placement[:, None], mixed1, flat(up1), flat(down1), flat(up0), flat(down0), *smalls, table, partial)


def segment_backward_kernel(grid, tile, steps, per_project, *refs):
    (qkv, d_first, cls_grad, seg_low, cls_out, mixed, tokens, project, output, partial, cls_up, cls_down, line_down, norm_sums, up_sums,
     own_small) = refs[:16]
    d_x, layer_out, up_sum, down_sum, mixed_sum, small_out = refs[16:22]
    d_mixed, d_qkv, d_branch, sum_project, sum_output, packed, sums_qkv, sums_out, small_held, small_sum = refs[22:32]
    first_sems = 32 + summing_length(grid, partial.shape[-2])
    held, *lands, send_sem, recv_sem = refs[32:first_sems]
    line_land, line_send, line_recv = refs[first_sems : first_sems + 3]
    *last_lands, last_send, last_recv, local_sem = refs[first_sems + 3 :]
    fs, ndims = grid.fsdp, len(grid.dims)
    width = d_first.shape[1]
    per_output = packed.shape[-2] - per_project
    step = pl.program_id(0)
    coords = grid.coords()
    reduce, ticks = summing(grid, coords, held, lands, up_sum, send_sem, recv_sem)
    line = []
    for ahead in range(1, fs):
        target, value = grid.peer(coords, ndims - 1, ahead)
        line.append(
            pltpu.make_async_remote_copy(
                line_down.at[value], line_land.at[ahead - 1], line_send.at[ahead - 1], line_recv.at[ahead - 1],
                device_id=target, device_id_type=MESH,
            )
        )
    plan = {}
    for tick in range(1, ticks - 1):
        at = (2, 5, 7)[tick - 1] if ticks == 5 and steps == 4 else min(2 * steps - 1, tick + 1)
        plan.setdefault(at, []).append(tick)

    def at_point(which):
        for at, some in plan.items():
            if at % 2 == which:

                @pl.when(step == at // 2)
                def _(some=some):
                    for tick in some:
                        reduce(tick)

    @pl.when(step == 0)
    def _():
        load = pltpu.make_async_copy(partial, held, local_sem.at[0])
        load.start()
        for total in (sums_qkv, sums_out, sum_project, sum_output, small_held):
            total[...] = jnp.zeros_like(total)
        grid.greet(coords)
        load.wait()
        reduce(0)
        for copy in line:
            copy.start()

    at_point(0)
    place = lax.broadcasted_iota(jnp.int32, (tile, 1), 0)
    grad, out = d_first[...], seg_low[...].astype(jnp.float32)
    for s in range(tile // SEG_LEN):
        here = pl.ds(step * (tile // SEG_LEN) + s, 1)
        grad = jnp.where(place == s * SEG_LEN, cls_grad[here, :], grad)
        out = jnp.where(place == s * SEG_LEN, cls_out[here, :], out)
    layer_out[...] = out.astype(jnp.bfloat16)
    branch = grad.astype(jnp.bfloat16)
    d_branch[...] = branch
    d_mixed[...] = dot_nn(branch, output[...]).astype(jnp.bfloat16)
    attend_back(qkv, d_mixed, d_qkv, tile, SEG_LEN, width, None)
    at_point(1)
    d_x[...] = grad + dot_nn(d_qkv[...], project[...])
    sums_qkv[...] += jnp.broadcast_to(row_sums(d_qkv[...]), sums_qkv.shape)
    sums_out[...] += jnp.broadcast_to(row_sums(branch), sums_out.shape)
    sum_output[...] += dot_tn(d_branch[...], mixed[...])
    for c in range(0, 3 * width, width):
        sum_project[pl.ds(c, width), :] += dot_tn(d_qkv[:, pl.ds(c, width)], tokens[...])

    @pl.when(step == steps - 1)
    def _():
        for d in range(grid.n):
            where, rest = [], d
            for size in grid.dims[::-1]:
                where.append(rest % size)
                rest //= size
            rows = [sum_project[pl.ds(d * per_project, per_project), :], sum_output[pl.ds(d * per_output, per_output), :]]
            where = tuple(where[::-1])
            packed[where] = jnp.concatenate(rows, 0).astype(jnp.bfloat16)
            per_pair = 2 * per_output
            at = d * per_pair if d * per_pair < width else d * per_pair + width
            for row, count, source, first, size in (
                (0, 5, norm_sums[0:5, :], d * per_output, per_output), (5, 1, sums_out[0:1, :], d * per_output, per_output),
                (6, 1, up_sums[0:1, :], d * 4 * per_output, 4 * per_output), (7, 1, sums_qkv[0:1, :], at, per_pair),
            ):
                small_held[where + (pl.ds(row, count), pl.ds(0, size))] = source[:, first : first + size]
        units, cuts = [], []
        for unit in pairs(packed.shape[-2]):
            units.append(list(range(len(cuts), len(cuts) + len(unit))))
            cuts += [(packed, mixed_sum, *cut) for cut in unit]
        units[0].append(len(cuts))
        cuts.append((small_held, small_sum, 0, 8, 0))
        last = Scatter(
            grid, coords, [(h, last_lands[k * ndims : (k + 1) * ndims], *rest) for k, (h, *rest) in enumerate(cuts)], last_send, last_recv
        )
        for tick in range(len(units) + ndims):
            for stage in range(ndims + 1):
                u = tick - stage
                if not 0 <= u < len(units):
                    continue
                for k in units[u]:
                    if stage > 0:
                        last.add(k, stage - 1)
                    if stage < ndims:
                        last.start(k, stage)
            if tick == 1:
                total = line_down[coords[-1]].astype(jnp.float32) + cls_down[...]
                for ahead, copy in enumerate(line):
                    copy.wait_recv()
                    total += line_land[ahead].astype(jnp.float32)
                down_sum[...] = total
            if tick == 2:
                reduce(ticks - 1)
                up_sum[...] += cls_up[...]
        small_out[0] = small_sum[...] + own_small[8:16, :]
        small_out[1] = own_small[0:8, :]
        for copy in line:
            copy.wait_send()
        for k in range(len(cuts)):
            last.sent(k, ndims)
        reduce(None)


def summing_length(grid, rows):
    return 1 + len(halves(rows, jnp.bfloat16)) * len(grid.dims) + 2


def segment_backward(
    grid, qkv, d_first, cls_grad, seg_low, cls_out, mixed, tokens, project, output, partial, cls_up, cls_down, line_down, norm_sums,
    up_sums, own_small, per_project, cid,
):
    rows, width = d_first.shape
    tile = 2 * SEG_LEN
    low, full = jnp.bfloat16, jnp.float32
    per_up = partial.shape[-2]
    mixed_rows = 4 * width // grid.n
    anywhere = pl.BlockSpec(memory_space=pl.ANY)

    def cut(columns):
        return pl.BlockSpec((tile, columns), lambda i: (i, 0))

    def fixed(*shape):
        return pl.BlockSpec(shape, lambda i: (0,) * len(shape))

    last_lands, last_count = [], 0
    for first, count, colour in [c for unit in pairs(mixed_rows) for c in unit]:
        last_lands += Scatter.landing(grid, count, width, low, colour)
        last_count += 1
    last_lands += Scatter.landing(grid, 8, 128, full, 0)
    return pl.pallas_call(
        functools.partial(segment_backward_kernel, grid, tile, rows // tile, per_project),
        grid=(rows // tile,),
        in_specs=[
            cut(3 * width), cut(width), whole(cls_grad.shape), cut(width), whole(cls_out.shape), cut(width), cut(width),
            whole(project.shape), whole(output.shape), anywhere,
            *[whole(a.shape) for a in (cls_up, cls_down, line_down, norm_sums, up_sums, own_small)],
        ],
        out_specs=[
            cut(width), cut(width), fixed(per_up, width), fixed(per_up, width), fixed(mixed_rows, width), fixed(2, 8, 128),
        ],
        out_shape=[
            jax.ShapeDtypeStruct((rows, width), full), jax.ShapeDtypeStruct((rows, width), low),
            jax.ShapeDtypeStruct((per_up, width), full), jax.ShapeDtypeStruct((per_up, width), full),
            jax.ShapeDtypeStruct((mixed_rows, width), full), jax.ShapeDtypeStruct((2, 8, 128), full),
        ],
        scratch_shapes=[
            pltpu.VMEM((tile, width), low), pltpu.VMEM((tile, 3 * width), low), pltpu.VMEM((tile, width), low),
            pltpu.VMEM((3 * width, width), full), pltpu.VMEM((width, width), full), pltpu.VMEM((*grid.dims, mixed_rows, width), low),
            pltpu.VMEM((8, 3 * width), full), pltpu.VMEM((8, width), full), pltpu.VMEM((*grid.dims, 8, 128), full), pltpu.VMEM((8, 128), full),
            *summing_scratch(grid, per_up, width),
            pltpu.VMEM((grid.fsdp - 1, per_up, width), low), pltpu.SemaphoreType.DMA((grid.fsdp - 1,)), pltpu.SemaphoreType.DMA((grid.fsdp - 1,)),
            *last_lands, *grid.sems(last_count + 1), pltpu.SemaphoreType.DMA((1,)),
        ],
        compiler_params=pltpu.CompilerParams(collective_id=cid, has_side_effects=True, vmem_limit_bytes=61 * 2**20),
        name="segment_backward",
    )(
        qkv, d_first, cls_grad, seg_low, cls_out, mixed, tokens, project, output, partial, cls_up, cls_down, line_down, norm_sums, up_sums,
        own_small,
    )


class Held:
    def __init__(self, value):
        self.value = value

    @property
    def shape(self):
        return self.value.shape

    @property
    def dtype(self):
        return self.value.dtype

    @staticmethod
    def plain(where):
        where = where if isinstance(where, tuple) else (where,)
        return tuple(slice(w.start, w.start + w.size) if isinstance(w, pl.Slice) else w for w in where)

    def __getitem__(self, where):
        return self.value[self.plain(where)]

    def __setitem__(self, where, value):
        self.value = self.value.at[self.plain(where)].set(value)


def sum_to_lines(partial):
    rows, width = partial.shape[-2:]
    fs = partial.shape[-3]
    return lax.psum_scatter(partial.reshape(-1, fs, rows, width), "dp", scatter_dimension=0, tiled=True)[0]


def cross_plain(grid, firsts, grads, placement, mixed1, up1, down1, up0, down0, smalls, table, sizes, partial, cid):
    slots, width = firsts.shape
    per_project, per_output, per_up, per_pair = sizes
    hidden_units = per_up * grid.n
    me = grid.flat()
    vec, vec_pair, vec_up = smalls

    def weights(b, up, down):
        return {
            "project_b": vec_pair[b], "output_b": vec[b, 0:1, :], "up_b": vec_up[b], "down_b": vec[b, 1:2, :],
            "gains": vec[b, 2:4, :], "shifts": vec[b, 4:6, :],
            "up": up.reshape(hidden_units, width), "down": down.reshape(hidden_units, width),
        }

    def blank(columns):
        return Held(jnp.zeros((slots, columns), jnp.bfloat16))

    def store():
        made = {k: blank(width) for k in ("mixed", "normed", "d_down", "d_mixed")}
        made.update({k: blank(hidden_units) for k in ("hidden", "slope", "d_inner")})
        made.update(qkv=blank(3 * width), d_qkv=blank(3 * width))
        return made

    def cut(matrix, size, axis=1):
        return lax.dynamic_slice_in_dim(matrix, me * size, size, axis)

    w0, w, r0, r = weights(0, up0, down0), weights(1, up1, down1), store(), store()
    parts = mixed1.reshape(grid.n, -1, width)
    w["project"] = parts[:, :per_project].reshape(3 * width, width)
    w["output"] = parts[:, per_project:].reshape(width, width)
    kept0 = feed_forward(firsts, w0, r0)
    seg_first = kept0[2] * w0["gains"][1:2, :] + w0["shifts"][1:2, :]
    doc, place = document_of(placement, slots // 2)
    picker = jnp.where(place[:, None] == jnp.arange(LONG_SEGS, dtype=jnp.int32)[None, :], 1.0, 0.0)
    x = seg_first + dot_nt(picker.astype(jnp.bfloat16), table[:, :LONG_SEGS].astype(jnp.bfloat16))
    x_low = x.astype(jnp.bfloat16)
    allowed = doc[:, None] == doc[None, :]
    allowed = jnp.concatenate([allowed, allowed], 0)
    kept = forward_rows(x_low, x, w, r, slots, slots, allowed)
    out = kept[2] * w["gains"][1:2, :] + w["shifts"][1:2, :]
    d_first, sums = mlp_back(grads, *kept, w, r)
    branch = d_first.astype(jnp.bfloat16)
    r["d_mixed"][...] = dot_nn(branch, w["output"]).astype(jnp.bfloat16)
    attend_back(r["qkv"], r["d_mixed"], r["d_qkv"], slots, slots, width, allowed)
    d_x = d_first + dot_nn(r["d_qkv"][...], w["project"])
    d_first0, sums0 = mlp_back(d_x, *kept0, w0, r0)
    qkv_sums = row_sums(r["d_qkv"][...])
    pair = jnp.concatenate([qkv_sums[:, :width], qkv_sums[:, 2 * width :]], 1)

    def laid(rows, size):
        return jnp.pad(cut(rows, size), ((0, 0), (0, 128 - size)))

    none = jnp.zeros((1, 128), jnp.float32)
    own_small = jnp.concatenate(
        [
            laid(jnp.concatenate(list(sums[:5]) + [row_sums(branch)], 0), per_output), laid(sums[5], per_up), laid(pair, per_pair),
            laid(jnp.concatenate(list(sums0[:5]), 0), per_output), none, laid(sums0[5], per_up), none,
        ],
        0,
    )
    g_table = lax.dot_general(cut(d_x, per_output), picker, (((0,), (0,)), ((), ())), precision=highest)
    per_slots = slots // grid.n
    return (
        dot_tn(cut(r["d_qkv"][...], per_project), x_low), dot_tn(cut(branch, per_output), r["mixed"][...]),
        dot_tn(cut(r["d_inner"][...], per_up), r["normed"][...]), dot_tn(cut(r["hidden"][...], per_up), r["d_down"][...]),
        dot_tn(cut(r0["d_inner"][...], per_up), r0["normed"][...]), dot_tn(cut(r0["hidden"][...], per_up), r0["d_down"][...]),
        own_small, g_table, cut(out, per_slots, 0), cut(d_first0, per_slots, 0), sum_to_lines(partial),
    )


def shards(
    grid,
    tokens,
    cotangent,
    placement,
    project_weight,
    project_bias,
    output_weight,
    output_bias,
    up_weight,
    up_bias,
    down_weight,
    down_bias,
    norm_gain,
    norm_bias,
    position_table,
):
    n = grid.n
    seg_count, seg_len, width = tokens.shape
    slots, rows = placement.shape[0], seg_count * seg_len
    per_project, per_output = project_weight.shape[2], output_weight.shape[2]
    per_pair, per_up = project_bias.shape[1], up_bias.shape[1]
    sizes = (per_project, per_output, per_up, per_pair)
    low_tokens = tokens.reshape(rows, width)

    mixed0, up0, down0, *lines, vec, vec_pair, vec_up, table = gather_weights(
        grid,
        [*(jnp.swapaxes(w, 1, 2) for w in (project_weight, output_weight, up_weight)), down_weight,
         project_bias, output_bias, up_bias, down_bias, norm_gain, norm_bias, position_table.T, cotangent],
        0,
    )
    smalls = [vec, vec_pair, vec_up]
    (qkv, mixed, d_first, seg_low, norm_sums, up_sums, project, output, all_first,
     mixed1, up1, down1, all_cot, partial_up, partial_down) = segment_forward(
        grid, low_tokens, cotangent.reshape(rows, width), mixed0, up0, down0, smalls, lines, per_project, 1
    )
    partial_up, partial_down = [p.reshape(*grid.dims, per_up, width) for p in (partial_up, partial_down)]
    g_project, g_output, g_up, g_down, z_up, z_down, own_small, g_table, cross_own, cls_grad, line_down = (cross_block if slots <= 256 else cross_plain)(
        grid, all_first.reshape(slots, width), all_cot.reshape(slots, width), placement, mixed1, up1, down1, up0, down0,
        smalls, table, sizes, partial_down, 2,
    )
    d_x, layer_out, up_sum, down_sum, mixed_sum, both = segment_backward(
        grid, qkv, d_first, cls_grad, seg_low, cross_own, mixed, low_tokens, project, output, partial_up, z_up, z_down, line_down,
        norm_sums, up_sums, own_small, per_project, 3,
    )
    return (
        layer_out.reshape(tokens.shape),
        d_x.reshape(tokens.shape),
        jnp.swapaxes(jnp.stack([mixed_sum[:per_project], g_project]), 1, 2),
        both[:, 7, :per_pair],
        jnp.swapaxes(jnp.stack([mixed_sum[per_project:], g_output]), 1, 2),
        both[:, 5, :per_output],
        jnp.swapaxes(jnp.stack([up_sum, g_up]), 1, 2),
        both[:, 6, :per_up],
        jnp.stack([down_sum, g_down]),
        both[:, 4, :per_output],
        both[:, 0:2, :per_output],
        both[:, 2:4, :per_output],
        g_table.T,
    )


def solution(mesh):
    grid = Grid(mesh)
    rows, cols, last = P(AXES, None, None), P(None, AXES), P(None, None, AXES)
    middle = P(None, AXES, None)
    return jax.shard_map(
        functools.partial(shards, grid),
        mesh=mesh,
        in_specs=(
            rows, rows, P(), last, cols, last, cols, last, cols, middle, cols, last, last, cols,
        ),
        out_specs=(rows, rows, last, cols, last, cols, last, cols, middle, cols, last, last, cols),
        check_vma=False,
    )
```

```python
import functools
import math

import jax
import jax.numpy as jnp
from jax import lax
from jax.experimental import pallas as pl
from jax.experimental.pallas import tpu as pltpu
from jax.sharding import PartitionSpec as P

HEADS = 12
HEAD_DIM = 64
SEG_LEN = 128
LONG_SEGS = 64
SHORT_SEGS = 16
MESH = pl.DeviceIdType.MESH
AXES = ("dp", "fsdp")

highest = lax.Precision.HIGHEST
epsilon = 1e-06
masked_score = -1e30


class Grid:
    def __init__(self, mesh):
        self.dp, self.fsdp = mesh.shape["dp"], mesh.shape["fsdp"]
        twos = int(math.log2(self.dp))
        self.dims = (2,) * twos + (self.fsdp,)
        self.n = self.dp * self.fsdp
        self.last = len(self.dims) - 1
        self.most = max(self.dims) - 1
        middle = list(range(self.last - 1))
        self.orders = (
            [self.last] + middle[::-1] + [self.last - 1],
            [self.last] + middle + [self.last - 1],
        )

    def coords(self):
        dp, fs = lax.axis_index("dp"), lax.axis_index("fsdp")
        twos = self.last
        return tuple((dp // 2 ** (twos - 1 - i)) % 2 for i in range(twos)) + (fs,)

    def flat(self):
        return lax.axis_index("dp") * self.fsdp + lax.axis_index("fsdp")

    def peer(self, coords, dim, step):
        other = list(coords)
        other[dim] = lax.rem(coords[dim] + step, self.dims[dim])
        dp = 0
        for value in other[:-1]:
            dp = dp * 2 + value
        return (dp, other[-1]), other[dim]

    def greet(self, coords):
        self.meet(self.call(coords))

    def call(self, coords):
        barrier = pltpu.get_barrier_semaphore()
        count = 0
        for dim, size in enumerate(self.dims):
            for step in range(1, size):
                where, unused = self.peer(coords, dim, step)
                pl.semaphore_signal(barrier, inc=1, device_id=where, device_id_type=MESH)
                count += 1
        return count

    def meet(self, count):
        pl.semaphore_wait(pltpu.get_barrier_semaphore(), count)

    def sems(self, chunks):
        shape = (chunks, len(self.dims), self.most)
        return [pltpu.SemaphoreType.DMA(shape), pltpu.SemaphoreType.DMA(shape)]


def index_of(coords, free, ndims):
    return tuple(slice(None) if d in free else coords[d] for d in range(ndims))


def halves(rows, dtype):
    tile = 16 if dtype == jnp.bfloat16 else 8
    if rows % (2 * tile) == 0:
        return [(0, rows // 2, 0), (rows // 2, rows // 2, 1)]
    return [(0, rows, 0)]


class Gather:
    def __init__(self, grid, coords, chunks, send_sem, recv_sem, base=0):
        self.grid, self.coords, self.chunks = grid, coords, chunks
        self.send_sem, self.recv_sem, self.base = send_sem, recv_sem, base
        self.stages = len(grid.dims)

    def copies(self, k, stage):
        own, line, dest, first, rows, colour = self.chunks[k]
        grid, coords = self.grid, self.coords
        order = grid.orders[colour]
        dim = order[stage]
        cut = (pl.ds(first, rows),)
        if stage == 0:
            source = own.at[cut]
            target_ref = dest.at[coords + cut] if line is None else line.at[(coords[-1],) + cut]
        else:
            target_ref = dest.at[index_of(coords, order[:stage], len(grid.dims)) + cut]
            source = line.at[(slice(None),) + cut] if line is not None and stage == 1 else target_ref
        made = []
        for step in range(1, grid.dims[dim]):
            target, unused = grid.peer(coords, dim, step)
            made.append(
                pltpu.make_async_remote_copy(
                    source,
                    target_ref,
                    self.send_sem.at[self.base + k, stage, step - 1],
                    self.recv_sem.at[self.base + k, stage, step - 1],
                    device_id=target,
                    device_id_type=MESH,
                )
            )
        return made

    def start(self, k, stage):
        for copy in self.copies(k, stage):
            copy.start()

    def landed(self, k, stage):
        for copy in self.copies(k, stage):
            copy.wait_recv()

    def sent(self, k, first_stage, last_stage):
        for stage in range(first_stage, last_stage):
            for copy in self.copies(k, stage):
                copy.wait_send()


class Scatter:
    def __init__(self, grid, coords, chunks, send_sem, recv_sem, base=0):
        self.grid, self.coords, self.chunks = grid, coords, chunks
        self.send_sem, self.recv_sem, self.base = send_sem, recv_sem, base
        self.stages = len(grid.dims)

    @staticmethod
    def landing(grid, rows, width, dtype, colour):
        order = grid.orders[colour][::-1]
        made = []
        for stage, dim in enumerate(order):
            left = [grid.dims[d] for d in range(len(order)) if d in order[stage + 1 :]]
            made.append(pltpu.VMEM((grid.dims[dim] - 1, *left, rows, width), dtype))
        return made

    def copies(self, k, stage):
        held, lands, out, first, rows, colour = self.chunks[k]
        grid, coords = self.grid, self.coords
        order = grid.orders[colour][::-1]
        dim = order[stage]
        made = []
        for step in range(1, grid.dims[dim]):
            target, value = grid.peer(coords, dim, step)
            there = list(coords)
            there[dim] = value
            where = index_of(there, order[stage + 1 :], len(order)) + (pl.ds(first, rows),)
            made.append(
                pltpu.make_async_remote_copy(
                    held.at[where],
                    lands[stage].at[step - 1],
                    self.send_sem.at[self.base + k, stage, step - 1],
                    self.recv_sem.at[self.base + k, stage, step - 1],
                    device_id=target,
                    device_id_type=MESH,
                )
            )
        return made

    def start(self, k, stage):
        for copy in self.copies(k, stage):
            copy.start()

    def add(self, k, stage):
        for copy in self.copies(k, stage):
            copy.wait_recv()
        held, lands, out, first, rows, colour = self.chunks[k]
        grid, coords = self.grid, self.coords
        order = grid.orders[colour][::-1]
        land = lands[stage]
        where = index_of(coords, order[stage + 1 :], len(order)) + (pl.ds(first, rows),)
        total = held[where]
        final = stage == self.stages - 1
        if final:
            total = total.astype(jnp.float32)
        for step in range(grid.dims[order[stage]] - 1):
            total += land[step].astype(total.dtype)
        if final:
            out[pl.ds(first, rows)] = total
        else:
            held[where] = total

    def sent(self, k, stages):
        for stage in range(stages):
            for copy in self.copies(k, stage):
                copy.wait_send()


def dot_nt(left, right):
    return lax.dot_general(
        left, right, (((1,), (1,)), ((), ())), preferred_element_type=jnp.float32
    )


def dot_nn(left, right):
    return lax.dot_general(
        left, right, (((1,), (0,)), ((), ())), preferred_element_type=jnp.float32
    )


def dot_tn(left, right):
    return lax.dot_general(
        left, right, (((0,), (0,)), ((), ())), preferred_element_type=jnp.float32
    )


def normalise(value):
    offset = value - jnp.mean(value, -1, keepdims=True)
    scale = lax.rsqrt(jnp.mean(offset * offset, -1, keepdims=True) + epsilon)
    return offset * scale, scale


def norm_back(grad, unit, scale, gain):
    pulled = grad * gain
    along = jnp.mean(pulled * unit, -1, keepdims=True)
    return scale * (pulled - jnp.mean(pulled, -1, keepdims=True) - unit * along)


def gelu_pair(x):
    bell = jnp.exp(-0.5 * x * x)
    t = 1.0 / (1.0 + (0.3275911 * 0.5**0.5) * jnp.abs(x))
    tail = t * (0.5 * 0.254829592 + t * (0.5 * -0.284496736 + t * (
        0.5 * 1.421413741 + t * (0.5 * -1.453152027 + t * (0.5 * 1.061405429)))))
    tail = tail * bell
    below = jnp.where(x < 0, tail, 1.0 - tail)
    return x * below, below + (x * 0.3989422804014327) * bell


def first_lanes():
    return lax.broadcasted_iota(jnp.int32, (1, 2 * HEAD_DIM), 1) < HEAD_DIM


def stack_heads(pair):
    zero = jnp.zeros_like(pair)
    left = first_lanes()
    return jnp.concatenate([jnp.where(left, pair, zero), jnp.where(left, zero, pair)], 0)


def unstack_heads(stacked):
    rows = stacked.shape[0] // 2
    return jnp.where(first_lanes(), stacked[:rows], stacked[rows:])


def pair_shares(query_stack, key_pair, allowed):
    scores = dot_nt(query_stack, key_pair)
    if allowed is not None:
        scores = jnp.where(allowed, scores, masked_score)
    raised = jnp.exp(scores - jnp.max(scores, -1, keepdims=True))
    return raised * (1.0 / jnp.sum(raised, -1, keepdims=True))


def attend_rows(qkv, mixed, rows, span, width, allowed):
    for start in range(0, rows, span):
        here = pl.ds(start, span)
        for p in range(width // (2 * HEAD_DIM)):
            at = p * 2 * HEAD_DIM
            query = stack_heads(qkv[here, pl.ds(at, 2 * HEAD_DIM)] * jnp.bfloat16(HEAD_DIM**-0.5))
            key = qkv[here, pl.ds(width + at, 2 * HEAD_DIM)]
            value = qkv[here, pl.ds(2 * width + at, 2 * HEAD_DIM)]
            shares = pair_shares(query, key, allowed)
            both = dot_nn(shares.astype(jnp.bfloat16), value)
            mixed[here, pl.ds(at, 2 * HEAD_DIM)] = unstack_heads(both).astype(jnp.bfloat16)


def attend_back(qkv, d_mixed, d_qkv, rows, span, width, allowed):
    scale = HEAD_DIM**-0.5
    for start in range(0, rows, span):
        here = pl.ds(start, span)
        for p in range(width // (2 * HEAD_DIM)):
            at = p * 2 * HEAD_DIM
            query = stack_heads(qkv[here, pl.ds(at, 2 * HEAD_DIM)] * jnp.bfloat16(scale))
            key = qkv[here, pl.ds(width + at, 2 * HEAD_DIM)]
            value = qkv[here, pl.ds(2 * width + at, 2 * HEAD_DIM)]
            grad = stack_heads(d_mixed[here, pl.ds(at, 2 * HEAD_DIM)])
            shares = pair_shares(query, key, allowed)
            d_shares = dot_nt(grad, value)
            delta = jnp.sum(shares * d_shares, -1, keepdims=True)
            d_scores = (shares * (d_shares - delta)).astype(jnp.bfloat16)
            d_query = unstack_heads(dot_nn(d_scores, key)) * scale
            d_key = dot_tn(d_scores, query)
            d_value = dot_tn(shares.astype(jnp.bfloat16), grad)
            d_qkv[here, pl.ds(at, 2 * HEAD_DIM)] = d_query.astype(jnp.bfloat16)
            d_qkv[here, pl.ds(width + at, 2 * HEAD_DIM)] = d_key.astype(jnp.bfloat16)
            d_qkv[here, pl.ds(2 * width + at, 2 * HEAD_DIM)] = d_value.astype(jnp.bfloat16)


def row_sums(value):
    return jnp.sum(value.astype(jnp.float32), 0, keepdims=True)


def whole(shape):
    return pl.BlockSpec(shape, lambda *i: (0,) * len(shape), pipeline_mode=pl.Buffered(1))


def select(rows, columns, first):
    row = lax.broadcasted_iota(jnp.int32, (rows, columns), 0)
    column = lax.broadcasted_iota(jnp.int32, (rows, columns), 1)
    return jnp.where(row == first + column, 1.0, 0.0).astype(jnp.bfloat16)


def spread_slots(rows_of_slots, n, per, size):
    columns = n * size
    step = min(columns, 768)
    out = []
    lane = lax.broadcasted_iota(jnp.int32, (128, 1), 0)
    slot = lax.broadcasted_iota(jnp.int32, (n * per, 1), 0) // per
    for c in range(0, columns, step):
        column = lax.broadcasted_iota(jnp.int32, (1, step), 1) + c
        ones = jnp.where(column % size == lane, 1.0, 0.0).astype(jnp.bfloat16)
        laid = dot_nn(rows_of_slots, ones)
        kept = jnp.where(slot == column // size, laid, 0.0)
        out.append(jnp.sum(kept.reshape(n, per, step), 0))
    return out[0] if len(out) == 1 else jnp.concatenate(out, 1)


SMALL_ROWS = 16


def misc_rows(per_output):
    return SMALL_ROWS + -(-per_output // 16) * 16


def weights_kernel(grid, sizes, *refs):
    width, per_project, per_output, per_up, per_pair, places_n = sizes
    n, ndims = grid.n, len(grid.dims)
    pw, ow, uw, dw, pb, ob, ub, db, ng, nb, pt, cot = refs[:12]
    mixed0, up0, down0, mixed1, up1, cot1, own_down1, vec, vec_pair, vec_up, table = refs[12:23]
    own_mixed, own_misc, misc_f, misc_all, own_cot, cot_head = refs[23:29]
    send_sem, recv_sem, local_sem = refs[29:]
    coords = grid.coords()
    me_line = coords[-1]
    cot_copy = pltpu.make_async_copy(cot.at[:, pl.ds(0, 8)], cot_head, local_sem.at[0])
    cot_copy.start()

    misc_f[...] = jnp.zeros_like(misc_f)
    at = 0
    for ref, size in ((pb, per_pair), (ob, per_output), (ub, per_up), (db, per_output)):
        misc_f[pl.ds(at, 2), pl.ds(0, size)] = ref[...].astype(jnp.float32)
        at += 2
    for ref in (ng, nb):
        for b in range(2):
            misc_f[pl.ds(at, 2), pl.ds(0, per_output)] = ref[b].astype(jnp.float32)
            at += 2
    misc_f[pl.ds(SMALL_ROWS, per_output), pl.ds(0, places_n)] = pt[...].astype(jnp.float32)
    own_misc[...] = misc_f[...].astype(jnp.bfloat16)

    def pack(b):
        rows = per_project + per_output
        own_mixed[b] = (
            dot_nn(place_rows(rows, per_project, 0), pw[b]) + dot_nn(place_rows(rows, per_output, per_project), ow[b])
        ).astype(jnp.bfloat16)

    def place_rows(rows, size, first):
        row = lax.broadcasted_iota(jnp.int32, (rows, size), 0)
        column = lax.broadcasted_iota(jnp.int32, (rows, size), 1)
        return jnp.where(row == first + column, 1.0, 0.0).astype(jnp.bfloat16)

    pack(0)
    grid.greet(coords)

    units, chunks = [], []

    def add(own, line, dest, cuts):
        for cut in cuts:
            chunks.append((own, line, dest, *cut))
        return list(range(len(chunks) - len(cuts), len(chunks)))

    mixed_rows = per_project + per_output
    units += [add(own_mixed.at[0], None, mixed0, u) for u in pairs(mixed_rows)]
    units[0] += add(own_misc, None, misc_all, [(0, misc_rows(per_output), 0)])
    up_units = len(units)
    units += [add(uw.at[0], None, up0, u) for u in pairs(per_up)]
    down_units = len(units)
    units += [add(dw.at[0], None, down0, u) for u in pairs(per_up)]
    line_units = [add(own_mixed.at[1], mixed1, None, [h]) for h in halves(mixed_rows, jnp.bfloat16)]
    line_units += [add(uw.at[1], up1, None, [h]) for h in halves(per_up, jnp.bfloat16)]
    line_units[0] += add(own_cot, cot1, None, [(0, own_cot.shape[0], 0)])
    gather = Gather(grid, coords, chunks, send_sem, recv_sem)

    def start(unit, stage):
        for k in unit:
            gather.start(k, stage)

    start(units[0], 0)
    pack(1)
    cot_copy.wait()
    for s in range(own_cot.shape[0]):
        own_cot[pl.ds(s, 1), :] = cot_head[s, 0:1, :]
    locals_ = [
        pltpu.make_async_copy(own_mixed.at[0], mixed0.at[coords], local_sem.at[0]),
        pltpu.make_async_copy(uw.at[0], up0.at[coords], local_sem.at[1]),
        pltpu.make_async_copy(dw.at[0], down0.at[coords], local_sem.at[2]),
        pltpu.make_async_copy(own_mixed.at[1], mixed1.at[me_line], local_sem.at[3]),
        pltpu.make_async_copy(uw.at[1], up1.at[me_line], local_sem.at[4]),
        pltpu.make_async_copy(dw.at[1], own_down1, local_sem.at[5]),
        pltpu.make_async_copy(own_cot, cot1.at[me_line], local_sem.at[6]),
    ]
    for copy in locals_:
        copy.start()
    misc_all[coords] = own_misc[...]
    for copy in locals_:
        copy.wait()

    def vectors():
        small = misc_all[..., 0:SMALL_ROWS, :].reshape(n * SMALL_ROWS, 128)
        singles = spread_slots(small, n, SMALL_ROWS, per_output)
        pairs = spread_slots(small, n, SMALL_ROWS, per_pair)
        ups = spread_slots(small, n, SMALL_ROWS, per_up)
        for b in range(2):
            vec[b, 0:1, :] = singles[2 + b : 3 + b]
            vec[b, 1:2, :] = singles[6 + b : 7 + b]
            vec[b, 2:4, :] = singles[8 + 2 * b : 10 + 2 * b]
            vec[b, 4:6, :] = singles[12 + 2 * b : 14 + 2 * b]
            vec[b, 6:8, :] = jnp.zeros((2, width), jnp.float32)
            vec_pair[b, :, 0:width] = pairs[b : b + 1, :width]
            vec_pair[b, :, width : 2 * width] = jnp.zeros((1, width), jnp.float32)
            vec_pair[b, :, 2 * width : 3 * width] = pairs[b : b + 1, width:]
            vec_up[b] = ups[4 + b : 5 + b]
        for d in range(n):
            where, rest = [], d
            for extent in grid.dims[::-1]:
                where.append(rest % extent)
                rest //= extent
            rows = misc_all[tuple(where[::-1]) + (pl.ds(SMALL_ROWS, misc_rows(per_output) - SMALL_ROWS),)].astype(jnp.float32)
            table[pl.ds(d * per_output, per_output), :] = rows[:per_output]

    count = len(units)
    line_ticks = {count - 6: line_units[:1], count - 4: line_units[1:2], count - 1: line_units[2:]} if count >= 7 else {0: line_units}
    for tick in range(1, count + ndims):
        for stage in range(1, ndims + 1):
            u = tick - stage
            if not 0 <= u < count:
                continue
            for k in units[u]:
                gather.landed(k, stage - 1)
                if stage < ndims:
                    gather.start(k, stage)
            if stage == 1:
                if u + 1 < count:
                    start(units[u + 1], 0)
                for unit in line_ticks.get(u, []):
                    start(unit, 0)
            if stage == ndims and u == 0:
                vectors()
    for unit in line_units:
        for k in unit:
            gather.landed(k, 0)
            gather.sent(k, 0, 1)
    for unit in units:
        for k in unit:
            gather.sent(k, 0, ndims)


def pairs(rows):
    if rows % 32:
        return [[(0, rows, 0)]]
    return [[(r, 16, 0), (r + 16, 16, 1)] for r in range(0, rows, 32)]


def gather_weights(grid, arrays, cid):
    project_weight, output_weight, up_weight, down_weight, project_bias = arrays[:5]
    per_project, per_output, per_up = project_weight.shape[1], output_weight.shape[1], up_weight.shape[1]
    width = project_weight.shape[2]
    per_pair = project_bias.shape[1]
    places_n = arrays[10].shape[1]
    segs = arrays[11].shape[0]
    n = grid.n
    low, full = jnp.bfloat16, jnp.float32
    mixed_rows = per_project + per_output
    small_rows = misc_rows(per_output)
    fs = grid.fsdp
    count = 2 + sum(len(u) for r in (mixed_rows, per_up, per_up) for u in pairs(r)) + sum(len(halves(r, low)) for r in (mixed_rows, per_up))
    vmem, anywhere = pl.BlockSpec(memory_space=pltpu.VMEM), pl.BlockSpec(memory_space=pl.ANY)

    def shape(s, d):
        return jax.ShapeDtypeStruct(s, d)

    return pl.pallas_call(
        functools.partial(weights_kernel, grid, (width, per_project, per_output, per_up, per_pair, places_n)),
        in_specs=[vmem] * 11 + [anywhere],
        out_specs=[anywhere] * 7 + [vmem] * 4,
        out_shape=[
            shape((*grid.dims, mixed_rows, width), low), shape((*grid.dims, per_up, width), low), shape((*grid.dims, per_up, width), low),
            shape((fs, mixed_rows, width), low), shape((fs, per_up, width), low), shape((fs, segs, width), full), shape((per_up, width), low),
            shape((2, 8, width), full), shape((2, 1, 3 * width), full), shape((2, 1, n * per_up), full), shape((width, 128), full),
        ],
        scratch_shapes=[
            pltpu.VMEM((2, mixed_rows, width), low),
            pltpu.VMEM((small_rows, 128), low), pltpu.VMEM((small_rows, 128), full), pltpu.VMEM((*grid.dims, small_rows, 128), low),
            pltpu.VMEM((segs, width), full), pltpu.VMEM((segs, 8, width), full),
        ]
        + grid.sems(count)
        + [pltpu.SemaphoreType.DMA((7,))],
        compiler_params=pltpu.CompilerParams(collective_id=cid, has_side_effects=True, vmem_limit_bytes=56 * 2**20),
        name="gather_weights",
    )(*arrays)


def forward_rows(x_low, x, w, r, rows, span, allowed, hook=lambda name: None):
    width = x.shape[1]
    step = width
    hook("project")
    for c in range(0, 3 * width, step):
        cut = pl.ds(c, step)
        r["qkv"][:, cut] = (dot_nt(x_low, w["project"][cut, :]) + w["project_b"][:, cut]).astype(jnp.bfloat16)
    attend_rows(r["qkv"], r["mixed"], rows, span, width, allowed)
    first = x + (dot_nt(r["mixed"][...], w["output"][...]) + w["output_b"])
    if "first" in r:
        r["first"](first)
    hook("first")
    unit_one, scale_one, unit_two, scale_two = feed_forward(first, w, r, hook)
    return unit_one, scale_one, unit_two, scale_two


def feed_forward(first, w, r, hook=lambda name: None):
    unit_one, scale_one = normalise(first)
    normed = unit_one * w["gains"][0:1, :] + w["shifts"][0:1, :]
    normed_low = normed.astype(jnp.bfloat16)
    r["normed"][...] = normed_low
    hidden_units = w["up"].shape[0]
    step = normed.shape[1]
    for c in range(0, hidden_units, step):
        cut = pl.ds(c, step)
        inner = dot_nt(normed_low, w["up"][cut, :]) + w["up_b"][:, cut]
        value, slope = gelu_pair(inner)
        r["hidden"][:, cut] = value.astype(jnp.bfloat16)
        r["slope"][:, cut] = slope.astype(r["slope"].dtype)
    hook("down")
    second = normed + (dot_nn(r["hidden"][...], w["down"][...]) + w["down_b"])
    unit_two, scale_two = normalise(second)
    return unit_one, scale_one, unit_two, scale_two


def mlp_back(grad, unit_one, scale_one, unit_two, scale_two, w, r, hook=lambda name: None):
    d_second = norm_back(grad, unit_two, scale_two, w["gains"][1:2, :])
    d_down = d_second.astype(jnp.bfloat16)
    r["d_down"][...] = d_down
    hidden_units = w["up"].shape[0]
    step = grad.shape[1]
    for c in range(0, hidden_units, step):
        cut = pl.ds(c, step)
        d_hidden = dot_nt(d_down, w["down"][cut, :])
        r["d_inner"][:, cut] = (d_hidden * r["slope"][:, cut].astype(jnp.float32)).astype(jnp.bfloat16)
    hook("up")
    d_normed = d_second + dot_nn(r["d_inner"][...], w["up"][...])
    d_first = norm_back(d_normed, unit_one, scale_one, w["gains"][0:1, :])
    sums = (
        row_sums(d_normed * unit_one), row_sums(grad * unit_two), row_sums(d_normed), row_sums(grad),
        row_sums(d_down), row_sums(r["d_inner"][...]),
    )
    return d_first, sums


def small_of(vec, vec_pair, vec_up, b):
    return {
        "project_b": vec_pair.at[b], "output_b": vec[b, 0:1, :], "up_b": vec_up.at[b], "down_b": vec[b, 1:2, :],
        "gains": vec[b, 2:4, :], "shifts": vec[b, 4:6, :],
    }


def unpack_mixed(grid, mixed, project, output, per_project):
    rows, width = mixed.shape[-2:]
    per_output = rows - per_project
    for d in range(grid.n):
        where, rest = [], d
        for size in grid.dims[::-1]:
            where.append(rest % size)
            rest //= size
        part = mixed[tuple(where[::-1])]
        project[pl.ds(d * per_project, per_project), :] = part[:per_project]
        output[pl.ds(d * per_output, per_output), :] = part[per_project:]


def spread(events, points):
    return [events[len(events) * p // points : len(events) * (p + 1) // points] for p in range(points)]


def segment_forward_kernel(grid, tile, steps, per_project, *refs):
    (tokens, grads, mixed0, up0, down0, vec, vec_pair, vec_up, line_mixed, line_up, line_cot, own_down) = refs[:12]
    names = ("qkv", "mixed", "d_first", "seg_low", "norm_sums", "up_sums")
    r = dict(zip(names, refs[12:18]))
    project_out, output_out, all_first, mixed1, up1, down1, all_cot, partial_up, partial_down = refs[18:27]
    r.update(zip(("slope", "normed", "hidden", "d_down", "d_inner"), refs[27:32]))
    held_mixed, project, output, up, down, own_first, sum_up, sum_down = refs[32:40]
    send_sem, recv_sem, local_sem = refs[40:]
    w = small_of(vec, vec_pair, vec_up, 0)
    w.update(project=project, output=output, up=up, down=down)
    width = tokens.shape[1]
    step = pl.program_id(0)
    last = steps - 1
    ndims = len(grid.dims)
    coords = grid.coords()
    loads = [pltpu.make_async_copy(*p, local_sem.at[i]) for i, p in enumerate(
        ((mixed0, held_mixed), (up0, up), (down0, down)))]
    stores = [pltpu.make_async_copy(*p, local_sem.at[3 + i]) for i, p in enumerate(
        ((project, project_out), (output, output_out)))]
    here = (coords[:-1]) + (slice(None),)
    lines = [pltpu.make_async_copy(a, b.at[here], local_sem.at[5 + i]) for i, (a, b) in enumerate(
        ((line_mixed, mixed1), (line_up, up1), (line_cot, all_cot)))]
    lines.append(pltpu.make_async_copy(own_down, down1.at[coords], local_sem.at[8]))
    keep_first = pltpu.make_async_copy(own_first, all_first.at[coords], local_sem.at[9])

    chunks, groups = [], []
    for own, line, dest, rows in (
        (None, line_mixed, mixed1, line_mixed.shape[1]), (None, line_up, up1, line_up.shape[1]), (own_down, None, down1, own_down.shape[0])
    ):
        cuts = halves(rows, jnp.bfloat16)
        groups.append(list(range(len(chunks), len(chunks) + len(cuts))))
        chunks += [(own, line, dest, *cut) for cut in cuts]
    groups[0].append(len(chunks))
    chunks.append((None, line_cot, all_cot, 0, line_cot.shape[1], 1))
    first_chunk = len(chunks)
    first_chunks = [first_chunk, first_chunk + 1]
    chunks += [(own_first, None, all_first, half, 1, half) for half in range(2)]
    gather = Gather(grid, coords, chunks, send_sem, recv_sem)

    ticks = ndims + 1

    def go(tick):
        if tick == 1:
            for copy in lines:
                copy.wait()
        for group in groups:
            late = chunks[group[0]][1] is None
            stage = tick if late else tick + 1
            for k in group:
                if stage > (0 if late else 1) and stage <= ndims:
                    gather.landed(k, stage - 1)
                if stage < ndims:
                    gather.start(k, stage)

    plan = {}
    for tick in range(1, ticks - 1):
        at = round((2 * steps - 1) * tick / (ticks - 2))
        if ndims == 4 and steps == 4:
            at = (1, 6, 7)[tick - 1]
        plan.setdefault(at, []).append(tick)

    def at_point(which):
        for at, some in plan.items():
            if at % 2 == which:

                @pl.when(step == at // 2)
                def _(some=some):
                    for tick in some:
                        go(tick)

    first_points = ["first", "back", "tail", "end"]
    first_events = [[] for unused in first_points]
    stages = list(range(ndims))
    for i, stage in enumerate(stages):
        first_events[min(i, len(first_points) - 1)].append(stage)

    def first_point(name):
        @pl.when(step == last)
        def _():
            for stage in first_events[first_points.index(name)]:
                if stage == 0:
                    keep_first.start()
                for k in first_chunks:
                    if stage > 0:
                        gather.landed(k, stage - 1)
                    if stage == 1 and k == first_chunk:
                        keep_first.wait()
                    gather.start(k, stage)

    @pl.when(step == 0)
    def _():
        for copy in loads:
            copy.start()
        grid.greet(coords)
        go(0)
        for copy in lines:
            copy.start()
        loads[0].wait()
        unpack_mixed(grid, held_mixed, project, output, per_project)
        for copy in stores:
            copy.start()

    def hook(name):
        if name == "first":
            first_point("first")

            @pl.when(step == 0)
            def _():
                for copy in loads[1:]:
                    copy.wait()

            at_point(0)

    def take_first(first):
        for s in range(tile // SEG_LEN):
            for half in range(2):
                row = first[s * SEG_LEN : s * SEG_LEN + 1, half * (width // 2) : (half + 1) * (width // 2)]
                own_first[half, pl.ds(step * (tile // SEG_LEN) + s, 1), :] = row

    r["first"] = take_first
    x_low = tokens[...]
    x = x_low.astype(jnp.float32)
    unit_one, scale_one, unit_two, scale_two = forward_rows(x_low, x, w, r, tile, SEG_LEN, None, hook)
    seg_out = unit_two * w["gains"][1:2, :] + w["shifts"][1:2, :]
    r["seg_low"][...] = seg_out.astype(jnp.bfloat16)
    first_point("back")
    place = lax.broadcasted_iota(jnp.int32, (tile, 1), 0) % SEG_LEN
    grad = jnp.where(place == 0, 0.0, grads[...])
    d_first, sums = mlp_back(grad, unit_one, scale_one, unit_two, scale_two, w, r, hook)
    r["d_first"][...] = d_first
    gathered = jnp.concatenate(list(sums[:5]) + [jnp.zeros((3, width), jnp.float32)], 0)

    @pl.when(step == 0)
    def _():
        r["norm_sums"][...] = jnp.zeros_like(r["norm_sums"])
        r["up_sums"][...] = jnp.zeros_like(r["up_sums"])
        sum_up[...] = jnp.zeros_like(sum_up)
        sum_down[...] = jnp.zeros_like(sum_down)

    r["norm_sums"][...] += gathered
    r["up_sums"][...] += jnp.broadcast_to(sums[5], r["up_sums"].shape)
    first_point("tail")
    for left, right, total in (("hidden", "d_down", sum_down), ("d_inner", "normed", sum_up)):
        for c in range(0, total.shape[0], width):
            total[pl.ds(c, width), :] += dot_tn(r[left][:, pl.ds(c, width)], r[right][...])
    first_point("end")
    at_point(1)

    @pl.when(step == last)
    def _():
        down[...] = sum_down[...].astype(jnp.bfloat16)
        up[...] = sum_up[...].astype(jnp.bfloat16)
        out = [pltpu.make_async_copy(*p, local_sem.at[i]) for i, p in enumerate(((down, partial_down), (up, partial_up)))]
        for copy in out:
            copy.start()
        go(ticks - 1)
        for g in range(len(groups)):
            for k in groups[g]:
                gather.sent(k, 1 if chunks[k][1] is not None else 0, ndims)
        for k in first_chunks:
            gather.landed(k, ndims - 1)
            gather.sent(k, 0, ndims)
        for copy in stores + out:
            copy.wait()


def segment_forward(grid, tokens, grads, mixed0, up0, down0, smalls, lines, per_project, cid):
    rows, width = tokens.shape
    per_up = up0.shape[-2]
    mixed_rows = mixed0.shape[-2]
    hidden_units = per_up * grid.n
    tile = 2 * SEG_LEN
    steps = rows // tile
    segs = rows // SEG_LEN
    low, full = jnp.bfloat16, jnp.float32
    up0, down0 = up0.reshape(hidden_units, width), down0.reshape(hidden_units, width)
    count = 3 + sum(len(halves(r, low)) for r in (mixed_rows, per_up, per_up))
    vmem, anywhere = pl.BlockSpec(memory_space=pltpu.VMEM), pl.BlockSpec(memory_space=pl.ANY)

    def cut(columns):
        return pl.BlockSpec((tile, columns), lambda i: (i, 0))

    def shape(columns, dtype):
        return jax.ShapeDtypeStruct((rows, columns), dtype)

    return pl.pallas_call(
        functools.partial(segment_forward_kernel, grid, tile, steps, per_project),
        grid=(steps,),
        in_specs=[cut(width), cut(width)] + [anywhere] * 3 + [whole(s.shape) for s in (*smalls, *lines)],
        out_specs=[
            cut(3 * width), cut(width), cut(width), cut(width),
            pl.BlockSpec((8, width), lambda i: (0, 0)), pl.BlockSpec((8, hidden_units), lambda i: (0, 0)),
        ]
        + [anywhere] * 9,
        out_shape=[
            shape(3 * width, low), shape(width, low), shape(width, full), shape(width, low),
            jax.ShapeDtypeStruct((8, width), full), jax.ShapeDtypeStruct((8, hidden_units), full),
            jax.ShapeDtypeStruct((3 * width, width), low), jax.ShapeDtypeStruct((width, width), low),
            jax.ShapeDtypeStruct((*grid.dims, 2, segs, width // 2), full),
            jax.ShapeDtypeStruct((*grid.dims, mixed_rows, width), low),
            jax.ShapeDtypeStruct((*grid.dims, per_up, width), low), jax.ShapeDtypeStruct((*grid.dims, per_up, width), low),
            jax.ShapeDtypeStruct((*grid.dims, segs, width), full),
            jax.ShapeDtypeStruct((hidden_units, width), low), jax.ShapeDtypeStruct((hidden_units, width), low),
        ],
        scratch_shapes=[
            pltpu.VMEM((tile, hidden_units), low), pltpu.VMEM((tile, width), low), pltpu.VMEM((tile, hidden_units), low),
            pltpu.VMEM((tile, width), low), pltpu.VMEM((tile, hidden_units), low), pltpu.VMEM((*grid.dims, mixed_rows, width), low),
            pltpu.VMEM((3 * width, width), low), pltpu.VMEM((width, width), low),
            pltpu.VMEM((hidden_units, width), low), pltpu.VMEM((hidden_units, width), low), pltpu.VMEM((2, segs, width // 2), full),
            pltpu.VMEM((hidden_units, width), full), pltpu.VMEM((hidden_units, width), full),
        ]
        + grid.sems(count)
        + [pltpu.SemaphoreType.DMA((10,))],
        compiler_params=pltpu.CompilerParams(collective_id=cid, has_side_effects=True, vmem_limit_bytes=60 * 2**20),
        name="segment_forward",
    )(tokens, grads, mixed0, up0, down0, *smalls, *lines)


def own_columns(value, first, size):
    return dot_nn(value, select(value.shape[1], size, first)).astype(jnp.bfloat16)


def own_sums(value, first, size):
    row = lax.broadcasted_iota(jnp.int32, (value.shape[1], size), 0)
    column = lax.broadcasted_iota(jnp.int32, (value.shape[1], size), 1)
    ones = jnp.where(row == first + column, 1.0, 0.0)
    return jnp.dot(value, ones, precision=highest, preferred_element_type=jnp.float32)


def document_of(placed, long_total):
    long_docs = long_total // LONG_SEGS
    is_long = placed < long_total
    rest = placed - long_total
    doc = jnp.where(is_long, placed // LONG_SEGS, long_docs + rest // SHORT_SEGS)
    return doc, jnp.where(is_long, placed % LONG_SEGS, rest % SHORT_SEGS)


def cross_kernel(grid, sizes, *refs):
    per_project, per_output, per_up, per_pair = sizes
    (firsts, grads, placed_row, placed_col, mixed1, up1, down1, up0, down0, vec, vec_pair, vec_up, table, partial) = refs[:14]
    g_project, g_output, g_up, g_down, z_up, z_down, smalls, g_table, cross_own, d_first_own, line_down = refs[14:25]
    names = ("qkv", "slope", "d_mixed", "mixed", "normed", "hidden", "d_down", "d_inner", "d_qkv")
    r = dict(zip(names, refs[25:34]))
    held_mixed, project, output, up, down, z_up_w, z_down_w, z_slope, z_normed, z_hidden, z_d_down, z_d_inner, rows_f = refs[34:47]
    held, *lands, send_sem, recv_sem, local_sem = refs[47:]
    coords = grid.coords()
    reduce, ticks = summing(grid, coords, held, lands, None, send_sem, recv_sem, 1)
    load_partial = pltpu.make_async_copy(partial, held, local_sem.at[5])
    load_partial.start()
    loads = [pltpu.make_async_copy(*p, local_sem.at[i]) for i, p in enumerate(
        ((up0, z_up_w), (down0, z_down_w), (mixed1, held_mixed), (up1, up), (down1, down)))]
    for copy in loads:
        copy.start()
    expected = grid.call(coords)
    slots, width = firsts.shape
    places_n = LONG_SEGS
    me = grid.flat()
    per_slots = slots // grid.n

    w0 = small_of(vec, vec_pair, vec_up, 0)
    w0.update(up=z_up_w, down=z_down_w)
    r0 = {"normed": z_normed, "hidden": z_hidden, "slope": z_slope, "d_down": z_d_down, "d_inner": z_d_inner}

    def hook0(name):
        if name == "down":
            loads[1].wait()
            load_partial.wait()
            grid.meet(expected)
            reduce(0)

    loads[0].wait()
    kept0 = feed_forward(firsts[...], w0, r0, hook0)
    seg_first = kept0[2] * w0["gains"][1:2, :] + w0["shifts"][1:2, :]
    doc_row, unused = document_of(placed_row[...], slots // 2)
    doc_col, place_col = document_of(placed_col[...], slots // 2)
    picker = place_col == lax.broadcasted_iota(jnp.int32, (slots, places_n), 1)
    picker_f = jnp.where(picker, 1.0, 0.0)
    x = seg_first + dot_nt(picker_f.astype(jnp.bfloat16), table[:, 0:places_n].astype(jnp.bfloat16))

    w = small_of(vec, vec_pair, vec_up, 1)
    w.update(project=project, output=output, up=up, down=down)
    loads[2].wait()
    unpack_mixed(grid, held_mixed, project, output, per_project)
    x_low = x.astype(jnp.bfloat16)
    allowed = doc_col == doc_row
    allowed = jnp.concatenate([allowed, allowed], 0)
    reduce(1)

    def hook(name):
        if name == "first":
            loads[3].wait()
        if name == "down":
            loads[4].wait()

    kept = forward_rows(x_low, x, w, r, slots, slots, allowed, hook)
    mine = pl.ds(pl.multiple_of(me * per_slots, per_slots), per_slots)
    rows_f[...] = kept[2] * w["gains"][1:2, :] + w["shifts"][1:2, :]
    cross_own[...] = rows_f[mine, :]
    d_first, sums = mlp_back(grads[...], *kept, w, r)
    reduce(2)
    branch = d_first.astype(jnp.bfloat16)
    r["d_mixed"][...] = dot_nn(branch, output[...]).astype(jnp.bfloat16)
    attend_back(r["qkv"], r["d_mixed"], r["d_qkv"], slots, slots, width, allowed)
    d_x = d_first + dot_nn(r["d_qkv"][...], project[...])
    for tick in range(3, ticks):
        reduce(tick)
    store = pltpu.make_async_copy(held.at[coords[:-1]], line_down, local_sem.at[5])
    store.start()

    g_project[...] = dot_tn(own_columns(r["d_qkv"][...], me * per_project, per_project), x_low)
    g_output[...] = dot_tn(own_columns(branch, me * per_output, per_output), r["mixed"][...])
    g_up[...] = dot_tn(own_columns(r["d_inner"][...], me * per_up, per_up), r["normed"][...])
    g_down[...] = dot_tn(own_columns(r["hidden"][...], me * per_up, per_up), r["d_down"][...])
    smalls[...] = jnp.zeros_like(smalls)
    norm_rows = jnp.concatenate(list(sums[:5]) + [row_sums(branch), jnp.zeros((2, width), jnp.float32)], 0)
    smalls[0:8, 0:per_output] = own_sums(norm_rows, me * per_output, per_output)
    up_rows = jnp.broadcast_to(sums[5], (8, sums[5].shape[1]))
    smalls[6:7, 0:per_up] = own_sums(up_rows, me * per_up, per_up)[0:1]
    qkv_sums = row_sums(r["d_qkv"][...])
    pair = jnp.concatenate([qkv_sums[:, :width], qkv_sums[:, 2 * width :]], 1)
    smalls[7:8, 0:per_pair] = own_sums(jnp.broadcast_to(pair, (8, 2 * width)), me * per_pair, per_pair)[0:1]
    g_table[...] = lax.dot_general(
        own_sums(d_x, me * per_output, per_output), picker_f, (((0,), (0,)), ((), ())),
        precision=highest, preferred_element_type=jnp.float32,
    )

    d_first0, sums = mlp_back(d_x, *kept0, w0, r0)
    rows_f[...] = d_first0
    d_first_own[...] = rows_f[mine, :]
    z_up[...] = dot_tn(own_columns(z_d_inner[...], me * per_up, per_up), z_normed[...])
    z_down[...] = dot_tn(own_columns(z_hidden[...], me * per_up, per_up), z_d_down[...])
    norm_rows = jnp.concatenate(list(sums[:5]) + [jnp.zeros((3, width), jnp.float32)], 0)
    smalls[8:16, 0:per_output] = own_sums(norm_rows, me * per_output, per_output)
    up_rows = jnp.broadcast_to(sums[5], (8, sums[5].shape[1]))
    smalls[14:15, 0:per_up] = own_sums(up_rows, me * per_up, per_up)[0:1]
    store.wait()
    reduce(None)


def summing(grid, coords, held, lands, out, send_sem, recv_sem, short=0):
    ndims = len(grid.dims) - short
    units = [halves(held.shape[-2], held.dtype)]
    cuts = [cut for unit in units for cut in unit]
    whole_dims = len(grid.dims)
    chunks = [(held, lands[k * whole_dims : (k + 1) * whole_dims], out, *cut) for k, cut in enumerate(cuts)]
    scatter = Scatter(grid, coords, chunks, send_sem, recv_sem)
    per = len(units[0])

    def reduce(tick):
        if tick is None:
            for k in range(len(chunks)):
                scatter.sent(k, ndims)
            return
        for stage in range(ndims + 1):
            u = tick - stage
            if not 0 <= u < len(units):
                continue
            for k in range(u * per, (u + 1) * per):
                if stage > 0:
                    scatter.add(k, stage - 1)
                if stage < ndims:
                    scatter.start(k, stage)

    return reduce, len(units) + ndims


def summing_scratch(grid, rows, width):
    low = jnp.bfloat16
    cuts = halves(rows, low)
    lands = [land for cut in cuts for land in Scatter.landing(grid, cut[1], width, low, cut[2])]
    return [pltpu.VMEM((*grid.dims, rows, width), low)] + lands + grid.sems(len(cuts))


def cross_block(grid, firsts, grads, placement, mixed1, up1, down1, up0, down0, smalls, table, sizes, partial, cid):
    slots, width = firsts.shape
    per_project, per_output, per_up, per_pair = sizes
    hidden_units = per_up * grid.n
    low, full = jnp.bfloat16, jnp.float32
    per_slots = slots // grid.n
    flat = lambda ref: ref.reshape(hidden_units, width)
    vmem, anywhere = pl.BlockSpec(memory_space=pltpu.VMEM), pl.BlockSpec(memory_space=pl.ANY)
    outs = [
        (per_project, width), (per_output, width), (per_up, width), (per_up, width), (per_up, width), (per_up, width),
        (16, 128), (per_output, LONG_SEGS), (per_slots, width), (per_slots, width),
    ]

    def held(*shape, dtype=low):
        return pltpu.VMEM(shape, dtype)

    return pl.pallas_call(
        functools.partial(cross_kernel, grid, sizes),
        in_specs=[vmem] * 4 + [anywhere] * 5 + [vmem] * 4 + [anywhere],
        out_specs=[vmem] * len(outs) + [anywhere],
        out_shape=[jax.ShapeDtypeStruct(s, full) for s in outs] + [jax.ShapeDtypeStruct((grid.fsdp, per_up, width), low)],
        scratch_shapes=[
            held(slots, 3 * width), held(slots, hidden_units), held(slots, width), held(slots, width), held(slots, width),
            held(slots, hidden_units), held(slots, width), held(slots, hidden_units), held(slots, 3 * width),
            held(*mixed1.shape), held(3 * width, width), held(width, width), held(hidden_units, width), held(hidden_units, width),
            held(hidden_units, width), held(hidden_units, width), held(slots, hidden_units), held(slots, width),
            held(slots, hidden_units), held(slots, width), held(slots, hidden_units), held(slots, width, dtype=full),
            *summing_scratch(grid, per_up, width),
            pltpu.SemaphoreType.DMA((6,)),
        ],
        compiler_params=pltpu.CompilerParams(collective_id=cid, has_side_effects=True, vmem_limit_bytes=63 * 2**20),
        name="cross_block",
    )(firsts, grads, placement[None, :], placement[:, None], mixed1, flat(up1), flat(down1), flat(up0), flat(down0), *smalls, table, partial)


def segment_backward_kernel(grid, tile, steps, per_project, *refs):
    (qkv, d_first, cls_grad, seg_low, cls_out, mixed, tokens, project, output, partial, cls_up, cls_down, line_down, norm_sums, up_sums,
     own_small) = refs[:16]
    d_x, layer_out, up_sum, down_sum, mixed_sum, small_out = refs[16:22]
    d_mixed, d_qkv, d_branch, sum_project, sum_output, packed, sums_qkv, sums_out, small_held, small_sum = refs[22:32]
    first_sems = 32 + summing_length(grid, partial.shape[-2])
    held, *lands, send_sem, recv_sem = refs[32:first_sems]
    line_land, line_send, line_recv = refs[first_sems : first_sems + 3]
    *last_lands, last_send, last_recv, local_sem = refs[first_sems + 3 :]
    fs, ndims = grid.fsdp, len(grid.dims)
    width = d_first.shape[1]
    per_output = packed.shape[-2] - per_project
    step = pl.program_id(0)
    coords = grid.coords()
    reduce, ticks = summing(grid, coords, held, lands, up_sum, send_sem, recv_sem)
    line = []
    for ahead in range(1, fs):
        target, value = grid.peer(coords, ndims - 1, ahead)
        line.append(
            pltpu.make_async_remote_copy(
                line_down.at[value], line_land.at[ahead - 1], line_send.at[ahead - 1], line_recv.at[ahead - 1],
                device_id=target, device_id_type=MESH,
            )
        )
    plan = {}
    for tick in range(1, ticks - 1):
        at = (2, 5, 7)[tick - 1] if ticks == 5 and steps == 4 else min(2 * steps - 1, tick + 1)
        plan.setdefault(at, []).append(tick)

    def at_point(which):
        for at, some in plan.items():
            if at % 2 == which:

                @pl.when(step == at // 2)
                def _(some=some):
                    for tick in some:
                        reduce(tick)

    @pl.when(step == 0)
    def _():
        load = pltpu.make_async_copy(partial, held, local_sem.at[0])
        load.start()
        for total in (sums_qkv, sums_out, sum_project, sum_output, small_held):
            total[...] = jnp.zeros_like(total)
        grid.greet(coords)
        load.wait()
        reduce(0)
        for copy in line:
            copy.start()

    at_point(0)
    place = lax.broadcasted_iota(jnp.int32, (tile, 1), 0)
    grad, out = d_first[...], seg_low[...].astype(jnp.float32)
    for s in range(tile // SEG_LEN):
        here = pl.ds(step * (tile // SEG_LEN) + s, 1)
        grad = jnp.where(place == s * SEG_LEN, cls_grad[here, :], grad)
        out = jnp.where(place == s * SEG_LEN, cls_out[here, :], out)
    layer_out[...] = out.astype(jnp.bfloat16)
    branch = grad.astype(jnp.bfloat16)
    d_branch[...] = branch
    d_mixed[...] = dot_nn(branch, output[...]).astype(jnp.bfloat16)
    attend_back(qkv, d_mixed, d_qkv, tile, SEG_LEN, width, None)
    at_point(1)
    d_x[...] = grad + dot_nn(d_qkv[...], project[...])
    sums_qkv[...] += jnp.broadcast_to(row_sums(d_qkv[...]), sums_qkv.shape)
    sums_out[...] += jnp.broadcast_to(row_sums(branch), sums_out.shape)
    sum_output[...] += dot_tn(d_branch[...], mixed[...])
    for c in range(0, 3 * width, width):
        sum_project[pl.ds(c, width), :] += dot_tn(d_qkv[:, pl.ds(c, width)], tokens[...])

    @pl.when(step == steps - 1)
    def _():
        for d in range(grid.n):
            where, rest = [], d
            for size in grid.dims[::-1]:
                where.append(rest % size)
                rest //= size
            rows = [sum_project[pl.ds(d * per_project, per_project), :], sum_output[pl.ds(d * per_output, per_output), :]]
            where = tuple(where[::-1])
            packed[where] = jnp.concatenate(rows, 0).astype(jnp.bfloat16)
            per_pair = 2 * per_output
            at = d * per_pair if d * per_pair < width else d * per_pair + width
            for row, count, source, first, size in (
                (0, 5, norm_sums[0:5, :], d * per_output, per_output), (5, 1, sums_out[0:1, :], d * per_output, per_output),
                (6, 1, up_sums[0:1, :], d * 4 * per_output, 4 * per_output), (7, 1, sums_qkv[0:1, :], at, per_pair),
            ):
                small_held[where + (pl.ds(row, count), pl.ds(0, size))] = source[:, first : first + size]
        units, cuts = [], []
        for unit in pairs(packed.shape[-2]):
            units.append(list(range(len(cuts), len(cuts) + len(unit))))
            cuts += [(packed, mixed_sum, *cut) for cut in unit]
        units[0].append(len(cuts))
        cuts.append((small_held, small_sum, 0, 8, 0))
        last = Scatter(
            grid, coords, [(h, last_lands[k * ndims : (k + 1) * ndims], *rest) for k, (h, *rest) in enumerate(cuts)], last_send, last_recv
        )
        for tick in range(len(units) + ndims):
            for stage in range(ndims + 1):
                u = tick - stage
                if not 0 <= u < len(units):
                    continue
                for k in units[u]:
                    if stage > 0:
                        last.add(k, stage - 1)
                    if stage < ndims:
                        last.start(k, stage)
            if tick == 1:
                total = line_down[coords[-1]].astype(jnp.float32) + cls_down[...]
                for ahead, copy in enumerate(line):
                    copy.wait_recv()
                    total += line_land[ahead].astype(jnp.float32)
                down_sum[...] = total
            if tick == 2:
                reduce(ticks - 1)
                up_sum[...] += cls_up[...]
        small_out[0] = small_sum[...] + own_small[8:16, :]
        small_out[1] = own_small[0:8, :]
        for copy in line:
            copy.wait_send()
        for k in range(len(cuts)):
            last.sent(k, ndims)
        reduce(None)


def summing_length(grid, rows):
    return 1 + len(halves(rows, jnp.bfloat16)) * len(grid.dims) + 2


def segment_backward(
    grid, qkv, d_first, cls_grad, seg_low, cls_out, mixed, tokens, project, output, partial, cls_up, cls_down, line_down, norm_sums,
    up_sums, own_small, per_project, cid,
):
    rows, width = d_first.shape
    tile = 2 * SEG_LEN
    low, full = jnp.bfloat16, jnp.float32
    per_up = partial.shape[-2]
    mixed_rows = 4 * width // grid.n
    anywhere = pl.BlockSpec(memory_space=pl.ANY)

    def cut(columns):
        return pl.BlockSpec((tile, columns), lambda i: (i, 0))

    def fixed(*shape):
        return pl.BlockSpec(shape, lambda i: (0,) * len(shape))

    last_lands, last_count = [], 0
    for first, count, colour in [c for unit in pairs(mixed_rows) for c in unit]:
        last_lands += Scatter.landing(grid, count, width, low, colour)
        last_count += 1
    last_lands += Scatter.landing(grid, 8, 128, full, 0)
    return pl.pallas_call(
        functools.partial(segment_backward_kernel, grid, tile, rows // tile, per_project),
        grid=(rows // tile,),
        in_specs=[
            cut(3 * width), cut(width), whole(cls_grad.shape), cut(width), whole(cls_out.shape), cut(width), cut(width),
            whole(project.shape), whole(output.shape), anywhere,
            *[whole(a.shape) for a in (cls_up, cls_down, line_down, norm_sums, up_sums, own_small)],
        ],
        out_specs=[
            cut(width), cut(width), fixed(per_up, width), fixed(per_up, width), fixed(mixed_rows, width), fixed(2, 8, 128),
        ],
        out_shape=[
            jax.ShapeDtypeStruct((rows, width), full), jax.ShapeDtypeStruct((rows, width), low),
            jax.ShapeDtypeStruct((per_up, width), full), jax.ShapeDtypeStruct((per_up, width), full),
            jax.ShapeDtypeStruct((mixed_rows, width), full), jax.ShapeDtypeStruct((2, 8, 128), full),
        ],
        scratch_shapes=[
            pltpu.VMEM((tile, width), low), pltpu.VMEM((tile, 3 * width), low), pltpu.VMEM((tile, width), low),
            pltpu.VMEM((3 * width, width), full), pltpu.VMEM((width, width), full), pltpu.VMEM((*grid.dims, mixed_rows, width), low),
            pltpu.VMEM((8, 3 * width), full), pltpu.VMEM((8, width), full), pltpu.VMEM((*grid.dims, 8, 128), full), pltpu.VMEM((8, 128), full),
            *summing_scratch(grid, per_up, width),
            pltpu.VMEM((grid.fsdp - 1, per_up, width), low), pltpu.SemaphoreType.DMA((grid.fsdp - 1,)), pltpu.SemaphoreType.DMA((grid.fsdp - 1,)),
            *last_lands, *grid.sems(last_count + 1), pltpu.SemaphoreType.DMA((1,)),
        ],
        compiler_params=pltpu.CompilerParams(collective_id=cid, has_side_effects=True, vmem_limit_bytes=61 * 2**20),
        name="segment_backward",
    )(
        qkv, d_first, cls_grad, seg_low, cls_out, mixed, tokens, project, output, partial, cls_up, cls_down, line_down, norm_sums, up_sums,
        own_small,
    )


class Held:
    def __init__(self, value):
        self.value = value

    @property
    def shape(self):
        return self.value.shape

    @property
    def dtype(self):
        return self.value.dtype

    @staticmethod
    def plain(where):
        where = where if isinstance(where, tuple) else (where,)
        return tuple(slice(w.start, w.start + w.size) if isinstance(w, pl.Slice) else w for w in where)

    def __getitem__(self, where):
        return self.value[self.plain(where)]

    def __setitem__(self, where, value):
        self.value = self.value.at[self.plain(where)].set(value)


def sum_to_lines(partial):
    rows, width = partial.shape[-2:]
    fs = partial.shape[-3]
    return lax.psum_scatter(partial.reshape(-1, fs, rows, width), "dp", scatter_dimension=0, tiled=True)[0]


def cross_plain(grid, firsts, grads, placement, mixed1, up1, down1, up0, down0, smalls, table, sizes, partial, cid):
    slots, width = firsts.shape
    per_project, per_output, per_up, per_pair = sizes
    hidden_units = per_up * grid.n
    me = grid.flat()
    vec, vec_pair, vec_up = smalls

    def weights(b, up, down):
        return {
            "project_b": vec_pair[b], "output_b": vec[b, 0:1, :], "up_b": vec_up[b], "down_b": vec[b, 1:2, :],
            "gains": vec[b, 2:4, :], "shifts": vec[b, 4:6, :],
            "up": up.reshape(hidden_units, width), "down": down.reshape(hidden_units, width),
        }

    def blank(columns):
        return Held(jnp.zeros((slots, columns), jnp.bfloat16))

    def store():
        made = {k: blank(width) for k in ("mixed", "normed", "d_down", "d_mixed")}
        made.update({k: blank(hidden_units) for k in ("hidden", "slope", "d_inner")})
        made.update(qkv=blank(3 * width), d_qkv=blank(3 * width))
        return made

    def cut(matrix, size, axis=1):
        return lax.dynamic_slice_in_dim(matrix, me * size, size, axis)

    w0, w, r0, r = weights(0, up0, down0), weights(1, up1, down1), store(), store()
    parts = mixed1.reshape(grid.n, -1, width)
    w["project"] = parts[:, :per_project].reshape(3 * width, width)
    w["output"] = parts[:, per_project:].reshape(width, width)
    kept0 = feed_forward(firsts, w0, r0)
    seg_first = kept0[2] * w0["gains"][1:2, :] + w0["shifts"][1:2, :]
    doc, place = document_of(placement, slots // 2)
    picker = jnp.where(place[:, None] == jnp.arange(LONG_SEGS, dtype=jnp.int32)[None, :], 1.0, 0.0)
    x = seg_first + dot_nt(picker.astype(jnp.bfloat16), table[:, :LONG_SEGS].astype(jnp.bfloat16))
    x_low = x.astype(jnp.bfloat16)
    allowed = doc[:, None] == doc[None, :]
    allowed = jnp.concatenate([allowed, allowed], 0)
    kept = forward_rows(x_low, x, w, r, slots, slots, allowed)
    out = kept[2] * w["gains"][1:2, :] + w["shifts"][1:2, :]
    d_first, sums = mlp_back(grads, *kept, w, r)
    branch = d_first.astype(jnp.bfloat16)
    r["d_mixed"][...] = dot_nn(branch, w["output"]).astype(jnp.bfloat16)
    attend_back(r["qkv"], r["d_mixed"], r["d_qkv"], slots, slots, width, allowed)
    d_x = d_first + dot_nn(r["d_qkv"][...], w["project"])
    d_first0, sums0 = mlp_back(d_x, *kept0, w0, r0)
    qkv_sums = row_sums(r["d_qkv"][...])
    pair = jnp.concatenate([qkv_sums[:, :width], qkv_sums[:, 2 * width :]], 1)

    def laid(rows, size):
        return jnp.pad(cut(rows, size), ((0, 0), (0, 128 - size)))

    none = jnp.zeros((1, 128), jnp.float32)
    own_small = jnp.concatenate(
        [
            laid(jnp.concatenate(list(sums[:5]) + [row_sums(branch)], 0), per_output), laid(sums[5], per_up), laid(pair, per_pair),
            laid(jnp.concatenate(list(sums0[:5]), 0), per_output), none, laid(sums0[5], per_up), none,
        ],
        0,
    )
    g_table = lax.dot_general(cut(d_x, per_output), picker, (((0,), (0,)), ((), ())), precision=highest)
    per_slots = slots // grid.n
    return (
        dot_tn(cut(r["d_qkv"][...], per_project), x_low), dot_tn(cut(branch, per_output), r["mixed"][...]),
        dot_tn(cut(r["d_inner"][...], per_up), r["normed"][...]), dot_tn(cut(r["hidden"][...], per_up), r["d_down"][...]),
        dot_tn(cut(r0["d_inner"][...], per_up), r0["normed"][...]), dot_tn(cut(r0["hidden"][...], per_up), r0["d_down"][...]),
        own_small, g_table, cut(out, per_slots, 0), cut(d_first0, per_slots, 0), sum_to_lines(partial),
    )


def shards(
    grid,
    tokens,
    cotangent,
    placement,
    project_weight,
    project_bias,
    output_weight,
    output_bias,
    up_weight,
    up_bias,
    down_weight,
    down_bias,
    norm_gain,
    norm_bias,
    position_table,
):
    n = grid.n
    seg_count, seg_len, width = tokens.shape
    slots, rows = placement.shape[0], seg_count * seg_len
    per_project, per_output = project_weight.shape[2], output_weight.shape[2]
    per_pair, per_up = project_bias.shape[1], up_bias.shape[1]
    sizes = (per_project, per_output, per_up, per_pair)
    low_tokens = tokens.reshape(rows, width)

    mixed0, up0, down0, *lines, vec, vec_pair, vec_up, table = gather_weights(
        grid,
        [*(jnp.swapaxes(w, 1, 2) for w in (project_weight, output_weight, up_weight)), down_weight,
         project_bias, output_bias, up_bias, down_bias, norm_gain, norm_bias, position_table.T, cotangent],
        0,
    )
    smalls = [vec, vec_pair, vec_up]
    (qkv, mixed, d_first, seg_low, norm_sums, up_sums, project, output, all_first,
     mixed1, up1, down1, all_cot, partial_up, partial_down) = segment_forward(
        grid, low_tokens, cotangent.reshape(rows, width), mixed0, up0, down0, smalls, lines, per_project, 1
    )
    partial_up, partial_down = [p.reshape(*grid.dims, per_up, width) for p in (partial_up, partial_down)]
    g_project, g_output, g_up, g_down, z_up, z_down, own_small, g_table, cross_own, cls_grad, line_down = (cross_block if slots <= 256 else cross_plain)(
        grid, all_first.reshape(n, 2, seg_count, width // 2).transpose(0, 2, 1, 3).reshape(slots, width), all_cot.reshape(slots, width), placement, mixed1, up1, down1, up0, down0,
        smalls, table, sizes, partial_down, 2,
    )
    d_x, layer_out, up_sum, down_sum, mixed_sum, both = segment_backward(
        grid, qkv, d_first, cls_grad, seg_low, cross_own, mixed, low_tokens, project, output, partial_up, z_up, z_down, line_down,
        norm_sums, up_sums, own_small, per_project, 3,
    )
    return (
        layer_out.reshape(tokens.shape),
        d_x.reshape(tokens.shape),
        jnp.swapaxes(jnp.stack([mixed_sum[:per_project], g_project]), 1, 2),
        both[:, 7, :per_pair],
        jnp.swapaxes(jnp.stack([mixed_sum[per_project:], g_output]), 1, 2),
        both[:, 5, :per_output],
        jnp.swapaxes(jnp.stack([up_sum, g_up]), 1, 2),
        both[:, 6, :per_up],
        jnp.stack([down_sum, g_down]),
        both[:, 4, :per_output],
        both[:, 0:2, :per_output],
        both[:, 2:4, :per_output],
        g_table.T,
    )


def solution(mesh):
    grid = Grid(mesh)
    rows, cols, last = P(AXES, None, None), P(None, AXES), P(None, None, AXES)
    middle = P(None, AXES, None)
    return jax.shard_map(
        functools.partial(shards, grid),
        mesh=mesh,
        in_specs=(
            rows, rows, P(), last, cols, last, cols, last, cols, middle, cols, last, last, cols,
        ),
        out_specs=(rows, rows, last, cols, last, cols, last, cols, middle, cols, last, last, cols),
        check_vma=False,
    )
```
